32 devices in a mesh: group: 4 (over z), table: 8 (over y, x, core).
Axes of the slice: x: 2, y: 2, z: 4, core: 2. Of those that a mesh axis runs over, the one named last changes fastest.
Arguments:
- table: float32 [128, 2048, 128], P('table'), may hold values from -0.36 to 0.36
- accum: float32 [128, 2048], P('table'), may hold values from 0.05 to 2
- w_hidden: bfloat16 [128, 128, 128], replicated, may hold values from -0.5 to 0.5
- w_out: float32 [128], replicated, may hold values from -1.8 to 1.8
- ids: int32 [128, 8, 4096], P('table', None, 'group'), may hold values from 0 to 2047, as said below
- labels: float32 [4096], P(('group', 'table')), may hold values from 0 to 1, as said below
- touched: int32 [128, 512], P('table'), may hold values from 0 to 2047, as said below
- row_noise: float32 [128, 512, 128], P('table'), may hold values from -1.8 to 1.8
- dense_noise: float32 [128, 128, 128], P('table', 'group'), may hold values from -3.6 to 3.6
Outputs:
- new_table: float32 [128, 2048, 128], P('table')
- new_accum: float32 [128, 2048], P('table')
- dense_grad: float32 [128, 128, 128], P('table', 'group')
The draws below stay inside these ranges and needn't reach their ends.
Inputs may be any that keep to these rules, and one draw needn't show every extreme that they name: `touched`: for each feature, 512 different rows of that feature's table. `ids`: every id of feature f is one of the rows listed for f in touched. `labels`: each target is 0 or 1.
All inputs are finite; a program needn't handle non-finite values.
Results may differ from the reference program's by a relative error of at most 0.003.
Values may be sent and summed in bfloat16 or wider, within the bound.
No kernel may reach another device: no remote copies, remote signals or barrier semaphores. Data moves between devices by JAX's collectives and lax.ppermute only.
A program may use at most 128 MiB of HBM per device.

```python
import math
import jax
import jax.numpy as jnp
from jax import lax

E = 128
F = 128
H1 = 128
HOTS = 8
ROWS_F = 2048
TOUCH_F = 512
EXAMPLES = 4096


def listed_rows(key):
    keys = jax.random.split(key, F)

    def one_feature(feature_key):
        return jax.random.permutation(feature_key, ROWS_F)[:TOUCH_F]
    return jax.vmap(one_feature)(keys).astype(jnp.int32)


def pick_slots(source, slots):
    return source[slots]


def rising_weights(key, lowest):
    values = jnp.clip(jax.random.normal(key, (F, E, H1), jnp.float32), -6.0, 6.0) * 0.045
    ramp = jnp.arange(F, dtype=jnp.float32) / max(F - 1, 1)
    amplitude = lowest + ramp
    return values * amplitude[:, None, None]


def draw_touched(key, part):
    listed = listed_rows(key)
    return listed


def draw_ids(key, part):
    listed = listed_rows(key)
    key = jax.random.fold_in(key, 5)
    first_key, second_key = jax.random.split(key)
    first = jax.random.randint(first_key, (F, HOTS, EXAMPLES), 0, TOUCH_F)
    second = jax.random.randint(second_key, (F, HOTS, EXAMPLES), 0, TOUCH_F)
    slots = jnp.minimum(first, second)
    return jax.vmap(pick_slots)(listed, slots).astype(jnp.int32)


def draw_w_hidden(key, part):
    key = jax.random.fold_in(key, 11)
    weights = rising_weights(key, 0.5)
    return weights.astype(jnp.bfloat16)


def draw_labels(key, part):
    key = jax.random.fold_in(key, 13)
    return jax.random.bernoulli(key, 0.5, (EXAMPLES,)).astype(jnp.float32)


def shard_levels(own_key, extent, pieces, smallest, largest):
    factor_of, own = 1.0, jax.random.fold_in(own_key, 6)
    for dim, shards_of in pieces:
        heights = jnp.exp(jax.random.uniform(jax.random.fold_in(own, dim), (shards_of,), jnp.float32, smallest / len(pieces), largest / len(pieces)))
        factor_of = factor_of * jnp.repeat(heights, extent[dim] // shards_of).reshape([-1 if axis == dim else 1 for axis in range(len(extent))])
    return factor_of


def gaussian(key, extent, deviation, limit, pieces=(), held_as=jnp.bfloat16):
    array = jax.random.normal(key, extent, jnp.float32) * deviation
    if len(pieces) > 0:
        array = shard_levels(key, extent, pieces, -0.22, 0.18) * array
    return jnp.clip(array, min=-limit, max=limit).astype(held_as)


def setup_inputs(seed: int = 0) -> dict:
    seeds = jax.random.split(jax.random.key(seed), 10)
    table = gaussian(seeds[0], (F, ROWS_F, E), 0.06, 0.36, ((0, 8),), jnp.float32)
    accum = jnp.clip(jnp.exp(math.log(2.0) - 3.6888794 * jax.random.uniform(seeds[1], (F, ROWS_F), jnp.float32) ** shard_levels(seeds[1], (F, ROWS_F), ((0, 8),), -0.2, 0.2)), 0.05, 2.0)
    w_hidden = draw_w_hidden(jax.random.fold_in(seeds[9], 71), 0)
    w_out = gaussian(seeds[3], (H1,), 0.3, 1.8, (), jnp.float32)
    ids = draw_ids(jax.random.fold_in(seeds[9], 71), 0)
    labels = draw_labels(jax.random.fold_in(seeds[9], 71), 0)
    touched = draw_touched(jax.random.fold_in(seeds[9], 71), 0)
    row_noise = gaussian(seeds[7], (F, TOUCH_F, E), 0.3, 1.8, ((0, 8),), jnp.float32)
    dense_noise = gaussian(seeds[8], (F, E, H1), 0.6, 3.6, ((0, 8), (1, 4)), jnp.float32)
    return {"table": table, "accum": accum, "w_hidden": w_hidden, "w_out": w_out, "ids": ids, "labels": labels, "touched": touched, "row_noise": row_noise, "dense_noise": dense_noise}


CLIP = 1.0
LEARN = 0.05

def silu_slope(pre):
    gate = jax.nn.sigmoid(pre)
    return gate * (1.0 + pre * (1.0 - gate))

def pick_rows(source, where):
    return source[where]

def put_rows(target, where, values):
    return target.at[where].set(values)

def add_rows(target, where, values):
    return target.at[where.reshape(-1)].add(values.reshape(-1, values.shape[-1]))

def reference(table, accum, w_hidden, w_out, ids, labels, touched, row_noise, dense_noise):
    block = math.gcd(EXAMPLES, 256)
    block_count = EXAMPLES // block
    table_low = table.astype(jnp.bfloat16).astype(jnp.float32)
    w_flat = w_hidden.reshape(F * E, H1).astype(jnp.float32)

    def one_block(carry, number):
        grads, dense = carry
        start = number * block
        bags = lax.dynamic_slice_in_dim(ids, start, block, 2)
        targets = lax.dynamic_slice_in_dim(labels, start, block, 0)
        looked = jax.vmap(pick_rows)(table_low, bags)
        pooled = jnp.transpose(lax.optimization_barrier(jnp.sum(looked, axis=1)), (1, 0, 2)).astype(jnp.bfloat16)
        flat = pooled.reshape(block, F * E).astype(jnp.float32)
        pre = jnp.dot(flat, w_flat)
        logit = lax.optimization_barrier(jnp.sum(jax.nn.silu(pre) * w_out, axis=1))
        prob = jax.nn.sigmoid(logit)
        delta = silu_slope(pre) * w_out * (prob - targets)[:, None]
        delta_low = delta.astype(jnp.bfloat16).astype(jnp.float32)
        grad_pool = jnp.dot(delta_low, w_flat.T).astype(jnp.bfloat16).reshape(block, F, E)
        repeats = lax.optimization_barrier(jnp.sum((bags[:, :, None, :] == bags[:, None, :, :]).astype(jnp.float32), axis=(1, 2)))
        grad_sq = lax.optimization_barrier(jnp.sum(jnp.square(grad_pool.astype(jnp.float32)), axis=2))
        embed_sq = lax.optimization_barrier(jnp.sum(repeats.T * grad_sq, axis=1))
        dense_sq = lax.optimization_barrier(jnp.sum(flat * flat, axis=1)) * lax.optimization_barrier(jnp.sum(delta * delta, axis=1))
        factor = CLIP / jnp.maximum(jnp.sqrt(embed_sq + dense_sq), CLIP)
        scaled = (factor[:, None, None] * grad_pool.astype(jnp.float32)).astype(jnp.bfloat16)
        clip_rows = (factor[:, None] * delta).astype(jnp.bfloat16)
        spread = jnp.broadcast_to(jnp.transpose(scaled.astype(jnp.float32), (1, 0, 2))[:, None], (F, HOTS, block, E))
        grads = jax.vmap(add_rows)(grads, bags, spread)
        dense = dense + jnp.einsum('bfe,bh->feh', pooled.astype(jnp.float32), clip_rows.astype(jnp.float32))
        return ((grads, dense), None)
    start_carry = (jnp.zeros((F, ROWS_F, E), jnp.float32), jnp.zeros((F, E, H1), jnp.float32))
    (grads, dense), unused = lax.scan(one_block, start_carry, jnp.arange(block_count, dtype=jnp.int32))
    listed = jax.vmap(pick_rows)(grads, touched) + row_noise
    new_acc = jax.vmap(pick_rows)(accum, touched) + lax.optimization_barrier(jnp.mean(listed * listed, axis=2))
    new_rows = jax.vmap(pick_rows)(table, touched) - LEARN * listed / jnp.sqrt(new_acc)[:, :, None]
    new_table = jax.vmap(put_rows)(table, touched, new_rows)
    new_accum = jax.vmap(put_rows)(accum, touched, new_acc)
    return (new_table, new_accum, dense + dense_noise)
```

```python
import functools

import jax
import jax.numpy as jnp
from jax import lax
from jax.experimental import pallas as pl
from jax.experimental.pallas import tpu as pltpu
from jax.sharding import PartitionSpec as P

CLIP = 1.0
LEARN = 0.05
LANES = 128
DIGITS = 4
HALF = 16
BLOCK = 1024
BATCH = 32
PAIR = 2
LISTED = 16
MIB = 1 << 20

NT = (((1,), (1,)), ((), ()))
TN = (((0,), (0,)), ((), ()))


def dot(left, right, dims=(((1,), (0,)), ((), ())), precision=None):
    return lax.dot_general(
        left, right, dims, preferred_element_type=jnp.float32, precision=precision
    )


def iota(shape, axis):
    return lax.broadcasted_iota(jnp.int32, shape, axis)


def slot_words(touched_row, rows_f):
    count = touched_row.shape[1]
    low = count // DIGITS
    tall = rows_f // LANES
    slot = iota((1, count), 1)
    rows = jnp.where((touched_row >> 7) == iota((tall, count), 0), 1.0, 0.0)
    lanes = jnp.where((touched_row & (LANES - 1)) == iota((LANES, count), 0), 1.0, 0.0)
    values = (lax.rem(slot, low), LISTED + 4 * lax.div(slot, low))
    held = jnp.concatenate([rows * value.astype(jnp.float32) for value in values], axis=0)
    parts = dot(held.astype(jnp.bfloat16), lanes.astype(jnp.bfloat16), NT).astype(jnp.int32)
    word = parts[:tall] | (parts[tall:] << 8)
    return word[: tall // 2] | (word[tall // 2 :] << HALF)


def pick_lanes(lines, row, lane):
    found = jnp.zeros(row.shape, lines[0].dtype)
    for number, line in enumerate(lines):
        got = jnp.take_along_axis(jnp.broadcast_to(line, row.shape), lane, axis=1)
        found = jnp.where(row == number, got, found)
    return found


def look_up(lines, ids, slots, where):
    word = pick_lanes(lines, (ids >> 7) & (len(lines) - 1), ids & (LANES - 1))
    upper = ids >= len(lines) * LANES
    word = jnp.where(upper, lax.shift_right_logical(word, HALF), word) & 0xFFFF
    slots[0, :, where] = word & 0xFF
    slots[1, :, where] = jnp.left_shift(jnp.ones_like(word), (word >> 8) & (LISTED - 1))


def places(low):
    shape = (low // HALF, HALF, LANES)
    return (iota(shape, 0) * HALF + iota(shape, 1)).astype(jnp.int16)


def tally(place, slots, where):
    total = jnp.zeros(place.shape, jnp.int16)
    nothing = jnp.zeros(place.shape, jnp.int16)
    wide = (HALF, LANES)
    for hot in range(slots.shape[1]):
        one_group = jnp.broadcast_to(slots[0, hot : hot + 1, where], wide).astype(jnp.int16)
        one_code = jnp.broadcast_to(slots[1, hot : hot + 1, where], wide).astype(jnp.int16)
        hit = place == jnp.broadcast_to(one_group[None], place.shape)
        total = total + jnp.where(hit, jnp.broadcast_to(one_code[None], place.shape), nothing)
    return total.reshape(-1, LANES)


def spread(codes):
    parts = []
    for digit in range(DIGITS):
        if digit < DIGITS - 1:
            part = codes & jnp.full(codes.shape, 15 << (4 * digit), jnp.int16)
        else:
            part = lax.shift_right_logical(codes, jnp.full(codes.shape, 4 * digit, jnp.int16))
        parts.append(part.astype(jnp.bfloat16))
    return jnp.concatenate(parts, axis=0)


def scale(digit):
    return float(16**digit if digit < DIGITS - 1 else 1)


def pool_kernel(own_ref, listed_ref, table_ref, touched_ref, ids_ref, w_ref, *rest):
    sent_refs, (rows_ref, words_ref, codes_ref, picked, sums, same, slots) = rest[:-7], rest[-7:]
    step = pl.program_id(0)
    rows_f, width = table_ref.shape[1:]
    hots, b_group = ids_ref.shape[1:]
    count = touched_ref.shape[1]
    low = count // DIGITS
    hidden = w_ref.shape[2]
    blocks, tall, chunk = sums.shape
    block = min(b_group, BLOCK)
    place = places(low)

    @pl.when(step == 0)
    def _():
        sums[...] = jnp.zeros_like(sums)
        same[...] = jnp.zeros_like(same)

    features = range(PAIR)
    lines = []
    for side in features:
        words = slot_words(touched_ref[pl.ds(step * PAIR + side, 1)], rows_f)
        words_ref[side] = words
        lines.append([words[number : number + 1] for number in range(words.shape[0])])
    for start in range(0, count, BATCH):
        for side in features:
            batch = range(start, start + BATCH)
            listed = [listed_ref[step * PAIR + side, slot] for slot in batch]
            rows = [table_ref[side, pl.ds(row, 1), :] for row in listed]
            for slot, row in zip(batch, rows):
                picked[side, slot : slot + 1, :] = row
    rows_t, w_t = [], []
    for side in features:
        whole = picked[side].astype(jnp.bfloat16).T
        rows_ref[side] = whole
        parts = [
            whole[:, digit * low : (digit + 1) * low] * jnp.bfloat16(1 / scale(digit))
            for digit in range(DIGITS)
        ]
        rows_t.append(jnp.concatenate(parts, axis=1))
        w_t.append(w_ref[side].T)

    def one_block(number):
        for inner in range(0, block, chunk):
            for side in features:
                where = pl.ds(pl.multiple_of(number * block + inner, chunk), chunk)
                ids = ids_ref[side, :, where]
                look_up(lines[side], ids, slots.at[side], slice(inner, inner + chunk))
                pairs = jnp.zeros(ids.shape, jnp.float32)
                for turn in range(1, hots // 2 + 1):
                    weight = 2.0 if turn < hots // 2 else 1.0
                    pairs = pairs + jnp.where(ids == pltpu.roll(ids, turn, 0), weight, 0.0)
                pairs = jnp.sum(pairs, axis=0, keepdims=True) + hots
                part = number * (block // chunk) + inner // chunk
                same[part, pl.ds(step * PAIR + side, 1)] = pairs
        for inner in range(0, block, 2 * chunk):
            pre, square = 0.0, 0.0
            for side in features:
                parts = []
                for start in (inner, inner + chunk):
                    codes = tally(place, slots.at[side], slice(start, start + chunk))
                    where = pl.ds(pl.multiple_of(number * block + start, chunk), chunk)
                    codes_ref[side, :, where] = codes
                    parts.append(spread(codes))
                pooled = dot(rows_t[side], jnp.concatenate(parts, axis=1)).astype(jnp.bfloat16)
                wide = pooled.astype(jnp.float32)
                square += jnp.sum((wide * wide).reshape(width // HALF, HALF, 2 * chunk), axis=0)
                pre += dot(w_t[side], pooled)
            for turn in range(2):
                part = number * (block // chunk) + inner // chunk + turn
                lanes = slice(turn * chunk, (turn + 1) * chunk)
                sums[part, :hidden] += pre[:, lanes]
                sums[part, hidden:] += square[:, lanes]

    each(b_group // block, one_block)

    @pl.when(step == pl.num_programs(0) - 1)
    def _():
        for apart, sent_ref in enumerate(sent_refs):
            part = own_ref[0] ^ apart
            sent_ref[:tall] = sums[part].astype(jnp.bfloat16)
            sent_ref[tall:] = same[part].astype(jnp.bfloat16)


def each(times, step):
    if times == 1:
        step(0)
    else:

        @pl.loop(0, times)
        def _(number):
            step(number)


def pool(own, table, touched, ids, w_hidden, chunk):
    f_dev, rows_f, width = table.shape
    hots, b_group = ids.shape[1:]
    count = touched.shape[1]
    hidden = w_hidden.shape[2]
    blocks = b_group // chunk
    repeat_rows = -(-f_dev // HALF) * HALF
    tall = hidden + HALF
    sent = (tall + repeat_rows, chunk)

    def now(*shape):
        return pl.BlockSpec((PAIR,) + shape, lambda i, o, s: (i, 0, 0))

    low = count // DIGITS
    outs = pl.pallas_call(
        pool_kernel,
        grid_spec=pltpu.PrefetchScalarGridSpec(
            num_scalar_prefetch=2,
            grid=(f_dev // PAIR,),
            in_specs=[
                now(rows_f, width),
                pl.BlockSpec(touched.shape, lambda i, o, s: (0, 0)),
                now(hots, b_group),
                pl.BlockSpec(
                    (PAIR, width, hidden), lambda i, o, s: (o[0] * (f_dev // PAIR) + i, 0, 0)
                ),
            ],
            out_specs=[pl.BlockSpec(sent, lambda i, o, s: (0, 0))] * blocks
            + [now(width, count), now(rows_f // 256, LANES), now(low, b_group)],
            scratch_shapes=[
                pltpu.VMEM((PAIR, count, width), jnp.float32),
                pltpu.VMEM((blocks, tall, chunk), jnp.float32),
                pltpu.VMEM((blocks, repeat_rows, chunk), jnp.float32),
                pltpu.VMEM((PAIR, 2, hots, min(b_group, BLOCK)), jnp.int32),
            ],
        ),
        out_shape=[jax.ShapeDtypeStruct(sent, jnp.bfloat16)] * blocks
        + [
            jax.ShapeDtypeStruct((f_dev, width, count), jnp.bfloat16),
            jax.ShapeDtypeStruct((f_dev, rows_f // 256, LANES), jnp.int32),
            jax.ShapeDtypeStruct((f_dev, low, b_group), jnp.int16),
        ],
        compiler_params=pltpu.CompilerParams(vmem_limit_bytes=56 * MIB),
        cost_estimate=pl.CostEstimate(
            flops=2 * f_dev * count * b_group * width * 8,
            bytes_accessed=table.size * 4,
            transcendentals=0,
        ),
        name="pool",
    )(own, touched, table, touched, ids, w_hidden)
    return outs[:-3], *outs[-3:]


def code_kernel(place_ref, lower_ref, upper_ref, ids_ref, *rest):
    codes_ref, slots = rest[-2:]
    low, b_group = codes_ref.shape[2:]
    block = min(b_group, BLOCK)
    place = places(low)
    lines = [
        [words_ref[0, number : number + 1] for number in range(words_ref.shape[1])]
        for words_ref in (lower_ref, upper_ref)
    ]

    def one_block(number):
        for inner in range(0, block, LANES):
            where = pl.ds(pl.multiple_of(number * block + inner, LANES), LANES)
            packed = ids_ref[0, 0, :, where]
            for half, ids in enumerate((packed & 0xFFFF, packed >> HALF)):
                look_up(lines[half], ids, slots.at[half], slice(inner, inner + LANES))
        for inner in range(0, block, LANES):
            where = pl.ds(pl.multiple_of(number * block + inner, LANES), LANES)
            for half in range(2):
                codes_ref[half, 0, :, where] = tally(
                    place, slots.at[half], slice(inner, inner + LANES)
                )

    each(b_group // block, one_block)


def code_counts(own, words, packed, low, start, stop, before=None):
    groups, half, hots, b_group = packed.shape
    others = groups - 1
    size = (stop - start) * 2 * low * others * b_group
    kept = () if before is None else (before,)
    return pl.pallas_call(
        code_kernel,
        grid_spec=pltpu.PrefetchScalarGridSpec(
            num_scalar_prefetch=1,
            grid=(stop - start, others),
            in_specs=[
                pl.BlockSpec((1,) + words.shape[1:], lambda f, g, o: (f + start, 0, 0)),
                pl.BlockSpec((1,) + words.shape[1:], lambda f, g, o: (f + start + half, 0, 0)),
                pl.BlockSpec(
                    (1, 1, hots, b_group), lambda f, g, o: (o[0] ^ (g + 1), f + start, 0, 0)
                ),
            ]
            + [pl.BlockSpec(memory_space=pl.ANY)] * len(kept),
            out_specs=pl.BlockSpec((2, 1, low, b_group), lambda f, g, o: (0, f + start, 0, g)),
            scratch_shapes=[pltpu.VMEM((2, 2, hots, min(b_group, BLOCK)), jnp.int32)],
        ),
        out_shape=jax.ShapeDtypeStruct((2, half, low, others * b_group), jnp.int16),
        input_output_aliases={4: 0} if kept else {},
        compiler_params=pltpu.CompilerParams(vmem_limit_bytes=48 * MIB),
        cost_estimate=pl.CostEstimate(
            flops=size * 400, bytes_accessed=size * 2, transcendentals=0
        ),
        name="code",
    )(own, words, words, packed, *kept)


def clip_kernel(own_ref, w_out_ref, labels_ref, w_ref, *rest):
    sent_refs, clip_ref = rest[:-1], rest[-1]
    features, width, hidden = w_ref.shape
    share = features // len(sent_refs)
    tall = hidden + HALF
    own = own_ref[0]

    w_out = w_out_ref[...]
    red = sent_refs[0][:tall].astype(jnp.float32)
    for sent_ref in sent_refs[1:]:
        red = red + sent_ref[:tall].astype(jnp.float32)
    pre = red[:hidden]
    flat_sq = jnp.sum(red[hidden:], axis=0, keepdims=True)
    gate = jax.nn.sigmoid(pre)
    logit = jnp.sum(pre * gate * w_out, axis=0, keepdims=True)
    miss = jax.nn.sigmoid(logit) - labels_ref[...]
    delta = gate * (1.0 + pre * (1.0 - gate)) * w_out * miss
    delta_low = delta.astype(jnp.bfloat16)
    lanes = pre.shape[1]

    total = jnp.zeros((8, lanes), jnp.float32)
    for apart, sent_ref in enumerate(sent_refs):
        w_part = w_ref[pl.ds((own ^ apart) * share, share)].reshape(share * width, hidden)
        grad = dot(w_part, delta_low)
        square = jnp.sum((grad * grad).reshape(share, width // 8, 8, lanes), axis=1)
        repeats = sent_ref[tall:].astype(jnp.float32)
        for inner in range(share):
            total = total + square[inner] * repeats[inner : inner + 1]
    norm_sq = jnp.sum(total, axis=0, keepdims=True)
    norm_sq = norm_sq + flat_sq * jnp.sum(delta * delta, axis=0, keepdims=True)
    factor = CLIP / jnp.maximum(jnp.sqrt(norm_sq), CLIP)
    clip_ref[...] = (factor * delta).T.astype(jnp.bfloat16)


def clip_rows(own, sent, w_out, labels, w_hidden):
    features, width, hidden = w_hidden.shape
    b_dev = labels.shape[0]
    vmem = pl.BlockSpec(memory_space=pltpu.VMEM)
    return pl.pallas_call(
        clip_kernel,
        in_specs=[pl.BlockSpec(memory_space=pltpu.SMEM)] + [vmem] * (3 + len(sent)),
        out_specs=vmem,
        out_shape=jax.ShapeDtypeStruct((b_dev, hidden), jnp.bfloat16),
        compiler_params=pltpu.CompilerParams(vmem_limit_bytes=32 * MIB),
        cost_estimate=pl.CostEstimate(
            flops=2 * features * width * hidden * b_dev,
            bytes_accessed=w_hidden.size * 2,
            transcendentals=b_dev * hidden,
        ),
        name="clip",
    )(own, w_out.reshape(hidden, 1), labels.reshape(1, b_dev), w_hidden, *sent)


def split(array, parts):
    found = []
    for part in range(parts):
        found.append(array.astype(jnp.bfloat16))
        array = array - found[-1].astype(jnp.float32)
    return found


def update_kernel(
    place_ref,
    listed_ref,
    own_codes_ref,
    codes_ref,
    near_ref,
    far_ref,
    table_ref,
    touched_ref,
    words_ref,
    accum_ref,
    noise_ref,
    w_ref,
    rows_ref,
    dense_noise_ref,
    table_out,
    accum_out,
    dense_out,
    update,
    clips,
):
    step = pl.program_id(0)
    last = pl.num_programs(0) - 1
    low, b_group = own_codes_ref.shape[1:]
    groups = near_ref.shape[1]
    rows_f, width = table_ref.shape[1:]
    hidden = clips.shape[1]
    count = low * DIGITS
    block = min(b_group, BLOCK)
    features = range(PAIR)

    @pl.when(step == 0)
    def _():
        chips, rows = near_ref.shape[0], near_ref.shape[2]
        for core, source in enumerate((near_ref, far_ref)):
            for chip in range(chips):
                for group in range(groups):
                    start = group * b_group + (place_ref[1] ^ (2 * chip + core)) * rows
                    clips[pl.ds(pl.multiple_of(start, rows), rows)] = source[chip, group]

    def put(side, start, stop):
        feature = jnp.maximum(step - 1, 0) * PAIR + side
        for first in range(start, stop, BATCH):
            batch = range(first, first + BATCH)
            spots = [pl.ds(listed_ref[feature, slot], 1) for slot in batch]
            rows = [table_ref[side, spot, :] for spot in spots]
            steps = [update[side, slot : slot + 1, :] for slot in batch]
            for spot, row, one_step in zip(spots, rows, steps):
                table_out[side, spot, :] = row - one_step

    def add(group, number, sums):
        where = pl.ds(pl.multiple_of(number * block, block), block)
        at = pl.ds(pl.multiple_of(group * b_group + number * block, block), block)
        found = []
        for side in features:
            if group == 0:
                codes = own_codes_ref[side, :, where]
            else:
                start = pl.multiple_of((group - 1) * b_group + number * block, block)
                codes = codes_ref[0, side, :, pl.ds(start, block)]
            found.append(sums[side] + dot(spread(codes), clips[at]))
        return tuple(found)

    def finish(side, sums):
        parts = [
            sums[digit * low : (digit + 1) * low] * (1 / scale(digit)) for digit in range(DIGITS)
        ]
        both = jnp.concatenate(split(jnp.concatenate(parts, axis=0), 2), axis=1)
        dense = dot(rows_ref[side], both)
        dense_out[side] = dense[:, :hidden] + dense[:, hidden:] + dense_noise_ref[side]
        w_twice = jnp.concatenate([w_ref[side], w_ref[side]], axis=1)
        listed = dot(both, w_twice, NT) + noise_ref[side]

        square = jnp.concatenate(split(listed * listed, 2), axis=1)
        mean = dot(square, jnp.full((2 * width, LANES), 1 / width, jnp.bfloat16))
        shape = (LANES, LANES)
        eye = iota(shape, 0) == iota(shape, 1)
        sections = [slice(start, start + LANES) for start in range(0, count, LANES)]
        touched = touched_ref[pl.ds(step * PAIR + side, 1)]
        touched = jnp.concatenate([touched[:, lanes] for lanes in sections * 2], axis=0)
        lines = [accum_ref[side, number : number + 1] for number in range(rows_f // LANES)]
        old = pick_lanes(lines, touched >> 7, touched & (LANES - 1))
        ones = jnp.where(eye, 1.0, 0.0).astype(jnp.bfloat16)
        parts = split(old, 3)
        diagonal = jnp.concatenate(
            [
                jnp.concatenate(
                    [ones * jnp.broadcast_to(part[q : q + 1], shape) for part in parts], axis=1
                )
                for q in range(len(sections))
            ],
            axis=0,
        )
        total = mean + dot(diagonal, jnp.full((3 * LANES, LANES), 1, jnp.bfloat16))
        update[side] = listed * (LEARN / jnp.sqrt(total))

        extra = [
            jnp.sum(jnp.where(eye, mean[rows], 0.0), axis=0, keepdims=True) for rows in sections
        ]
        words = words_ref[side]
        for half, word in enumerate((words & 0xFFFF, lax.shift_right_logical(words, HALF))):
            gain = pick_lanes(extra, (word >> 10) & (DIGITS - 1), word & (LANES - 1))
            rows = slice(half * words.shape[0], (half + 1) * words.shape[0])
            accum_out[side, rows] = accum_ref[side, rows] + jnp.where(
                (word >> 8) >= LISTED, gain, 0.0
            )

    @pl.when(step < last)
    def _():
        table_out[...] = table_ref[...]
        sums = tuple(jnp.zeros((count, hidden), jnp.float32) for side in features)
        if b_group == block:
            share = count // groups
            for group in range(groups):
                for side in features:
                    put(side, group * share, (group + 1) * share)
                sums = add(group, 0, sums)
        else:
            for side in features:
                put(side, 0, count)
            for group in range(groups):
                sums = lax.fori_loop(0, b_group // block, functools.partial(add, group), sums)
        for side in features:
            finish(side, sums[side])

    @pl.when(step == last)
    def _():
        table_out[...] = table_ref[...]
        for side in features:
            put(side, 0, count)


def update_rows(
    place,
    own_codes,
    codes,
    near,
    far,
    table,
    touched,
    words,
    accum,
    noise,
    w_hidden,
    rows_t,
    dense_noise,
):
    f_dev, rows_f, width = table.shape
    low, b_group = own_codes.shape[1:]
    half, others = codes.shape[1], codes.shape[3]
    hidden = near.shape[-1]
    count = touched.shape[1]
    part = dense_noise.shape[1]
    tall = rows_f // LANES
    steps = f_dev // PAIR

    def current(i):
        return jnp.minimum(i, steps - 1)

    def now(*shape):
        return pl.BlockSpec((PAIR,) + shape, lambda i, p, s: (current(i), 0, 0))

    def before(*shape):
        return pl.BlockSpec((PAIR,) + shape, lambda i, p, s: (jnp.maximum(i - 1, 0), 0, 0))

    def whole(array):
        return pl.BlockSpec(array.shape, lambda i, p, s: (0,) * array.ndim)

    def code_place(i, p, s):
        return (current(i) // (half // PAIR), current(i) % (half // PAIR), 0, 0)

    new_table, new_accum, dense = pl.pallas_call(
        update_kernel,
        grid_spec=pltpu.PrefetchScalarGridSpec(
            num_scalar_prefetch=2,
            grid=(steps + 1,),
            in_specs=[
                now(low, b_group),
                pl.BlockSpec((1, PAIR, low, others), code_place),
                whole(near),
                whole(far),
                before(rows_f, width),
                whole(touched),
                now(*words.shape[1:]),
                now(tall, LANES),
                now(count, width),
                pl.BlockSpec(
                    (PAIR, width, hidden), lambda i, p, s: (p[1] * steps + current(i), 0, 0)
                ),
                pl.BlockSpec((PAIR, part, count), lambda i, p, s: (current(i), p[0], 0)),
                now(part, hidden),
            ],
            out_specs=[before(rows_f, width), now(tall, LANES), now(part, hidden)],
            scratch_shapes=[
                pltpu.VMEM((PAIR, count, width), jnp.float32),
                pltpu.VMEM((b_group + others, hidden), jnp.bfloat16),
            ],
        ),
        out_shape=[
            jax.ShapeDtypeStruct((f_dev, rows_f, width), jnp.float32),
            jax.ShapeDtypeStruct((f_dev, tall, LANES), jnp.float32),
            jax.ShapeDtypeStruct((f_dev, part, hidden), jnp.float32),
        ],
        compiler_params=pltpu.CompilerParams(vmem_limit_bytes=56 * MIB),
        cost_estimate=pl.CostEstimate(
            flops=2 * f_dev * count * (b_group + others) * hidden,
            bytes_accessed=table.size * 8 + codes.size * 2,
            transcendentals=0,
        ),
        name="update",
    )(
        place,
        touched,
        own_codes,
        codes,
        near,
        far,
        table,
        touched,
        words,
        accum.reshape(f_dev, tall, LANES),
        noise,
        w_hidden,
        rows_t,
        dense_noise,
    )
    return new_table, new_accum.reshape(f_dev, rows_f), dense


def swap(array, axis, apart):
    size = lax.axis_size(axis)
    return lax.ppermute(array, axis, [(i, i ^ apart) for i in range(size)])


def body(table, accum, w_hidden, w_out, ids, labels, touched, row_noise, dense_noise):
    f_dev = table.shape[0]
    b_dev = labels.shape[0]
    low = touched.shape[1] // DIGITS
    own = lax.axis_index("table")
    group = lax.axis_index("group")
    groups, tables = lax.axis_size("group"), lax.axis_size("table")
    place = jnp.stack([group, own]).astype(jnp.int32)
    own_index = own.astype(jnp.int32).reshape(1)
    group_index = group.astype(jnp.int32).reshape(1)

    half = f_dev // 2
    packed = ids[:half] | (ids[half:] << HALF)
    ids, packed = lax.optimization_barrier((ids, packed))
    packed = lax.all_gather(packed, "group")

    sent, rows_t, slots, own_codes = pool(own_index, table, touched, ids, w_hidden, b_dev)
    words = slots
    stops = [half * share // 8 for share in (1, 3, 5)] + [half]
    arrived = [sent[0]] + [swap(sent[d], "table", d) for d in range(1, tables)]
    codes = None
    if stops[0]:
        codes = code_counts(group_index, words, packed, low, 0, stops[0])
    arrived, codes = lax.optimization_barrier((arrived, codes))
    clips = clip_rows(own_index, arrived, w_out, labels, w_hidden)

    def go_on(number, codes, words, waits):
        if stops[number] > stops[number - 1]:
            span = (stops[number - 1], stops[number])
            codes = code_counts(group_index, words, packed, low, *span, codes)
        return lax.optimization_barrier((codes, waits))

    words, clips = lax.optimization_barrier((words, clips))
    column = [clips] + [swap(clips, "group", d) for d in range(1, groups)]
    codes, column = go_on(1, codes, words, column)
    column = jnp.stack(column)
    words, column = lax.optimization_barrier((words, column))
    near = [column] + [swap(column, "table", d) for d in range(2, tables, 2)]
    codes, near = go_on(2, codes, words, near)
    near = jnp.stack(near)
    words, near = lax.optimization_barrier((words, near))
    far = swap(near, "table", 1)
    codes, far = go_on(3, codes, words, far)
    return update_rows(
        place,
        own_codes,
        codes,
        near,
        far,
        table,
        touched,
        slots,
        accum,
        row_noise,
        w_hidden,
        rows_t,
        dense_noise,
    )


def solution(mesh):
    in_specs = (
        P("table", None, None),
        P("table", None),
        P(),
        P(),
        P("table", None, "group"),
        P(("group", "table")),
        P("table", None),
        P("table", None, None),
        P("table", "group", None),
    )
    out_specs = (P("table", None, None), P("table", None), P("table", "group", None))
    return jax.shard_map(body, mesh=mesh, in_specs=in_specs, out_specs=out_specs, check_vma=False)
```

```python
import functools

import jax
import jax.numpy as jnp
from jax import lax
from jax.experimental import pallas as pl
from jax.experimental.pallas import tpu as pltpu
from jax.sharding import PartitionSpec as P

CLIP = 1.0
LEARN = 0.05
LANES = 128
DIGITS = 4
HALF = 16
BLOCK = 1024
ROWS = 512
OWN, GROUP, BASE, FAR_BASE = range(4)
PAIR = 2
LISTED = 16
MIB = 1 << 20

NT = (((1,), (1,)), ((), ()))
TN = (((0,), (0,)), ((), ()))


def dot(left, right, dims=(((1,), (0,)), ((), ())), precision=None):
    return lax.dot_general(
        left, right, dims, preferred_element_type=jnp.float32, precision=precision
    )


def iota(shape, axis):
    return lax.broadcasted_iota(jnp.int32, shape, axis)


def slot_words(touched_row, rows_f):
    count = touched_row.shape[1]
    low = count // DIGITS
    tall = rows_f // LANES
    slot = iota((1, count), 1)
    rows = jnp.where((touched_row >> 7) == iota((tall, count), 0), 1.0, 0.0)
    lanes = jnp.where((touched_row & (LANES - 1)) == iota((LANES, count), 0), 1.0, 0.0)
    values = (lax.rem(slot, low), LISTED + 4 * lax.div(slot, low))
    held = jnp.concatenate([rows * value.astype(jnp.float32) for value in values], axis=0)
    parts = dot(held.astype(jnp.bfloat16), lanes.astype(jnp.bfloat16), NT).astype(jnp.int32)
    word = parts[:tall] | (parts[tall:] << 8)
    return word[: tall // 2] | (word[tall // 2 :] << HALF)


def pick_lanes(lines, row, lane):
    got = [
        jnp.take_along_axis(jnp.broadcast_to(line, row.shape), lane, axis=1) for line in lines
    ]
    bit = 1
    while len(got) > 1:
        odd = (row & bit) != 0
        got = [jnp.where(odd, got[i + 1], got[i]) for i in range(0, len(got), 2)]
        bit *= 2
    return got[0]


def look_up(lines, ids, slots, where):
    word = pick_lanes(lines, ids >> 7, ids & (LANES - 1))
    upper = ids >= len(lines) * LANES
    word = jnp.where(upper, lax.shift_right_logical(word, HALF), word) & 0xFFFF
    slots[0, :, where] = word & 0xFF
    slots[1, :, where] = jnp.left_shift(jnp.ones_like(word), (word >> 8) & (LISTED - 1))


def places(low):
    shape = (low // HALF, HALF, LANES)
    return (iota(shape, 0) * HALF + iota(shape, 1)).astype(jnp.int16)


def tally(place, slots, where):
    total = jnp.zeros(place.shape, jnp.int16)
    nothing = jnp.zeros(place.shape, jnp.int16)
    wide = (HALF, LANES)
    for hot in range(slots.shape[1]):
        one_group = jnp.broadcast_to(slots[0, hot : hot + 1, where], wide).astype(jnp.int16)
        one_code = jnp.broadcast_to(slots[1, hot : hot + 1, where], wide).astype(jnp.int16)
        hit = place == jnp.broadcast_to(one_group[None], place.shape)
        total = total + jnp.where(hit, jnp.broadcast_to(one_code[None], place.shape), nothing)
    return total.reshape(-1, LANES)


def spread(codes):
    parts = []
    for digit in range(DIGITS):
        if digit < DIGITS - 1:
            part = codes & jnp.full(codes.shape, 15 << (4 * digit), jnp.int16)
        else:
            part = lax.shift_right_logical(codes, jnp.full(codes.shape, 4 * digit, jnp.int16))
        parts.append(part.astype(jnp.bfloat16))
    return jnp.concatenate(parts, axis=0)


def scale(digit):
    return float(16**digit if digit < DIGITS - 1 else 1)


def pool_kernel(
    place_ref,
    table_ref,
    touched_ref,
    ids_ref,
    w_ref,
    sent_ref,
    rows_ref,
    words_ref,
    codes_ref,
    sums,
    same,
    slots,
):
    step = pl.program_id(0)
    rows_f, width = table_ref.shape[1:]
    hots, b_group = ids_ref.shape[1:]
    count = touched_ref.shape[1]
    low = count // DIGITS
    hidden = w_ref.shape[2]
    blocks, tall, chunk = sums.shape
    block = min(b_group, BLOCK)
    place = places(low)

    @pl.when(step == 0)
    def _():
        sums[...] = jnp.zeros_like(sums)
        same[...] = jnp.zeros_like(same)

    features = range(PAIR)
    lines = []
    for side in features:
        words = slot_words(touched_ref[pl.ds(step * PAIR + side, 1)], rows_f)
        words_ref[side] = words
        lines.append([words[number : number + 1] for number in range(words.shape[0])])
    lane = iota((HALF, LANES), 1)
    columns, picked = [], []
    for side in features:
        row = touched_ref[pl.ds(step * PAIR + side, 1)].astype(jnp.float32)
        column = jnp.broadcast_to(row, (LANES, count)).T.astype(jnp.int32).astype(jnp.int16)
        columns.append(column.reshape(count // HALF, HALF, LANES))
        picked.append(jnp.zeros((count, width), jnp.float32))
    one = jnp.ones(columns[0].shape, jnp.bfloat16)
    for start in range(0, rows_f, ROWS):
        for side in features:
            parts = []
            for first in range(start, start + ROWS, LANES):
                number = (lane + first).astype(jnp.int16)
                hit = columns[side] == jnp.broadcast_to(number[None], one.shape)
                parts.append(jnp.where(hit, one, jnp.zeros_like(one)).reshape(count, LANES))
            rows = table_ref[side, start : start + ROWS].astype(jnp.bfloat16)
            picked[side] = picked[side] + dot(jnp.concatenate(parts, axis=1), rows)
    rows_t, w_t = [], []
    for side in features:
        whole = picked[side].astype(jnp.bfloat16).T
        rows_ref[side] = whole
        parts = [
            whole[:, digit * low : (digit + 1) * low] * jnp.bfloat16(1 / scale(digit))
            for digit in range(DIGITS)
        ]
        rows_t.append(jnp.concatenate(parts, axis=1))
        w_t.append(w_ref[side].T)

    def one_block(number):
        for inner in range(0, block, chunk):
            for side in features:
                where = pl.ds(pl.multiple_of(number * block + inner, chunk), chunk)
                ids = ids_ref[side, :, where]
                look_up(lines[side], ids, slots.at[side], slice(inner, inner + chunk))
                pairs = jnp.zeros(ids.shape, jnp.float32)
                for turn in range(1, hots // 2 + 1):
                    weight = 2.0 if turn < hots // 2 else 1.0
                    pairs = pairs + jnp.where(ids == pltpu.roll(ids, turn, 0), weight, 0.0)
                pairs = jnp.sum(pairs, axis=0, keepdims=True) + hots
                part = number * (block // chunk) + inner // chunk
                same[part, pl.ds(step * PAIR + side, 1)] = pairs
        for inner in range(0, block, 2 * chunk):
            pre, square = 0.0, 0.0
            for side in features:
                parts = []
                for start in (inner, inner + chunk):
                    codes = tally(place, slots.at[side], slice(start, start + chunk))
                    where = pl.ds(pl.multiple_of(number * block + start, chunk), chunk)
                    codes_ref[side, :, where] = codes
                    parts.append(spread(codes))
                pooled = dot(rows_t[side], jnp.concatenate(parts, axis=1)).astype(jnp.bfloat16)
                wide = pooled.astype(jnp.float32)
                square += jnp.sum((wide * wide).reshape(width // HALF, HALF, 2 * chunk), axis=0)
                pre += dot(w_t[side], pooled)
            for turn in range(2):
                part = number * (block // chunk) + inner // chunk + turn
                lanes = slice(turn * chunk, (turn + 1) * chunk)
                sums[part, :hidden] += pre[:, lanes]
                sums[part, hidden:] += square[:, lanes]

    each(b_group // block, one_block)

    @pl.when(step == pl.num_programs(0) - 1)
    def _():
        for part in range(blocks):
            sent_ref[part, :tall] = sums[part].astype(jnp.bfloat16)
            sent_ref[part, tall:] = same[part].astype(jnp.bfloat16)


def each(times, step):
    if times == 1:
        step(0)
    else:

        @pl.loop(0, times)
        def _(number):
            step(number)


def pool(place, table, touched, ids, w_hidden, chunk):
    f_dev, rows_f, width = table.shape
    hots, b_group = ids.shape[1:]
    count = touched.shape[1]
    low = count // DIGITS
    hidden = w_hidden.shape[2]
    blocks = b_group // chunk
    repeat_rows = -(-f_dev // HALF) * HALF
    tall = hidden + HALF
    sent = (blocks, tall + repeat_rows, chunk)
    steps = f_dev // PAIR

    def now(*shape):
        return pl.BlockSpec((PAIR,) + shape, lambda i, p: (i, 0, 0))

    return pl.pallas_call(
        pool_kernel,
        grid_spec=pltpu.PrefetchScalarGridSpec(
            num_scalar_prefetch=1,
            grid=(steps,),
            in_specs=[
                now(rows_f, width),
                pl.BlockSpec(touched.shape, lambda i, p: (0, 0)),
                now(hots, b_group),
                pl.BlockSpec((PAIR, width, hidden), lambda i, p: (p[OWN] * steps + i, 0, 0)),
            ],
            out_specs=[
                pl.BlockSpec(sent, lambda i, p: (0, 0, 0)),
                now(width, count),
                now(rows_f // 256, LANES),
                now(low, b_group),
            ],
            scratch_shapes=[
                pltpu.VMEM((blocks, tall, chunk), jnp.float32),
                pltpu.VMEM((blocks, repeat_rows, chunk), jnp.float32),
                pltpu.VMEM((PAIR, 2, hots, min(b_group, BLOCK)), jnp.int32),
            ],
        ),
        out_shape=[
            jax.ShapeDtypeStruct(sent, jnp.bfloat16),
            jax.ShapeDtypeStruct((f_dev, width, count), jnp.bfloat16),
            jax.ShapeDtypeStruct((f_dev, rows_f // 256, LANES), jnp.int32),
            jax.ShapeDtypeStruct((f_dev, low, b_group), jnp.int16),
        ],
        compiler_params=pltpu.CompilerParams(vmem_limit_bytes=56 * MIB),
        cost_estimate=pl.CostEstimate(
            flops=2 * f_dev * count * b_group * width * 8,
            bytes_accessed=table.size * 4,
            transcendentals=0,
        ),
        name="pool",
    )(place, table, touched, ids, w_hidden)


def code_kernel(place_ref, words_ref, ids_ref, *rest):
    codes_ref, slots = rest[-2:]
    low, b_group = codes_ref.shape[1:]
    block = min(b_group, BLOCK)
    place = places(low)
    lines = [
        [words_ref[side, number : number + 1] for number in range(words_ref.shape[1])]
        for side in range(PAIR)
    ]

    def one_block(number):
        for inner in range(0, block, LANES):
            where = pl.ds(pl.multiple_of(number * block + inner, LANES), LANES)
            packed = ids_ref[0, 0, :, where]
            for side, ids in enumerate((packed & 0xFFFF, packed >> HALF)):
                look_up(lines[side], ids, slots.at[side], slice(inner, inner + LANES))
        for inner in range(0, block, LANES):
            where = pl.ds(pl.multiple_of(number * block + inner, LANES), LANES)
            for side in range(PAIR):
                codes_ref[side, :, where] = tally(
                    place, slots.at[side], slice(inner, inner + LANES)
                )

    each(b_group // block, one_block)


def code_counts(place, words, packed, low, start, stop, before=None):
    others, pairs, hots, b_group = packed.shape
    size = (stop - start) * PAIR * low * others * b_group
    kept = () if before is None else (before,)
    return pl.pallas_call(
        code_kernel,
        grid_spec=pltpu.PrefetchScalarGridSpec(
            num_scalar_prefetch=1,
            grid=(stop - start, others),
            in_specs=[
                pl.BlockSpec((PAIR,) + words.shape[1:], lambda f, g, p: (p[BASE] + f + start, 0, 0)),
                pl.BlockSpec((1, 1, hots, b_group), lambda f, g, p: (g, f + start, 0, 0)),
            ]
            + [pl.BlockSpec(memory_space=pl.ANY)] * len(kept),
            out_specs=pl.BlockSpec((PAIR, low, b_group), lambda f, g, p: (f + start, 0, g)),
            scratch_shapes=[pltpu.VMEM((PAIR, 2, hots, min(b_group, BLOCK)), jnp.int32)],
        ),
        out_shape=jax.ShapeDtypeStruct((pairs * PAIR, low, others * b_group), jnp.int16),
        input_output_aliases={3: 0} if kept else {},
        compiler_params=pltpu.CompilerParams(vmem_limit_bytes=48 * MIB),
        cost_estimate=pl.CostEstimate(
            flops=size * 400, bytes_accessed=size * 2, transcendentals=0
        ),
        name="code",
    )(place, words, packed, *kept)


def clip_kernel(w_out_ref, labels_ref, w_ref, sent_ref, clip_ref):
    features, width, hidden = w_ref.shape
    devices = sent_ref.shape[0]
    share = features // devices
    tall = hidden + HALF
    w_out = w_out_ref[...]
    red = sent_ref[0, :tall].astype(jnp.float32)
    for device in range(1, devices):
        red = red + sent_ref[device, :tall].astype(jnp.float32)
    pre = red[:hidden]
    flat_sq = jnp.sum(red[hidden:], axis=0, keepdims=True)
    gate = jax.nn.sigmoid(pre)
    logit = jnp.sum(pre * gate * w_out, axis=0, keepdims=True)
    miss = jax.nn.sigmoid(logit) - labels_ref[...]
    delta = gate * (1.0 + pre * (1.0 - gate)) * w_out * miss
    delta_low = delta.astype(jnp.bfloat16)
    lanes = pre.shape[1]

    total = jnp.zeros((8, lanes), jnp.float32)
    for device in range(devices):
        w_part = w_ref[device * share : (device + 1) * share].reshape(share * width, hidden)
        grad = dot(w_part, delta_low)
        square = jnp.sum((grad * grad).reshape(share, width // 8, 8, lanes), axis=1)
        repeats = sent_ref[device, tall:].astype(jnp.float32)
        for inner in range(share):
            total = total + square[inner] * repeats[inner : inner + 1]
    norm_sq = jnp.sum(total, axis=0, keepdims=True)
    norm_sq = norm_sq + flat_sq * jnp.sum(delta * delta, axis=0, keepdims=True)
    factor = CLIP / jnp.maximum(jnp.sqrt(norm_sq), CLIP)
    clip_ref[...] = (factor * delta).T.astype(jnp.bfloat16)


def clip_rows(sent, w_out, labels, w_hidden):
    features, width, hidden = w_hidden.shape
    b_dev = labels.shape[0]
    vmem = pl.BlockSpec(memory_space=pltpu.VMEM)
    return pl.pallas_call(
        clip_kernel,
        in_specs=[vmem] * 4,
        out_specs=vmem,
        out_shape=jax.ShapeDtypeStruct((b_dev, hidden), jnp.bfloat16),
        compiler_params=pltpu.CompilerParams(vmem_limit_bytes=32 * MIB),
        cost_estimate=pl.CostEstimate(
            flops=2 * features * width * hidden * b_dev,
            bytes_accessed=w_hidden.size * 2,
            transcendentals=b_dev * hidden,
        ),
        name="clip",
    )(w_out.reshape(hidden, 1), labels.reshape(1, b_dev), w_hidden, sent)


def split(array, parts):
    found = []
    for part in range(parts):
        found.append(array.astype(jnp.bfloat16))
        array = array - found[-1].astype(jnp.float32)
    return found


def sum_kernel(place_ref, own_codes_ref, codes_ref, near_ref, far_ref, sums_ref, clips):
    low, b_group = own_codes_ref.shape[1:]
    groups = near_ref.shape[1]
    hidden = clips.shape[1]
    count = low * DIGITS
    block = min(b_group, BLOCK)
    features = range(PAIR)

    @pl.when(pl.program_id(0) == 0)
    def _():
        chips, rows = near_ref.shape[0], near_ref.shape[2]
        for core, source in enumerate((near_ref, far_ref)):
            for chip in range(chips):
                for group in range(groups):
                    start = group * b_group + (place_ref[OWN] ^ (2 * chip + core)) * rows
                    clips[pl.ds(pl.multiple_of(start, rows), rows)] = source[chip, group]

    def add(group, number, sums):
        where = pl.ds(pl.multiple_of(number * block, block), block)
        at = pl.ds(pl.multiple_of(group * b_group + number * block, block), block)
        found = []
        for side in features:
            if group == 0:
                codes = own_codes_ref[side, :, where]
            else:
                start = pl.multiple_of((group - 1) * b_group + number * block, block)
                codes = codes_ref[side, :, pl.ds(start, block)]
            found.append(sums[side] + dot(spread(codes), clips[at]))
        return tuple(found)

    sums = tuple(jnp.zeros((count, hidden), jnp.float32) for side in features)
    for group in range(groups):
        if b_group == block:
            sums = add(group, 0, sums)
        else:
            sums = lax.fori_loop(0, b_group // block, functools.partial(add, group), sums)
    for side in features:
        for digit in range(DIGITS):
            rows = slice(digit * low, (digit + 1) * low)
            sums_ref[side, rows] = (sums[side][rows] * (1 / scale(digit))).astype(jnp.bfloat16)


def sum_clips(place, own_codes, codes, near, far, start, stop):
    low, b_group = own_codes.shape[1:]
    others = codes.shape[2]
    hidden = near.shape[-1]
    count = low * DIGITS
    features = (stop - start) * PAIR

    def whole(array):
        return pl.BlockSpec(array.shape, lambda i, p: (0,) * array.ndim)

    return pl.pallas_call(
        sum_kernel,
        grid_spec=pltpu.PrefetchScalarGridSpec(
            num_scalar_prefetch=1,
            grid=(stop - start,),
            in_specs=[
                pl.BlockSpec((PAIR, low, b_group), lambda i, p: (p[BASE] + start + i, 0, 0)),
                pl.BlockSpec((PAIR, low, others), lambda i, p: (start + i, 0, 0)),
                whole(near),
                whole(far),
            ],
            out_specs=pl.BlockSpec((PAIR, count, hidden), lambda i, p: (i, 0, 0)),
            scratch_shapes=[pltpu.VMEM((b_group + others, hidden), jnp.bfloat16)],
        ),
        out_shape=jax.ShapeDtypeStruct((features, count, hidden), jnp.bfloat16),
        compiler_params=pltpu.CompilerParams(vmem_limit_bytes=48 * MIB),
        cost_estimate=pl.CostEstimate(
            flops=2 * features * count * (b_group + others) * hidden,
            bytes_accessed=features * low * (b_group + others) * 2,
            transcendentals=0,
        ),
        name="sums",
    )(place, own_codes, codes, near, far)


def update_kernel(
    place_ref,
    first_ref,
    second_ref,
    table_ref,
    touched_ref,
    words_ref,
    accum_ref,
    noise_ref,
    w_ref,
    rows_ref,
    dense_noise_ref,
    *rest,
    base,
    cut,
):
    table_out, accum_out, dense_out, update = rest[-4:]
    step = pl.program_id(0)
    last = pl.num_programs(0) - 1
    rows_f, width = table_ref.shape[1:]
    count = first_ref.shape[1]
    features = range(PAIR)

    def touched_of(step, side):
        return touched_ref[pl.ds((place_ref[base] + step) * PAIR + side, 1)]

    def put():
        shape = (ROWS // HALF, HALF, count)
        number = (iota(shape, 0) * HALF + iota(shape, 1)).astype(jnp.int16)
        one = jnp.ones(shape, jnp.bfloat16)
        rows = [
            jnp.broadcast_to(touched_of(jnp.maximum(step - 1, 0), side), (HALF, count))
            for side in features
        ]
        for start in range(0, rows_f, ROWS):
            for side in features:
                row = (rows[side] - start).astype(jnp.int16)
                hit = number == jnp.broadcast_to(row[None], shape)
                hit = jnp.where(hit, one, jnp.zeros_like(one)).reshape(ROWS, count)
                steps = dot(hit, update[side])
                where = slice(start, start + ROWS)
                table_out[side, where] = table_ref[side, where] - (
                    steps[:, :width] + steps[:, width:]
                )

    def finish(side):
        sums = jnp.where(step < cut, first_ref[side], second_ref[side])
        dense_out[side] = dot(rows_ref[side], sums) + dense_noise_ref[side]
        listed = dot(sums, w_ref[side], NT) + noise_ref[side]

        square = jnp.concatenate(split(listed * listed, 2), axis=1)
        mean = dot(square, jnp.full((2 * width, LANES), 1 / width, jnp.bfloat16))
        shape = (LANES, LANES)
        eye = iota(shape, 0) == iota(shape, 1)
        sections = [slice(start, start + LANES) for start in range(0, count, LANES)]
        touched = touched_of(step, side)
        touched = jnp.concatenate([touched[:, lanes] for lanes in sections * 2], axis=0)
        lines = [accum_ref[side, number : number + 1] for number in range(rows_f // LANES)]
        old = pick_lanes(lines, touched >> 7, touched & (LANES - 1))
        ones = jnp.where(eye, 1.0, 0.0).astype(jnp.bfloat16)
        parts = split(old, 3)
        diagonal = jnp.concatenate(
            [
                jnp.concatenate(
                    [ones * jnp.broadcast_to(part[q : q + 1], shape) for part in parts], axis=1
                )
                for q in range(len(sections))
            ],
            axis=0,
        )
        total = mean + dot(diagonal, jnp.full((3 * LANES, LANES), 1, jnp.bfloat16))
        steps = listed * (LEARN / jnp.sqrt(total))
        update[side] = jnp.concatenate(split(steps, 2), axis=1)

        extra = [
            jnp.sum(jnp.where(eye, mean[rows], 0.0), axis=0, keepdims=True) for rows in sections
        ]
        words = words_ref[side]
        for half, word in enumerate((words & 0xFFFF, lax.shift_right_logical(words, HALF))):
            gain = pick_lanes(extra, word >> 10, word & (LANES - 1))
            rows = slice(half * words.shape[0], (half + 1) * words.shape[0])
            accum_out[side, rows] = accum_ref[side, rows] + jnp.where(
                (word >> 8) >= LISTED, gain, 0.0
            )

    @pl.when(step < last)
    def _():
        put()
        for side in features:
            finish(side)

    @pl.when(step == last)
    def _():
        put()


def update_rows(
    place, base, sums, table, touched, words, accum, noise, w_hidden, rows_t, dense_noise, before=None
):
    f_dev, rows_f, width = table.shape
    hidden = w_hidden.shape[2]
    count = touched.shape[1]
    part = dense_noise.shape[1]
    tall = rows_f // LANES
    lengths = [array.shape[0] // PAIR for array in sums]
    cut, steps = lengths[0], sum(lengths)
    first, second = (sums * 2)[:2]
    kept = () if before is None else tuple(before)

    def at(i, p):
        return p[base] + jnp.minimum(i, steps - 1)

    def now(*shape):
        return pl.BlockSpec((PAIR,) + shape, lambda i, p: (at(i, p), 0, 0))

    def late(*shape):
        return pl.BlockSpec((PAIR,) + shape, lambda i, p: (p[base] + jnp.maximum(i - 1, 0), 0, 0))

    def summed(start, length):
        return pl.BlockSpec(
            (PAIR, count, hidden), lambda i, p: (jnp.clip(i - start, 0, length - 1), 0, 0)
        )

    return pl.pallas_call(
        functools.partial(update_kernel, base=base, cut=cut),
        grid_spec=pltpu.PrefetchScalarGridSpec(
            num_scalar_prefetch=1,
            grid=(steps + 1,),
            in_specs=[
                summed(0, cut),
                summed(cut, lengths[-1]),
                late(rows_f, width),
                pl.BlockSpec(touched.shape, lambda i, p: (0, 0)),
                now(*words.shape[1:]),
                now(tall, LANES),
                now(count, width),
                pl.BlockSpec(
                    (PAIR, width, hidden),
                    lambda i, p: (p[OWN] * (f_dev // PAIR) + at(i, p), 0, 0),
                ),
                pl.BlockSpec((PAIR, part, count), lambda i, p: (at(i, p), p[GROUP], 0)),
                now(part, hidden),
            ]
            + [pl.BlockSpec(memory_space=pl.ANY)] * len(kept),
            out_specs=[late(rows_f, width), now(tall, LANES), now(part, hidden)],
            scratch_shapes=[pltpu.VMEM((PAIR, count, 2 * width), jnp.bfloat16)],
        ),
        out_shape=[
            jax.ShapeDtypeStruct((f_dev, rows_f, width), jnp.float32),
            jax.ShapeDtypeStruct((f_dev, tall, LANES), jnp.float32),
            jax.ShapeDtypeStruct((f_dev, part, hidden), jnp.float32),
        ],
        input_output_aliases={11 + number: number for number in range(len(kept))},
        compiler_params=pltpu.CompilerParams(vmem_limit_bytes=56 * MIB),
        cost_estimate=pl.CostEstimate(
            flops=4 * steps * PAIR * count * rows_f * width,
            bytes_accessed=steps * PAIR * rows_f * width * 8,
            transcendentals=0,
        ),
        name="update",
    )(
        place,
        first,
        second,
        table,
        touched,
        words,
        accum,
        noise,
        w_hidden,
        rows_t,
        dense_noise,
        *kept,
    )


def swap(array, axis, apart):
    size = lax.axis_size(axis)
    return lax.ppermute(array, axis, [(i, i ^ apart) for i in range(size)])


def body(table, accum, w_hidden, w_out, ids, labels, touched, row_noise, dense_noise):
    f_dev, rows_f = table.shape[:2]
    b_dev = labels.shape[0]
    low = touched.shape[1] // DIGITS
    groups, tables = lax.axis_size("group"), lax.axis_size("table")
    own = lax.axis_index("table").astype(jnp.int32)
    group = lax.axis_index("group").astype(jnp.int32)
    pairs = f_dev // 2 // PAIR
    base = (group & 1) * pairs
    far_base = pairs - base

    packed = ids[0::2] | (ids[1::2] << HALF)
    place = jnp.stack([own, group, base, far_base])
    halves = [lax.dynamic_slice_in_dim(packed, start, pairs, 0) for start in (base, far_base)]
    ids, halves, place = lax.optimization_barrier((ids, halves, place))
    packed = [swap(halves[d & 1], "group", d) for d in range(1, groups)]

    sent, rows_t, words, own_codes = pool(place, table, touched, ids, w_hidden, b_dev)
    packed = jnp.stack(packed)
    stops = [pairs * share // 4 for share in range(5)]

    def more_codes(number, codes, waits, ready=None):
        if stops[number + 1] > stops[number]:
            begin = words
            if ready is not None:
                begin, ready = lax.optimization_barrier((words, ready))
            codes = code_counts(
                place, begin, packed, low, stops[number], stops[number + 1], codes
            )
        return lax.optimization_barrier((codes, waits))

    arrived = lax.all_to_all(sent, "table", split_axis=0, concat_axis=0, tiled=True)
    codes, arrived = more_codes(0, None, arrived)
    clips = clip_rows(arrived, w_out, labels, w_hidden)
    column = [clips] + [swap(clips, "group", d) for d in range(1, groups)]
    codes, column = more_codes(1, codes, column, clips)
    column = jnp.stack(column)
    near = [column] + [swap(column, "table", d) for d in range(2, tables, 2)]
    codes, near = more_codes(2, codes, near, column)
    near = jnp.stack(near)
    far = swap(near, "table", 1)
    codes, far = more_codes(3, codes, far, near)

    cut = (pairs + 1) // 2
    mine = [sum_clips(place, own_codes, codes, near, far, 0, cut)]
    theirs = [swap(mine[0], "group", 1)]
    if cut < pairs:
        codes, mine[0] = lax.optimization_barrier((codes, mine[0]))
        mine.append(sum_clips(place, own_codes, codes, near, far, cut, pairs))
        theirs.append(swap(mine[1], "group", 1))
    given = (table, touched, words, accum.reshape(f_dev, rows_f // LANES, LANES), row_noise)
    given += (w_hidden, rows_t, dense_noise)
    found = update_rows(place, BASE, mine, *given)
    found = update_rows(place, FAR_BASE, theirs, *given, found)
    new_table, new_accum, dense = found
    return new_table, new_accum.reshape(f_dev, rows_f), dense


def solution(mesh):
    in_specs = (
        P("table", None, None),
        P("table", None),
        P(),
        P(),
        P("table", None, "group"),
        P(("group", "table")),
        P("table", None),
        P("table", None, None),
        P("table", "group", None),
    )
    out_specs = (P("table", None, None), P("table", None), P("table", "group", None))
    return jax.shard_map(body, mesh=mesh, in_specs=in_specs, out_specs=out_specs, check_vma=False)
```

```python
import functools

import jax
import jax.numpy as jnp
from jax import lax
from jax.experimental import pallas as pl
from jax.experimental.pallas import tpu as pltpu
from jax.sharding import PartitionSpec as P

CLIP = 1.0
LEARN = 0.05
LANES = 128
DIGITS = 4
HALF = 16
BLOCK = 1024
ROWS = 512
OWN, GROUP, BASE, FAR_BASE = range(4)
PAIR = 2
LISTED = 16
MIB = 1 << 20

NT = (((1,), (1,)), ((), ()))
TN = (((0,), (0,)), ((), ()))


def dot(left, right, dims=(((1,), (0,)), ((), ())), precision=None):
    return lax.dot_general(
        left, right, dims, preferred_element_type=jnp.float32, precision=precision
    )


def iota(shape, axis):
    return lax.broadcasted_iota(jnp.int32, shape, axis)


def slot_words(touched_row, rows_f):
    count = touched_row.shape[1]
    low = count // DIGITS
    tall = rows_f // LANES
    slot = iota((1, count), 1)
    rows = jnp.where((touched_row >> 7) == iota((tall, count), 0), 1.0, 0.0)
    lanes = jnp.where((touched_row & (LANES - 1)) == iota((LANES, count), 0), 1.0, 0.0)
    values = (lax.rem(slot, low), LISTED + 4 * lax.div(slot, low))
    held = jnp.concatenate([rows * value.astype(jnp.float32) for value in values], axis=0)
    parts = dot(held.astype(jnp.bfloat16), lanes.astype(jnp.bfloat16), NT).astype(jnp.int32)
    word = parts[:tall] | (parts[tall:] << 8)
    return word[: tall // 2] | (word[tall // 2 :] << HALF)


def pick_lanes(lines, row, lane):
    got = [
        jnp.take_along_axis(jnp.broadcast_to(line, row.shape), lane, axis=1) for line in lines
    ]
    bit = 1
    while len(got) > 1:
        odd = (row & bit) != 0
        got = [jnp.where(odd, got[i + 1], got[i]) for i in range(0, len(got), 2)]
        bit *= 2
    return got[0]


def look_up(lines, ids, slots, where):
    word = pick_lanes(lines, ids >> 7, ids & (LANES - 1))
    upper = ids >= len(lines) * LANES
    word = jnp.where(upper, lax.shift_right_logical(word, HALF), word) & 0xFFFF
    slots[0, :, where] = word & 0xFF
    slots[1, :, where] = jnp.left_shift(jnp.ones_like(word), (word >> 8) & (LISTED - 1))


def places(low):
    shape = (low // HALF, HALF, LANES)
    return (iota(shape, 0) * HALF + iota(shape, 1)).astype(jnp.int16)


def tally(place, slots, where):
    total = None
    nothing = jnp.zeros(place.shape, jnp.int16)
    wide = (HALF, LANES)
    for hot in range(slots.shape[1]):
        one_group = jnp.broadcast_to(slots[0, hot : hot + 1, where], wide).astype(jnp.int16)
        one_code = jnp.broadcast_to(slots[1, hot : hot + 1, where], wide).astype(jnp.int16)
        hit = place == jnp.broadcast_to(one_group[None], place.shape)
        part = jnp.where(hit, jnp.broadcast_to(one_code[None], place.shape), nothing)
        total = part if total is None else total + part
    return total.reshape(-1, LANES)


def spread(codes):
    parts = []
    for digit in range(DIGITS):
        if digit < DIGITS - 1:
            part = codes & jnp.full(codes.shape, 15 << (4 * digit), jnp.int16)
        else:
            part = lax.shift_right_logical(codes, jnp.full(codes.shape, 4 * digit, jnp.int16))
        parts.append(part.astype(jnp.bfloat16))
    return jnp.concatenate(parts, axis=0)


def scale(digit):
    return float(16**digit if digit < DIGITS - 1 else 1)


def pool_kernel(
    place_ref,
    table_ref,
    touched_ref,
    ids_ref,
    w_ref,
    sent_ref,
    rows_ref,
    words_ref,
    codes_ref,
    sums,
    same,
    slots,
):
    step = pl.program_id(0)
    rows_f, width = table_ref.shape[1:]
    hots, b_group = ids_ref.shape[1:]
    count = touched_ref.shape[1]
    low = count // DIGITS
    hidden = w_ref.shape[2]
    blocks, tall, chunk = sums.shape
    block = min(b_group, BLOCK)
    place = places(low)

    @pl.when(step == 0)
    def _():
        sums[...] = jnp.zeros_like(sums)
        same[...] = jnp.zeros_like(same)

    features = range(PAIR)
    lines = []
    for side in features:
        words = slot_words(touched_ref[pl.ds(step * PAIR + side, 1)], rows_f)
        words_ref[side] = words
        lines.append([words[number : number + 1] for number in range(words.shape[0])])
    lane = iota((HALF, LANES), 1)
    columns, picked = [], []
    for side in features:
        row = touched_ref[pl.ds(step * PAIR + side, 1)].astype(jnp.float32)
        column = jnp.broadcast_to(row, (LANES, count)).T.astype(jnp.int32).astype(jnp.int16)
        columns.append(column.reshape(count // HALF, HALF, LANES))
        picked.append(jnp.zeros((count, width), jnp.float32))
    one = jnp.ones(columns[0].shape, jnp.bfloat16)
    for start in range(0, rows_f, ROWS):
        for side in features:
            parts = []
            for first in range(start, start + ROWS, LANES):
                number = (lane + first).astype(jnp.int16)
                hit = columns[side] == jnp.broadcast_to(number[None], one.shape)
                parts.append(jnp.where(hit, one, jnp.zeros_like(one)).reshape(count, LANES))
            rows = table_ref[side, start : start + ROWS].astype(jnp.bfloat16)
            picked[side] = picked[side] + dot(jnp.concatenate(parts, axis=1), rows)
    rows_t, w_t = [], []
    for side in features:
        whole = picked[side].astype(jnp.bfloat16).T
        rows_ref[side] = whole
        parts = [
            whole[:, digit * low : (digit + 1) * low] * jnp.bfloat16(1 / scale(digit))
            for digit in range(DIGITS)
        ]
        rows_t.append(jnp.concatenate(parts, axis=1))
        w_t.append(w_ref[side].T)

    def one_block(number):
        for inner in range(0, block, chunk):
            for side in features:
                where = pl.ds(pl.multiple_of(number * block + inner, chunk), chunk)
                ids = ids_ref[side, :, where]
                look_up(lines[side], ids, slots.at[side], slice(inner, inner + chunk))
                pairs = jnp.zeros(ids.shape, jnp.float32)
                for turn in range(1, hots // 2 + 1):
                    weight = 2.0 if turn < hots // 2 else 1.0
                    pairs = pairs + jnp.where(ids == pltpu.roll(ids, turn, 0), weight, 0.0)
                pairs = jnp.sum(pairs, axis=0, keepdims=True) + hots
                part = number * (block // chunk) + inner // chunk
                same[part, pl.ds(step * PAIR + side, 1)] = pairs
        for inner in range(0, block, 2 * chunk):
            pre, square = 0.0, 0.0
            for side in features:
                parts = []
                for start in (inner, inner + chunk):
                    codes = tally(place, slots.at[side], slice(start, start + chunk))
                    where = pl.ds(pl.multiple_of(number * block + start, chunk), chunk)
                    codes_ref[side, :, where] = codes
                    parts.append(spread(codes))
                pooled = dot(rows_t[side], jnp.concatenate(parts, axis=1)).astype(jnp.bfloat16)
                wide = pooled.astype(jnp.float32)
                square += jnp.sum((wide * wide).reshape(width // HALF, HALF, 2 * chunk), axis=0)
                pre += dot(w_t[side], pooled)
            for turn in range(2):
                part = number * (block // chunk) + inner // chunk + turn
                lanes = slice(turn * chunk, (turn + 1) * chunk)
                sums[part, :hidden] += pre[:, lanes]
                sums[part, hidden:] += square[:, lanes]

    each(b_group // block, one_block)

    @pl.when(step == pl.num_programs(0) - 1)
    def _():
        for part in range(blocks):
            sent_ref[part, :tall] = sums[part].astype(jnp.bfloat16)
            sent_ref[part, tall:] = same[part].astype(jnp.bfloat16)


def each(times, step):
    if times == 1:
        step(0)
    else:

        @pl.loop(0, times)
        def _(number):
            step(number)


def pool(place, table, touched, ids, w_hidden, chunk):
    f_dev, rows_f, width = table.shape
    hots, b_group = ids.shape[1:]
    count = touched.shape[1]
    low = count // DIGITS
    hidden = w_hidden.shape[2]
    blocks = b_group // chunk
    repeat_rows = -(-f_dev // HALF) * HALF
    tall = hidden + HALF
    sent = (blocks, tall + repeat_rows, chunk)
    steps = f_dev // PAIR

    def now(*shape):
        return pl.BlockSpec((PAIR,) + shape, lambda i, p: (i, 0, 0))

    return pl.pallas_call(
        pool_kernel,
        grid_spec=pltpu.PrefetchScalarGridSpec(
            num_scalar_prefetch=1,
            grid=(steps,),
            in_specs=[
                now(rows_f, width),
                pl.BlockSpec(touched.shape, lambda i, p: (0, 0)),
                now(hots, b_group),
                pl.BlockSpec((PAIR, width, hidden), lambda i, p: (p[OWN] * steps + i, 0, 0)),
            ],
            out_specs=[
                pl.BlockSpec(sent, lambda i, p: (0, 0, 0)),
                now(width, count),
                now(rows_f // 256, LANES),
                now(low, b_group),
            ],
            scratch_shapes=[
                pltpu.VMEM((blocks, tall, chunk), jnp.float32),
                pltpu.VMEM((blocks, repeat_rows, chunk), jnp.float32),
                pltpu.VMEM((PAIR, 2, hots, min(b_group, BLOCK)), jnp.int32),
            ],
        ),
        out_shape=[
            jax.ShapeDtypeStruct(sent, jnp.bfloat16),
            jax.ShapeDtypeStruct((f_dev, width, count), jnp.bfloat16),
            jax.ShapeDtypeStruct((f_dev, rows_f // 256, LANES), jnp.int32),
            jax.ShapeDtypeStruct((f_dev, low, b_group), jnp.int16),
        ],
        compiler_params=pltpu.CompilerParams(vmem_limit_bytes=56 * MIB),
        cost_estimate=pl.CostEstimate(
            flops=2 * f_dev * count * b_group * width * 8,
            bytes_accessed=table.size * 4,
            transcendentals=0,
        ),
        name="pool",
    )(place, table, touched, ids, w_hidden)


def code_kernel(place_ref, words_ref, ids_ref, *rest):
    codes_ref, slots = rest[-2:]
    low, b_group = codes_ref.shape[1:]
    block = min(b_group, BLOCK)
    place = places(low)
    lines = [
        [words_ref[side, number : number + 1] for number in range(words_ref.shape[1])]
        for side in range(PAIR)
    ]

    def one_block(number):
        for inner in range(0, block, LANES):
            where = pl.ds(pl.multiple_of(number * block + inner, LANES), LANES)
            packed = ids_ref[0, 0, :, where]
            for side, ids in enumerate((packed & 0xFFFF, packed >> HALF)):
                look_up(lines[side], ids, slots.at[side], slice(inner, inner + LANES))
        for inner in range(0, block, LANES):
            where = pl.ds(pl.multiple_of(number * block + inner, LANES), LANES)
            for side in range(PAIR):
                codes_ref[side, :, where] = tally(
                    place, slots.at[side], slice(inner, inner + LANES)
                )

    each(b_group // block, one_block)


def code_counts(place, words, packed, low, start, stop, before=None):
    others, pairs, hots, b_group = packed.shape
    size = (stop - start) * PAIR * low * others * b_group
    kept = () if before is None else (before,)
    return pl.pallas_call(
        code_kernel,
        grid_spec=pltpu.PrefetchScalarGridSpec(
            num_scalar_prefetch=1,
            grid=(stop - start, others),
            in_specs=[
                pl.BlockSpec((PAIR,) + words.shape[1:], lambda f, g, p: (p[BASE] + f + start, 0, 0)),
                pl.BlockSpec((1, 1, hots, b_group), lambda f, g, p: (g, f + start, 0, 0)),
            ]
            + [pl.BlockSpec(memory_space=pl.ANY)] * len(kept),
            out_specs=pl.BlockSpec((PAIR, low, b_group), lambda f, g, p: (f + start, 0, g)),
            scratch_shapes=[pltpu.VMEM((PAIR, 2, hots, min(b_group, BLOCK)), jnp.int32)],
        ),
        out_shape=jax.ShapeDtypeStruct((pairs * PAIR, low, others * b_group), jnp.int16),
        input_output_aliases={3: 0} if kept else {},
        compiler_params=pltpu.CompilerParams(vmem_limit_bytes=48 * MIB),
        cost_estimate=pl.CostEstimate(
            flops=size * 400, bytes_accessed=size * 2, transcendentals=0
        ),
        name="code",
    )(place, words, packed, *kept)


def clip_kernel(w_out_ref, labels_ref, w_ref, sent_ref, clip_ref):
    features, width, hidden = w_ref.shape
    devices = sent_ref.shape[0]
    share = features // devices
    tall = hidden + HALF
    w_out = w_out_ref[...]
    red = sent_ref[0, :tall].astype(jnp.float32)
    for device in range(1, devices):
        red = red + sent_ref[device, :tall].astype(jnp.float32)
    pre = red[:hidden]
    flat_sq = jnp.sum(red[hidden:], axis=0, keepdims=True)
    gate = jax.nn.sigmoid(pre)
    logit = jnp.sum(pre * gate * w_out, axis=0, keepdims=True)
    miss = jax.nn.sigmoid(logit) - labels_ref[...]
    delta = gate * (1.0 + pre * (1.0 - gate)) * w_out * miss
    delta_low = delta.astype(jnp.bfloat16)
    lanes = pre.shape[1]

    total = jnp.zeros((8, lanes), jnp.float32)
    for device in range(devices):
        w_part = w_ref[device * share : (device + 1) * share].reshape(share * width, hidden)
        grad = dot(w_part, delta_low)
        square = jnp.sum((grad * grad).reshape(share, width // 8, 8, lanes), axis=1)
        repeats = sent_ref[device, tall:].astype(jnp.float32)
        for inner in range(share):
            total = total + square[inner] * repeats[inner : inner + 1]
    norm_sq = jnp.sum(total, axis=0, keepdims=True)
    norm_sq = norm_sq + flat_sq * jnp.sum(delta * delta, axis=0, keepdims=True)
    factor = CLIP / jnp.maximum(jnp.sqrt(norm_sq), CLIP)
    clip_ref[...] = (factor * delta).T.astype(jnp.bfloat16)


def clip_rows(sent, w_out, labels, w_hidden):
    features, width, hidden = w_hidden.shape
    b_dev = labels.shape[0]
    vmem = pl.BlockSpec(memory_space=pltpu.VMEM)
    return pl.pallas_call(
        clip_kernel,
        in_specs=[vmem] * 4,
        out_specs=vmem,
        out_shape=jax.ShapeDtypeStruct((b_dev, hidden), jnp.bfloat16),
        compiler_params=pltpu.CompilerParams(vmem_limit_bytes=32 * MIB),
        cost_estimate=pl.CostEstimate(
            flops=2 * features * width * hidden * b_dev,
            bytes_accessed=w_hidden.size * 2,
            transcendentals=b_dev * hidden,
        ),
        name="clip",
    )(w_out.reshape(hidden, 1), labels.reshape(1, b_dev), w_hidden, sent)


def split(array, parts):
    found = []
    for part in range(parts):
        found.append(array.astype(jnp.bfloat16))
        array = array - found[-1].astype(jnp.float32)
    return found


def sum_kernel(place_ref, own_codes_ref, codes_ref, near_ref, far_ref, sums_ref, clips):
    low, b_group = own_codes_ref.shape[1:]
    groups = near_ref.shape[1]
    hidden = clips.shape[1]
    count = low * DIGITS
    block = min(b_group, BLOCK)
    features = range(PAIR)

    @pl.when(pl.program_id(0) == 0)
    def _():
        chips, rows = near_ref.shape[0], near_ref.shape[2]
        for core, source in enumerate((near_ref, far_ref)):
            for chip in range(chips):
                for group in range(groups):
                    start = group * b_group + (place_ref[OWN] ^ (2 * chip + core)) * rows
                    clips[pl.ds(pl.multiple_of(start, rows), rows)] = source[chip, group]

    def add(group, number, sums):
        where = pl.ds(pl.multiple_of(number * block, block), block)
        at = pl.ds(pl.multiple_of(group * b_group + number * block, block), block)
        found = []
        for side in features:
            if group == 0:
                codes = own_codes_ref[side, :, where]
            else:
                start = pl.multiple_of((group - 1) * b_group + number * block, block)
                codes = codes_ref[side, :, pl.ds(start, block)]
            found.append(sums[side] + dot(spread(codes), clips[at]))
        return tuple(found)

    sums = tuple(jnp.zeros((count, hidden), jnp.float32) for side in features)
    for group in range(groups):
        if b_group == block:
            sums = add(group, 0, sums)
        else:
            sums = lax.fori_loop(0, b_group // block, functools.partial(add, group), sums)
    for side in features:
        for digit in range(DIGITS):
            rows = slice(digit * low, (digit + 1) * low)
            sums_ref[side, rows] = (sums[side][rows] * (1 / scale(digit))).astype(jnp.bfloat16)


def sum_clips(place, own_codes, codes, near, far, start, stop):
    low, b_group = own_codes.shape[1:]
    others = codes.shape[2]
    hidden = near.shape[-1]
    count = low * DIGITS
    features = (stop - start) * PAIR

    def whole(array):
        return pl.BlockSpec(array.shape, lambda i, p: (0,) * array.ndim)

    return pl.pallas_call(
        sum_kernel,
        grid_spec=pltpu.PrefetchScalarGridSpec(
            num_scalar_prefetch=1,
            grid=(stop - start,),
            in_specs=[
                pl.BlockSpec((PAIR, low, b_group), lambda i, p: (p[BASE] + start + i, 0, 0)),
                pl.BlockSpec((PAIR, low, others), lambda i, p: (start + i, 0, 0)),
                whole(near),
                whole(far),
            ],
            out_specs=pl.BlockSpec((PAIR, count, hidden), lambda i, p: (i, 0, 0)),
            scratch_shapes=[pltpu.VMEM((b_group + others, hidden), jnp.bfloat16)],
        ),
        out_shape=jax.ShapeDtypeStruct((features, count, hidden), jnp.bfloat16),
        compiler_params=pltpu.CompilerParams(vmem_limit_bytes=48 * MIB),
        cost_estimate=pl.CostEstimate(
            flops=2 * features * count * (b_group + others) * hidden,
            bytes_accessed=features * low * (b_group + others) * 2,
            transcendentals=0,
        ),
        name="sums",
    )(place, own_codes, codes, near, far)


def update_kernel(
    place_ref,
    first_ref,
    second_ref,
    table_ref,
    touched_ref,
    words_ref,
    accum_ref,
    noise_ref,
    w_ref,
    rows_ref,
    dense_noise_ref,
    *rest,
    base,
    cut,
):
    table_out, accum_out, dense_out, update = rest[-4:]
    step = pl.program_id(0)
    last = pl.num_programs(0) - 1
    rows_f, width = table_ref.shape[1:]
    count = first_ref.shape[1]
    features = range(PAIR)

    def touched_of(step, side):
        return touched_ref[pl.ds((place_ref[base] + step) * PAIR + side, 1)]

    def put():
        shape = (ROWS // HALF, HALF, count)
        number = (iota(shape, 0) * HALF + iota(shape, 1)).astype(jnp.int16)
        one = jnp.ones(shape, jnp.bfloat16)
        rows = [
            jnp.broadcast_to(touched_of(jnp.maximum(step - 1, 0), side), (HALF, count))
            for side in features
        ]
        for start in range(0, rows_f, ROWS):
            for side in features:
                row = (rows[side] - start).astype(jnp.int16)
                hit = number == jnp.broadcast_to(row[None], shape)
                hit = jnp.where(hit, one, jnp.zeros_like(one)).reshape(ROWS, count)
                steps = dot(hit, update[side])
                where = slice(start, start + ROWS)
                table_out[side, where] = table_ref[side, where] - (
                    steps[:, :width] + steps[:, width:]
                )

    def finish(side):
        sums = jnp.where(step < cut, first_ref[side], second_ref[side])
        dense_out[side] = dot(rows_ref[side], sums) + dense_noise_ref[side]
        listed = dot(sums, w_ref[side], NT) + noise_ref[side]

        square = jnp.concatenate(split(listed * listed, 2), axis=1)
        mean = dot(square, jnp.full((2 * width, LANES), 1 / width, jnp.bfloat16))
        shape = (LANES, LANES)
        eye = iota(shape, 0) == iota(shape, 1)
        sections = [slice(start, start + LANES) for start in range(0, count, LANES)]
        touched = touched_of(step, side)
        touched = jnp.concatenate([touched[:, lanes] for lanes in sections * 2], axis=0)
        lines = [accum_ref[side, number : number + 1] for number in range(rows_f // LANES)]
        old = pick_lanes(lines, touched >> 7, touched & (LANES - 1))
        extra = [
            jnp.sum(jnp.where(eye, mean[rows], 0.0), axis=0, keepdims=True) for rows in sections
        ]
        ones = jnp.where(eye, 1.0, 0.0).astype(jnp.bfloat16)
        parts = split(LEARN / jnp.sqrt(old + jnp.concatenate(extra * 2, axis=0)), 3)
        diagonal = jnp.concatenate(
            [
                jnp.concatenate(
                    [ones * jnp.broadcast_to(part[q : q + 1], shape) for part in parts], axis=1
                )
                for q in range(len(sections))
            ],
            axis=0,
        )
        steps = listed * dot(diagonal, jnp.full((3 * LANES, LANES), 1, jnp.bfloat16))
        update[side] = jnp.concatenate(split(steps, 2), axis=1)
        words = words_ref[side]
        for half, word in enumerate((words & 0xFFFF, lax.shift_right_logical(words, HALF))):
            gain = pick_lanes(extra, word >> 10, word & (LANES - 1))
            rows = slice(half * words.shape[0], (half + 1) * words.shape[0])
            accum_out[side, rows] = accum_ref[side, rows] + jnp.where(
                (word >> 8) >= LISTED, gain, 0.0
            )

    @pl.when(step < last)
    def _():
        put()
        for side in features:
            finish(side)

    @pl.when(step == last)
    def _():
        put()


def update_rows(
    place, base, sums, table, touched, words, accum, noise, w_hidden, rows_t, dense_noise, before=None
):
    f_dev, rows_f, width = table.shape
    hidden = w_hidden.shape[2]
    count = touched.shape[1]
    part = dense_noise.shape[1]
    tall = rows_f // LANES
    lengths = [array.shape[0] // PAIR for array in sums]
    cut, steps = lengths[0], sum(lengths)
    first, second = (sums * 2)[:2]
    kept = () if before is None else tuple(before)

    def at(i, p):
        return p[base] + jnp.minimum(i, steps - 1)

    def now(*shape):
        return pl.BlockSpec((PAIR,) + shape, lambda i, p: (at(i, p), 0, 0))

    def late(*shape):
        return pl.BlockSpec((PAIR,) + shape, lambda i, p: (p[base] + jnp.maximum(i - 1, 0), 0, 0))

    def summed(start, length):
        return pl.BlockSpec(
            (PAIR, count, hidden), lambda i, p: (jnp.clip(i - start, 0, length - 1), 0, 0)
        )

    return pl.pallas_call(
        functools.partial(update_kernel, base=base, cut=cut),
        grid_spec=pltpu.PrefetchScalarGridSpec(
            num_scalar_prefetch=1,
            grid=(steps + 1,),
            in_specs=[
                summed(0, cut),
                summed(cut, lengths[-1]),
                late(rows_f, width),
                pl.BlockSpec(touched.shape, lambda i, p: (0, 0)),
                now(*words.shape[1:]),
                now(tall, LANES),
                now(count, width),
                pl.BlockSpec(
                    (PAIR, width, hidden),
                    lambda i, p: (p[OWN] * (f_dev // PAIR) + at(i, p), 0, 0),
                ),
                pl.BlockSpec((PAIR, part, count), lambda i, p: (at(i, p), p[GROUP], 0)),
                now(part, hidden),
            ]
            + [pl.BlockSpec(memory_space=pl.ANY)] * len(kept),
            out_specs=[late(rows_f, width), now(tall, LANES), now(part, hidden)],
            scratch_shapes=[pltpu.VMEM((PAIR, count, 2 * width), jnp.bfloat16)],
        ),
        out_shape=[
            jax.ShapeDtypeStruct((f_dev, rows_f, width), jnp.float32),
            jax.ShapeDtypeStruct((f_dev, tall, LANES), jnp.float32),
            jax.ShapeDtypeStruct((f_dev, part, hidden), jnp.float32),
        ],
        input_output_aliases={11 + number: number for number in range(len(kept))},
        compiler_params=pltpu.CompilerParams(vmem_limit_bytes=56 * MIB),
        cost_estimate=pl.CostEstimate(
            flops=steps * count * hidden, bytes_accessed=steps * count, transcendentals=0
        ),
        name="update",
    )(
        place,
        first,
        second,
        table,
        touched,
        words,
        accum,
        noise,
        w_hidden,
        rows_t,
        dense_noise,
        *kept,
    )


def swap(array, axis, apart):
    size = lax.axis_size(axis)
    return lax.ppermute(array, axis, [(i, i ^ apart) for i in range(size)])


def body(table, accum, w_hidden, w_out, ids, labels, touched, row_noise, dense_noise):
    f_dev, rows_f = table.shape[:2]
    b_dev = labels.shape[0]
    low = touched.shape[1] // DIGITS
    groups, tables = lax.axis_size("group"), lax.axis_size("table")
    own = lax.axis_index("table").astype(jnp.int32)
    group = lax.axis_index("group").astype(jnp.int32)
    pairs = f_dev // 2 // PAIR
    base = (group & 1) * pairs
    far_base = pairs - base

    packed = ids[0::2] | (ids[1::2] << HALF)
    place = jnp.stack([own, group, base, far_base])
    halves = [lax.dynamic_slice_in_dim(packed, start, pairs, 0) for start in (base, far_base)]
    ids, halves, place = lax.optimization_barrier((ids, halves, place))
    packed = [swap(halves[d & 1], "group", d) for d in range(1, groups)]

    sent, rows_t, words, own_codes = pool(place, table, touched, ids, w_hidden, b_dev)
    packed = jnp.stack(packed)
    stops = [pairs * share // 4 for share in range(5)]

    def more_codes(number, codes, waits, ready=None):
        if stops[number + 1] > stops[number]:
            begin = words
            if ready is not None:
                begin, ready = lax.optimization_barrier((words, ready))
            codes = code_counts(
                place, begin, packed, low, stops[number], stops[number + 1], codes
            )
        return lax.optimization_barrier((codes, waits))

    sent, packed = lax.optimization_barrier((sent, packed))
    arrived = lax.all_to_all(sent, "table", split_axis=0, concat_axis=0, tiled=True)
    codes, arrived = more_codes(0, None, arrived)
    clips = clip_rows(arrived, w_out, labels, w_hidden)
    column = [clips] + [swap(clips, "group", d) for d in range(1, groups)]
    codes, column = more_codes(1, codes, column, clips)
    column = jnp.stack(column)
    near = [column] + [swap(column, "table", d) for d in range(2, tables, 2)]
    codes, near = more_codes(2, codes, near, column)
    near = jnp.stack(near)
    far = swap(near, "table", 1)
    codes, far = more_codes(3, codes, far, near)

    cut = (pairs + 1) // 2
    mine = [sum_clips(place, own_codes, codes, near, far, 0, cut)]
    theirs = [swap(mine[0], "group", 1)]
    if cut < pairs:
        codes, mine[0] = lax.optimization_barrier((codes, mine[0]))
        mine.append(sum_clips(place, own_codes, codes, near, far, cut, pairs))
        theirs.append(swap(mine[1], "group", 1))
    given = (table, touched, words, accum.reshape(f_dev, rows_f // LANES, LANES), row_noise)
    given += (w_hidden, rows_t, dense_noise)
    mine, theirs[0] = lax.optimization_barrier((mine, theirs[0]))
    found = update_rows(place, BASE, mine, *given)
    found = update_rows(place, FAR_BASE, theirs, *given, found)
    new_table, new_accum, dense = found
    return new_table, new_accum.reshape(f_dev, rows_f), dense


def solution(mesh):
    in_specs = (
        P("table", None, None),
        P("table", None),
        P(),
        P(),
        P("table", None, "group"),
        P(("group", "table")),
        P("table", None),
        P("table", None, None),
        P("table", "group", None),
    )
    out_specs = (P("table", None, None), P("table", None), P("table", "group", None))
    return jax.shard_map(body, mesh=mesh, in_specs=in_specs, out_specs=out_specs, check_vma=False)
```

```python
import functools

import jax
import jax.numpy as jnp
from jax import lax
from jax.experimental import pallas as pl
from jax.experimental.pallas import tpu as pltpu
from jax.sharding import PartitionSpec as P

CLIP = 1.0
LEARN = 0.05
LANES = 128
DIGITS = 4
HALF = 16
BLOCK = 1024
BATCH = 32
ROWS = 512
OWN, GROUP = range(2)
PAIR = 2
LISTED = 16
MIB = 1 << 20

NT = (((1,), (1,)), ((), ()))
TN = (((0,), (0,)), ((), ()))


def dot(left, right, dims=(((1,), (0,)), ((), ())), precision=None):
    return lax.dot_general(
        left, right, dims, preferred_element_type=jnp.float32, precision=precision
    )


def iota(shape, axis):
    return lax.broadcasted_iota(jnp.int32, shape, axis)


def slot_words(touched_row, rows_f):
    count = touched_row.shape[1]
    low = count // DIGITS
    tall = rows_f // LANES
    slot = iota((1, count), 1)
    rows = jnp.where((touched_row >> 7) == iota((tall, count), 0), 1.0, 0.0)
    lanes = jnp.where((touched_row & (LANES - 1)) == iota((LANES, count), 0), 1.0, 0.0)
    values = (lax.rem(slot, low), LISTED + 4 * lax.div(slot, low))
    held = jnp.concatenate([rows * value.astype(jnp.float32) for value in values], axis=0)
    parts = dot(held.astype(jnp.bfloat16), lanes.astype(jnp.bfloat16), NT).astype(jnp.int32)
    word = parts[:tall] | (parts[tall:] << 8)
    return word[: tall // 2] | (word[tall // 2 :] << HALF)


def pick_lanes(lines, row, lane):
    got = [
        jnp.take_along_axis(jnp.broadcast_to(line, row.shape), lane, axis=1) for line in lines
    ]
    bit = 1
    while len(got) > 1:
        odd = (row & bit) != 0
        got = [jnp.where(odd, got[i + 1], got[i]) for i in range(0, len(got), 2)]
        bit *= 2
    return got[0]


def look_up(lines, ids, slots, where):
    word = pick_lanes(lines, ids >> 7, ids & (LANES - 1))
    upper = ids >= len(lines) * LANES
    word = jnp.where(upper, lax.shift_right_logical(word, HALF), word) & 0xFFFF
    slots[0, :, where] = word & 0xFF
    slots[1, :, where] = jnp.left_shift(jnp.ones_like(word), (word >> 8) & (LISTED - 1))


def places(low):
    shape = (low // HALF, HALF, LANES)
    return (iota(shape, 0) * HALF + iota(shape, 1)).astype(jnp.int16)


def tally(place, slots, where):
    total = None
    nothing = jnp.zeros(place.shape, jnp.int16)
    wide = (HALF, LANES)
    for hot in range(slots.shape[1]):
        one_group = jnp.broadcast_to(slots[0, hot : hot + 1, where], wide).astype(jnp.int16)
        one_code = jnp.broadcast_to(slots[1, hot : hot + 1, where], wide).astype(jnp.int16)
        hit = place == jnp.broadcast_to(one_group[None], place.shape)
        part = jnp.where(hit, jnp.broadcast_to(one_code[None], place.shape), nothing)
        total = part if total is None else total + part
    return total.reshape(-1, LANES)


def spread(codes):
    parts = []
    for digit in range(DIGITS):
        if digit < DIGITS - 1:
            part = codes & jnp.full(codes.shape, 15 << (4 * digit), jnp.int16)
        else:
            part = lax.shift_right_logical(codes, jnp.full(codes.shape, 4 * digit, jnp.int16))
        parts.append(part.astype(jnp.bfloat16))
    return jnp.concatenate(parts, axis=0)


def spread_pairs(codes):
    parts = []
    lower = codes & jnp.full(codes.shape, 0xFF, jnp.int16)
    upper = lax.shift_right_logical(codes, jnp.full(codes.shape, 8, jnp.int16))
    for both in (lower.astype(jnp.bfloat16), upper.astype(jnp.bfloat16)):
        up = jnp.bfloat16(128)
        parts += [both, (both * jnp.bfloat16(1 / 16) + up) - up]
    return jnp.concatenate(parts, axis=0)


def scale(digit):
    return float(16**digit if digit < DIGITS - 1 else 1)


def pool_kernel(
    place_ref,
    table_ref,
    touched_ref,
    ids_ref,
    w_ref,
    sent_ref,
    rows_ref,
    words_ref,
    codes_ref,
    sums,
    same,
    slots,
):
    step = pl.program_id(0)
    rows_f, width = table_ref.shape[1:]
    hots, b_group = ids_ref.shape[1:]
    count = touched_ref.shape[1]
    low = count // DIGITS
    hidden = w_ref.shape[2]
    blocks, tall, chunk = sums.shape
    block = min(b_group, BLOCK)
    place = places(low)

    @pl.when(step == 0)
    def _():
        sums[...] = jnp.zeros_like(sums)
        same[...] = jnp.zeros_like(same)

    features = range(PAIR)
    lines = []
    for side in features:
        words = slot_words(touched_ref[pl.ds(step * PAIR + side, 1)], rows_f)
        words_ref[side] = words
        lines.append([words[number : number + 1] for number in range(words.shape[0])])
    lane = iota((HALF, LANES), 1)
    columns, picked = [], []
    for side in features:
        row = touched_ref[pl.ds(step * PAIR + side, 1)].astype(jnp.float32)
        column = jnp.broadcast_to(row, (LANES, count)).T.astype(jnp.int32).astype(jnp.int16)
        columns.append(column.reshape(count // HALF, HALF, LANES))
        picked.append(jnp.zeros((count, width), jnp.float32))
    one = jnp.ones(columns[0].shape, jnp.bfloat16)
    for start in range(0, rows_f, ROWS):
        for side in features:
            parts = []
            for first in range(start, start + ROWS, LANES):
                number = (lane + first).astype(jnp.int16)
                hit = columns[side] == jnp.broadcast_to(number[None], one.shape)
                parts.append(jnp.where(hit, one, jnp.zeros_like(one)).reshape(count, LANES))
            rows = table_ref[side, start : start + ROWS].astype(jnp.bfloat16)
            picked[side] = picked[side] + dot(jnp.concatenate(parts, axis=1), rows)
    rows_t, w_t = [], []
    for side in features:
        whole = picked[side].astype(jnp.bfloat16).T
        rows_ref[side] = whole
        parts = [
            whole[:, digit * low : (digit + 1) * low] * jnp.bfloat16(1 / scale(digit))
            for digit in range(DIGITS)
        ]
        rows_t.append(jnp.concatenate(parts, axis=1))
        w_t.append(w_ref[side].T)

    def one_block(number):
        for inner in range(0, block, chunk):
            for side in features:
                where = pl.ds(pl.multiple_of(number * block + inner, chunk), chunk)
                ids = ids_ref[side, :, where]
                look_up(lines[side], ids, slots.at[side], slice(inner, inner + chunk))
                pairs = jnp.zeros(ids.shape, jnp.float32)
                for turn in range(1, hots // 2 + 1):
                    weight = 2.0 if turn < hots // 2 else 1.0
                    pairs = pairs + jnp.where(ids == pltpu.roll(ids, turn, 0), weight, 0.0)
                pairs = jnp.sum(pairs, axis=0, keepdims=True) + hots
                part = number * (block // chunk) + inner // chunk
                same[part, pl.ds(step * PAIR + side, 1)] = pairs
        for inner in range(0, block, 2 * chunk):
            pre, square = 0.0, 0.0
            for side in features:
                parts = []
                for start in (inner, inner + chunk):
                    codes = tally(place, slots.at[side], slice(start, start + chunk))
                    where = pl.ds(pl.multiple_of(number * block + start, chunk), chunk)
                    codes_ref[side, :, where] = codes
                    parts.append(spread(codes))
                pooled = dot(rows_t[side], jnp.concatenate(parts, axis=1)).astype(jnp.bfloat16)
                wide = pooled.astype(jnp.float32)
                square += jnp.sum((wide * wide).reshape(width // HALF, HALF, 2 * chunk), axis=0)
                pre += dot(w_t[side], pooled)
            for turn in range(2):
                part = number * (block // chunk) + inner // chunk + turn
                lanes = slice(turn * chunk, (turn + 1) * chunk)
                sums[part, :hidden] += pre[:, lanes]
                sums[part, hidden:] += square[:, lanes]

    each(b_group // block, one_block)

    @pl.when(step == pl.num_programs(0) - 1)
    def _():
        for part in range(blocks):
            sent_ref[part, :tall] = sums[part].astype(jnp.bfloat16)
            sent_ref[part, tall:] = same[part].astype(jnp.bfloat16)


def each(times, step):
    if times == 1:
        step(0)
    else:

        @pl.loop(0, times)
        def _(number):
            step(number)


def pool(place, table, touched, ids, w_hidden, chunk):
    f_dev, rows_f, width = table.shape
    hots, b_group = ids.shape[1:]
    count = touched.shape[1]
    low = count // DIGITS
    hidden = w_hidden.shape[2]
    blocks = b_group // chunk
    repeat_rows = -(-f_dev // HALF) * HALF
    tall = hidden + HALF
    sent = (blocks, tall + repeat_rows, chunk)
    steps = f_dev // PAIR

    def now(*shape):
        return pl.BlockSpec((PAIR,) + shape, lambda i, p: (i, 0, 0))

    return pl.pallas_call(
        pool_kernel,
        grid_spec=pltpu.PrefetchScalarGridSpec(
            num_scalar_prefetch=1,
            grid=(steps,),
            in_specs=[
                now(rows_f, width),
                pl.BlockSpec(touched.shape, lambda i, p: (0, 0)),
                now(hots, b_group),
                pl.BlockSpec((PAIR, width, hidden), lambda i, p: (p[OWN] * steps + i, 0, 0)),
            ],
            out_specs=[
                pl.BlockSpec(sent, lambda i, p: (0, 0, 0)),
                now(width, count),
                now(rows_f // 256, LANES),
                now(low, b_group),
            ],
            scratch_shapes=[
                pltpu.VMEM((blocks, tall, chunk), jnp.float32),
                pltpu.VMEM((blocks, repeat_rows, chunk), jnp.float32),
                pltpu.VMEM((PAIR, 2, hots, min(b_group, BLOCK)), jnp.int32),
            ],
        ),
        out_shape=[
            jax.ShapeDtypeStruct(sent, jnp.bfloat16),
            jax.ShapeDtypeStruct((f_dev, width, count), jnp.bfloat16),
            jax.ShapeDtypeStruct((f_dev, rows_f // 256, LANES), jnp.int32),
            jax.ShapeDtypeStruct((f_dev, low, b_group), jnp.int16),
        ],
        compiler_params=pltpu.CompilerParams(vmem_limit_bytes=56 * MIB),
        cost_estimate=pl.CostEstimate(
            flops=2 * f_dev * count * b_group * width * 8,
            bytes_accessed=table.size * 4,
            transcendentals=0,
        ),
        name="pool",
    )(place, table, touched, ids, w_hidden)


def code_kernel(words_ref, ids_ref, *rest):
    codes_ref, slots = rest[-2:]
    low, b_group = codes_ref.shape[1:]
    block = min(b_group, BLOCK)
    place = places(low)
    lines = [
        [words_ref[side, number : number + 1] for number in range(words_ref.shape[1])]
        for side in range(PAIR)
    ]

    def one_block(number):
        for inner in range(0, block, LANES):
            where = pl.ds(pl.multiple_of(number * block + inner, LANES), LANES)
            packed = ids_ref[0, 0, :, where]
            for side, ids in enumerate((packed & 0xFFFF, packed >> HALF)):
                look_up(lines[side], ids, slots.at[side], slice(inner, inner + LANES))
        for inner in range(0, block, LANES):
            where = pl.ds(pl.multiple_of(number * block + inner, LANES), LANES)
            for side in range(PAIR):
                codes_ref[side, :, where] = tally(
                    place, slots.at[side], slice(inner, inner + LANES)
                )

    each(b_group // block, one_block)


def code_counts(words, packed, low, start, stop, before=None):
    others, pairs, hots, b_group = packed.shape
    size = (stop - start) * PAIR * low * others * b_group
    kept = () if before is None else (before,)
    return pl.pallas_call(
        code_kernel,
        grid=(stop - start, others),
        in_specs=[
            pl.BlockSpec((PAIR,) + words.shape[1:], lambda f, g: (f + start, 0, 0)),
            pl.BlockSpec((1, 1, hots, b_group), lambda f, g: (g, f + start, 0, 0)),
        ]
        + [pl.BlockSpec(memory_space=pl.ANY)] * len(kept),
        out_specs=pl.BlockSpec((PAIR, low, b_group), lambda f, g: (f + start, 0, g)),
        scratch_shapes=[pltpu.VMEM((PAIR, 2, hots, min(b_group, BLOCK)), jnp.int32)],
        out_shape=jax.ShapeDtypeStruct((pairs * PAIR, low, others * b_group), jnp.int16),
        input_output_aliases={2: 0} if kept else {},
        compiler_params=pltpu.CompilerParams(vmem_limit_bytes=48 * MIB),
        cost_estimate=pl.CostEstimate(
            flops=size * 400, bytes_accessed=size * 2, transcendentals=0
        ),
        name="code",
    )(words, packed, *kept)


def clip_kernel(w_out_ref, labels_ref, w_ref, sent_ref, clip_ref):
    features, width, hidden = w_ref.shape
    devices = sent_ref.shape[0]
    share = features // devices
    tall = hidden + HALF
    w_out = w_out_ref[...]
    red = sent_ref[0, :tall].astype(jnp.float32)
    for device in range(1, devices):
        red = red + sent_ref[device, :tall].astype(jnp.float32)
    pre = red[:hidden]
    flat_sq = jnp.sum(red[hidden:], axis=0, keepdims=True)
    gate = jax.nn.sigmoid(pre)
    logit = jnp.sum(pre * gate * w_out, axis=0, keepdims=True)
    miss = jax.nn.sigmoid(logit) - labels_ref[...]
    delta = gate * (1.0 + pre * (1.0 - gate)) * w_out * miss
    delta_low = delta.astype(jnp.bfloat16)
    lanes = pre.shape[1]

    total = jnp.zeros((8, lanes), jnp.float32)
    for device in range(devices):
        w_part = w_ref[device * share : (device + 1) * share].reshape(share * width, hidden)
        grad = dot(w_part, delta_low)
        square = jnp.sum((grad * grad).reshape(share, width // 8, 8, lanes), axis=1)
        repeats = sent_ref[device, tall:].astype(jnp.float32)
        for inner in range(share):
            total = total + square[inner] * repeats[inner : inner + 1]
    norm_sq = jnp.sum(total, axis=0, keepdims=True)
    norm_sq = norm_sq + flat_sq * jnp.sum(delta * delta, axis=0, keepdims=True)
    factor = CLIP / jnp.maximum(jnp.sqrt(norm_sq), CLIP)
    clip_ref[...] = (factor * delta).T.astype(jnp.bfloat16)


def clip_rows(sent, w_out, labels, w_hidden):
    features, width, hidden = w_hidden.shape
    b_dev = labels.shape[0]
    vmem = pl.BlockSpec(memory_space=pltpu.VMEM)
    return pl.pallas_call(
        clip_kernel,
        in_specs=[vmem] * 4,
        out_specs=vmem,
        out_shape=jax.ShapeDtypeStruct((b_dev, hidden), jnp.bfloat16),
        compiler_params=pltpu.CompilerParams(vmem_limit_bytes=32 * MIB),
        cost_estimate=pl.CostEstimate(
            flops=2 * features * width * hidden * b_dev,
            bytes_accessed=w_hidden.size * 2,
            transcendentals=b_dev * hidden,
        ),
        name="clip",
    )(w_out.reshape(hidden, 1), labels.reshape(1, b_dev), w_hidden, sent)


def split(array, parts):
    found = []
    for part in range(parts):
        found.append(array.astype(jnp.bfloat16))
        array = array - found[-1].astype(jnp.float32)
    return found


def update_kernel(
    place_ref,
    listed_ref,
    own_codes_ref,
    codes_ref,
    near_ref,
    far_ref,
    table_ref,
    touched_ref,
    words_ref,
    accum_ref,
    noise_ref,
    w_ref,
    rows_ref,
    dense_noise_ref,
    table_out,
    accum_out,
    dense_out,
    update,
    clips,
):
    step = pl.program_id(0)
    last = pl.num_programs(0) - 1
    low, b_group = own_codes_ref.shape[1:]
    groups = near_ref.shape[1]
    rows_f, width = table_ref.shape[1:]
    hidden = clips.shape[1]
    count = low * DIGITS
    block = min(b_group, BLOCK)
    features = range(PAIR)

    @pl.when(step == 0)
    def _():
        chips, rows = near_ref.shape[0], near_ref.shape[2]
        for core, source in enumerate((near_ref, far_ref)):
            for chip in range(chips):
                for group in range(groups):
                    start = group * b_group + (place_ref[OWN] ^ (2 * chip + core)) * rows
                    clips[pl.ds(pl.multiple_of(start, rows), rows)] = source[chip, group]

    def put(side, start, stop):
        feature = jnp.maximum(step - 1, 0) * PAIR + side
        for first in range(start, stop, BATCH):
            batch = range(first, first + BATCH)
            spots = [pl.ds(listed_ref[feature, slot], 1) for slot in batch]
            rows = [table_ref[side, spot, :] for spot in spots]
            steps = [update[side, slot : slot + 1, :] for slot in batch]
            for spot, row, one_step in zip(spots, rows, steps):
                table_out[side, spot, :] = row - one_step

    def add(group, side, number, sums):
        where = pl.ds(pl.multiple_of(number * block, block), block)
        at = pl.ds(pl.multiple_of(group * b_group + number * block, block), block)
        if group == 0:
            codes = own_codes_ref[side, :, where]
        else:
            start = pl.multiple_of((group - 1) * b_group + number * block, block)
            codes = codes_ref[side, :, pl.ds(start, block)]
        return sums + dot(spread_pairs(codes), clips[at])

    def finish(side, sums):
        parts = [sums[start : start + low] for start in range(0, count, low)]
        for pair in range(0, DIGITS, 2):
            parts[pair] = parts[pair] - 16.0 * parts[pair + 1]
        both = jnp.concatenate(split(jnp.concatenate(parts, axis=0), 2), axis=1)
        dense = dot(rows_ref[side], both)
        dense_out[side] = dense[:, :hidden] + dense[:, hidden:] + dense_noise_ref[side]
        w_twice = jnp.concatenate([w_ref[side], w_ref[side]], axis=1)
        listed = dot(both, w_twice, NT) + noise_ref[side]

        square = jnp.concatenate(split(listed * listed, 2), axis=1)
        mean = dot(square, jnp.full((2 * width, LANES), 1 / width, jnp.bfloat16))
        shape = (LANES, LANES)
        eye = iota(shape, 0) == iota(shape, 1)
        sections = [slice(start, start + LANES) for start in range(0, count, LANES)]
        touched = touched_ref[pl.ds(step * PAIR + side, 1)]
        touched = jnp.concatenate([touched[:, lanes] for lanes in sections * 2], axis=0)
        lines = [accum_ref[side, number : number + 1] for number in range(rows_f // LANES)]
        old = pick_lanes(lines, touched >> 7, touched & (LANES - 1))
        ones = jnp.where(eye, 1.0, 0.0).astype(jnp.bfloat16)
        parts = split(old, 3)
        diagonal = jnp.concatenate(
            [
                jnp.concatenate(
                    [ones * jnp.broadcast_to(part[q : q + 1], shape) for part in parts], axis=1
                )
                for q in range(len(sections))
            ],
            axis=0,
        )
        total = mean + dot(diagonal, jnp.full((3 * LANES, LANES), 1, jnp.bfloat16))
        update[side] = listed * (LEARN / jnp.sqrt(total))

        extra = [
            jnp.sum(jnp.where(eye, mean[rows], 0.0), axis=0, keepdims=True) for rows in sections
        ]
        words = words_ref[side]
        for half, word in enumerate((words & 0xFFFF, lax.shift_right_logical(words, HALF))):
            gain = pick_lanes(extra, (word >> 10) & (DIGITS - 1), word & (LANES - 1))
            rows = slice(half * words.shape[0], (half + 1) * words.shape[0])
            accum_out[side, rows] = accum_ref[side, rows] + jnp.where(
                (word >> 8) >= LISTED, gain, 0.0
            )

    @pl.when(step < last)
    def _():
        table_out[...] = table_ref[...]
        share = count // groups
        for side in features:
            sums = jnp.zeros((count, hidden), jnp.float32)
            for group in range(groups):
                put(side, group * share, (group + 1) * share)
                if b_group == block:
                    sums = add(group, side, 0, sums)
                else:
                    some = functools.partial(add, group, side)
                    sums = lax.fori_loop(0, b_group // block, some, sums)
            finish(side, sums)

    @pl.when(step == last)
    def _():
        table_out[...] = table_ref[...]
        for side in features:
            put(side, 0, count)


def update_rows(
    place,
    own_codes,
    codes,
    near,
    far,
    table,
    touched,
    words,
    accum,
    noise,
    w_hidden,
    rows_t,
    dense_noise,
):
    f_dev, rows_f, width = table.shape
    low, b_group = own_codes.shape[1:]
    others = codes.shape[2]
    hidden = near.shape[-1]
    count = touched.shape[1]
    part = dense_noise.shape[1]
    tall = rows_f // LANES
    steps = f_dev // PAIR

    def current(i):
        return jnp.minimum(i, steps - 1)

    def now(*shape):
        return pl.BlockSpec((PAIR,) + shape, lambda i, p, s: (current(i), 0, 0))

    def before(*shape):
        return pl.BlockSpec((PAIR,) + shape, lambda i, p, s: (jnp.maximum(i - 1, 0), 0, 0))

    def whole(array):
        return pl.BlockSpec(array.shape, lambda i, p, s: (0,) * array.ndim)

    new_table, new_accum, dense = pl.pallas_call(
        update_kernel,
        grid_spec=pltpu.PrefetchScalarGridSpec(
            num_scalar_prefetch=2,
            grid=(steps + 1,),
            in_specs=[
                now(low, b_group),
                now(low, others),
                whole(near),
                whole(far),
                before(rows_f, width),
                whole(touched),
                now(*words.shape[1:]),
                now(tall, LANES),
                now(count, width),
                pl.BlockSpec(
                    (PAIR, width, hidden), lambda i, p, s: (p[OWN] * steps + current(i), 0, 0)
                ),
                pl.BlockSpec((PAIR, part, count), lambda i, p, s: (current(i), p[GROUP], 0)),
                now(part, hidden),
            ],
            out_specs=[before(rows_f, width), now(tall, LANES), now(part, hidden)],
            scratch_shapes=[
                pltpu.VMEM((PAIR, count, width), jnp.float32),
                pltpu.VMEM((b_group + others, hidden), jnp.bfloat16),
            ],
        ),
        out_shape=[
            jax.ShapeDtypeStruct((f_dev, rows_f, width), jnp.float32),
            jax.ShapeDtypeStruct((f_dev, tall, LANES), jnp.float32),
            jax.ShapeDtypeStruct((f_dev, part, hidden), jnp.float32),
        ],
        compiler_params=pltpu.CompilerParams(vmem_limit_bytes=56 * MIB),
        cost_estimate=pl.CostEstimate(
            flops=2 * f_dev * count * (b_group + others) * hidden,
            bytes_accessed=table.size * 8 + codes.size * 2,
            transcendentals=0,
        ),
        name="update",
    )(
        place,
        touched,
        own_codes,
        codes,
        near,
        far,
        table,
        touched,
        words,
        accum.reshape(f_dev, tall, LANES),
        noise,
        w_hidden,
        rows_t,
        dense_noise,
    )
    return new_table, new_accum.reshape(f_dev, rows_f), dense


def swap(array, axis, apart):
    size = lax.axis_size(axis)
    return lax.ppermute(array, axis, [(i, i ^ apart) for i in range(size)])


def body(table, accum, w_hidden, w_out, ids, labels, touched, row_noise, dense_noise):
    f_dev = table.shape[0]
    b_dev = labels.shape[0]
    low = touched.shape[1] // DIGITS
    groups, tables = lax.axis_size("group"), lax.axis_size("table")
    own = lax.axis_index("table").astype(jnp.int32)
    group = lax.axis_index("group").astype(jnp.int32)
    place = jnp.stack([own, group])
    pairs = f_dev // PAIR

    packed = ids[0::2] | (ids[1::2] << HALF)
    ids, packed, place = lax.optimization_barrier((ids, packed, place))
    packed = [swap(packed, "group", d) for d in range(1, groups)]

    sent, rows_t, words, own_codes = pool(place, table, touched, ids, w_hidden, b_dev)
    packed = jnp.stack(packed)
    stops = [pairs * share // 4 for share in range(5)]

    def more_codes(number, codes, waits, ready=None):
        if stops[number + 1] > stops[number]:
            begin = words
            if ready is not None:
                begin, ready = lax.optimization_barrier((words, ready))
            codes = code_counts(
                begin, packed, low, stops[number], stops[number + 1], codes
            )
        return lax.optimization_barrier((codes, waits))

    sent, packed = lax.optimization_barrier((sent, packed))
    arrived = lax.all_to_all(sent, "table", split_axis=0, concat_axis=0, tiled=True)
    codes, arrived = more_codes(0, None, arrived)
    clips = clip_rows(arrived, w_out, labels, w_hidden)
    column = [clips] + [swap(clips, "group", d) for d in range(1, groups)]
    codes, column = more_codes(1, codes, column, clips)
    column = jnp.stack(column)
    near = [column] + [swap(column, "table", d) for d in range(2, tables, 2)]
    codes, near = more_codes(2, codes, near, column)
    near = jnp.stack(near)
    far = swap(near, "table", 1)
    codes, far = more_codes(3, codes, far, near)

    return update_rows(
        place,
        own_codes,
        codes,
        near,
        far,
        table,
        touched,
        words,
        accum,
        row_noise,
        w_hidden,
        rows_t,
        dense_noise,
    )


def solution(mesh):
    in_specs = (
        P("table", None, None),
        P("table", None),
        P(),
        P(),
        P("table", None, "group"),
        P(("group", "table")),
        P("table", None),
        P("table", None, None),
        P("table", "group", None),
    )
    out_specs = (P("table", None, None), P("table", None), P("table", "group", None))
    return jax.shard_map(body, mesh=mesh, in_specs=in_specs, out_specs=out_specs, check_vma=False)
```

```python
import functools

import jax
import jax.numpy as jnp
from jax import lax
from jax.experimental import pallas as pl
from jax.experimental.pallas import tpu as pltpu
from jax.sharding import PartitionSpec as P

CLIP = 1.0
LEARN = 0.05
LANES = 128
DIGITS = 4
HALF = 16
BLOCK = 1024
BATCH = 32
ROWS = 512
OWN, GROUP = range(2)
PAIR = 2
LISTED = 16
MIB = 1 << 20

NT = (((1,), (1,)), ((), ()))
TN = (((0,), (0,)), ((), ()))


def dot(left, right, dims=(((1,), (0,)), ((), ())), precision=None):
    return lax.dot_general(
        left, right, dims, preferred_element_type=jnp.float32, precision=precision
    )


def iota(shape, axis):
    return lax.broadcasted_iota(jnp.int32, shape, axis)


def slot_words(touched_row, rows_f):
    count = touched_row.shape[1]
    low = count // DIGITS
    tall = rows_f // LANES
    slot = iota((1, count), 1)
    rows = jnp.where((touched_row >> 7) == iota((tall, count), 0), 1.0, 0.0)
    lanes = jnp.where((touched_row & (LANES - 1)) == iota((LANES, count), 0), 1.0, 0.0)
    values = (lax.rem(slot, low), LISTED + 4 * lax.div(slot, low))
    held = jnp.concatenate([rows * value.astype(jnp.float32) for value in values], axis=0)
    parts = dot(held.astype(jnp.bfloat16), lanes.astype(jnp.bfloat16), NT).astype(jnp.int32)
    word = parts[:tall] | (parts[tall:] << 8)
    return word[: tall // 2] | (word[tall // 2 :] << HALF)


def pick_lanes(lines, row, lane):
    got = [
        jnp.take_along_axis(jnp.broadcast_to(line, row.shape), lane, axis=1) for line in lines
    ]
    bit = 1
    while len(got) > 1:
        odd = (row & bit) != 0
        got = [jnp.where(odd, got[i + 1], got[i]) for i in range(0, len(got), 2)]
        bit *= 2
    return got[0]


def look_up(lines, ids, slots, where):
    word = pick_lanes(lines, ids >> 7, ids & (LANES - 1))
    upper = ids >= len(lines) * LANES
    word = jnp.where(upper, lax.shift_right_logical(word, HALF), word) & 0xFFFF
    slots[0, :, where] = word & 0xFF
    slots[1, :, where] = jnp.left_shift(jnp.ones_like(word), (word >> 8) & (LISTED - 1))


def places(low):
    shape = (low // HALF, HALF, LANES)
    return (iota(shape, 0) * HALF + iota(shape, 1)).astype(jnp.int16)


def tally(place, slots, where):
    total = None
    nothing = jnp.zeros(place.shape, jnp.int16)
    wide = (HALF, LANES)
    for hot in range(slots.shape[1]):
        one_group = jnp.broadcast_to(slots[0, hot : hot + 1, where], wide).astype(jnp.int16)
        one_code = jnp.broadcast_to(slots[1, hot : hot + 1, where], wide).astype(jnp.int16)
        hit = place == jnp.broadcast_to(one_group[None], place.shape)
        part = jnp.where(hit, jnp.broadcast_to(one_code[None], place.shape), nothing)
        total = part if total is None else total + part
    return total.reshape(-1, LANES)


def spread(codes):
    parts = []
    for digit in range(DIGITS):
        if digit < DIGITS - 1:
            part = codes & jnp.full(codes.shape, 15 << (4 * digit), jnp.int16)
        else:
            part = lax.shift_right_logical(codes, jnp.full(codes.shape, 4 * digit, jnp.int16))
        parts.append(part.astype(jnp.bfloat16))
    return jnp.concatenate(parts, axis=0)


def scale(digit):
    return float(16**digit if digit < DIGITS - 1 else 1)


def pool_kernel(
    place_ref,
    table_ref,
    touched_ref,
    ids_ref,
    w_ref,
    sent_ref,
    rows_ref,
    words_ref,
    counts_ref,
    sums,
    same,
    slots,
):
    step = pl.program_id(0)
    rows_f, width = table_ref.shape[1:]
    hots, b_group = ids_ref.shape[1:]
    count = touched_ref.shape[1]
    low = count // DIGITS
    hidden = w_ref.shape[2]
    blocks, tall, chunk = sums.shape
    block = min(b_group, BLOCK)
    place = places(low)

    @pl.when(step == 0)
    def _():
        sums[...] = jnp.zeros_like(sums)
        same[...] = jnp.zeros_like(same)

    features = range(PAIR)
    lines = []
    for side in features:
        words = slot_words(touched_ref[pl.ds(step * PAIR + side, 1)], rows_f)
        words_ref[side] = words
        lines.append([words[number : number + 1] for number in range(words.shape[0])])
    lane = iota((HALF, LANES), 1)
    columns, picked = [], []
    for side in features:
        row = touched_ref[pl.ds(step * PAIR + side, 1)].astype(jnp.float32)
        column = jnp.broadcast_to(row, (LANES, count)).T.astype(jnp.int32).astype(jnp.int16)
        columns.append(column.reshape(count // HALF, HALF, LANES))
        picked.append(jnp.zeros((count, width), jnp.float32))
    one = jnp.ones(columns[0].shape, jnp.bfloat16)
    for start in range(0, rows_f, ROWS):
        for side in features:
            parts = []
            for first in range(start, start + ROWS, LANES):
                number = (lane + first).astype(jnp.int16)
                hit = columns[side] == jnp.broadcast_to(number[None], one.shape)
                parts.append(jnp.where(hit, one, jnp.zeros_like(one)).reshape(count, LANES))
            rows = table_ref[side, start : start + ROWS].astype(jnp.bfloat16)
            picked[side] = picked[side] + dot(jnp.concatenate(parts, axis=1), rows)
    rows_t, w_t = [], []
    for side in features:
        whole = picked[side].astype(jnp.bfloat16).T
        rows_ref[side] = whole
        parts = [
            whole[:, digit * low : (digit + 1) * low] * jnp.bfloat16(1 / scale(digit))
            for digit in range(DIGITS)
        ]
        rows_t.append(jnp.concatenate(parts, axis=1))
        w_t.append(w_ref[side].T)

    def one_block(number):
        for inner in range(0, block, chunk):
            for side in features:
                where = pl.ds(pl.multiple_of(number * block + inner, chunk), chunk)
                ids = ids_ref[side, :, where]
                look_up(lines[side], ids, slots.at[side], slice(inner, inner + chunk))
                pairs = jnp.zeros(ids.shape, jnp.float32)
                for turn in range(1, hots // 2 + 1):
                    weight = 2.0 if turn < hots // 2 else 1.0
                    pairs = pairs + jnp.where(ids == pltpu.roll(ids, turn, 0), weight, 0.0)
                pairs = jnp.sum(pairs, axis=0, keepdims=True) + hots
                part = number * (block // chunk) + inner // chunk
                same[part, pl.ds(step * PAIR + side, 1)] = pairs
        for inner in range(0, block, 2 * chunk):
            pre, square = 0.0, 0.0
            for side in features:
                parts = []
                for start in (inner, inner + chunk):
                    parts.append(
                        spread(tally(place, slots.at[side], slice(start, start + chunk)))
                    )
                counts = jnp.concatenate(parts, axis=1)
                where = pl.ds(pl.multiple_of(number * block + inner, 2 * chunk), 2 * chunk)
                counts_ref[side, :, where] = counts
                pooled = dot(rows_t[side], counts).astype(jnp.bfloat16)
                wide = pooled.astype(jnp.float32)
                square += jnp.sum((wide * wide).reshape(width // HALF, HALF, 2 * chunk), axis=0)
                pre += dot(w_t[side], pooled)
            for turn in range(2):
                part = number * (block // chunk) + inner // chunk + turn
                lanes = slice(turn * chunk, (turn + 1) * chunk)
                sums[part, :hidden] += pre[:, lanes]
                sums[part, hidden:] += square[:, lanes]

    each(b_group // block, one_block)

    @pl.when(step == pl.num_programs(0) - 1)
    def _():
        for part in range(blocks):
            sent_ref[part, :tall] = sums[part].astype(jnp.bfloat16)
            sent_ref[part, tall:] = same[part].astype(jnp.bfloat16)


def each(times, step):
    if times == 1:
        step(0)
    else:

        @pl.loop(0, times)
        def _(number):
            step(number)


def pool(place, table, touched, ids, w_hidden, chunk):
    f_dev, rows_f, width = table.shape
    hots, b_group = ids.shape[1:]
    count = touched.shape[1]
    hidden = w_hidden.shape[2]
    blocks = b_group // chunk
    repeat_rows = -(-f_dev // HALF) * HALF
    tall = hidden + HALF
    sent = (blocks, tall + repeat_rows, chunk)
    steps = f_dev // PAIR

    def now(*shape):
        return pl.BlockSpec((PAIR,) + shape, lambda i, p: (i, 0, 0))

    return pl.pallas_call(
        pool_kernel,
        grid_spec=pltpu.PrefetchScalarGridSpec(
            num_scalar_prefetch=1,
            grid=(steps,),
            in_specs=[
                now(rows_f, width),
                pl.BlockSpec(touched.shape, lambda i, p: (0, 0)),
                now(hots, b_group),
                pl.BlockSpec((PAIR, width, hidden), lambda i, p: (p[OWN] * steps + i, 0, 0)),
            ],
            out_specs=[
                pl.BlockSpec(sent, lambda i, p: (0, 0, 0)),
                now(width, count),
                now(rows_f // 256, LANES),
                now(count, b_group),
            ],
            scratch_shapes=[
                pltpu.VMEM((blocks, tall, chunk), jnp.float32),
                pltpu.VMEM((blocks, repeat_rows, chunk), jnp.float32),
                pltpu.VMEM((PAIR, 2, hots, min(b_group, BLOCK)), jnp.int32),
            ],
        ),
        out_shape=[
            jax.ShapeDtypeStruct(sent, jnp.bfloat16),
            jax.ShapeDtypeStruct((f_dev, width, count), jnp.bfloat16),
            jax.ShapeDtypeStruct((f_dev, rows_f // 256, LANES), jnp.int32),
            jax.ShapeDtypeStruct((f_dev, count, b_group), jnp.bfloat16),
        ],
        compiler_params=pltpu.CompilerParams(vmem_limit_bytes=56 * MIB),
        cost_estimate=pl.CostEstimate(
            flops=2 * f_dev * count * b_group * width * 8,
            bytes_accessed=table.size * 4,
            transcendentals=0,
        ),
        name="pool",
    )(place, table, touched, ids, w_hidden)


def code_kernel(words_ref, ids_ref, *rest):
    codes_ref, slots = rest[-2:]
    low, b_group = codes_ref.shape[1:]
    block = min(b_group, BLOCK)
    place = places(low)
    lines = [
        [words_ref[side, number : number + 1] for number in range(words_ref.shape[1])]
        for side in range(PAIR)
    ]

    def one_block(number):
        for inner in range(0, block, LANES):
            where = pl.ds(pl.multiple_of(number * block + inner, LANES), LANES)
            packed = ids_ref[0, 0, :, where]
            for side, ids in enumerate((packed & 0xFFFF, packed >> HALF)):
                look_up(lines[side], ids, slots.at[side], slice(inner, inner + LANES))
        for inner in range(0, block, LANES):
            where = pl.ds(pl.multiple_of(number * block + inner, LANES), LANES)
            for side in range(PAIR):
                codes_ref[side, :, where] = tally(
                    place, slots.at[side], slice(inner, inner + LANES)
                )

    each(b_group // block, one_block)


def code_counts(words, packed, low, start, stop, before=None):
    others, pairs, hots, b_group = packed.shape
    size = (stop - start) * PAIR * low * others * b_group
    kept = () if before is None else (before,)
    return pl.pallas_call(
        code_kernel,
        grid=(stop - start, others),
        in_specs=[
            pl.BlockSpec((PAIR,) + words.shape[1:], lambda f, g: (f + start, 0, 0)),
            pl.BlockSpec((1, 1, hots, b_group), lambda f, g: (g, f + start, 0, 0)),
        ]
        + [pl.BlockSpec(memory_space=pl.ANY)] * len(kept),
        out_specs=pl.BlockSpec((PAIR, low, b_group), lambda f, g: (f + start, 0, g)),
        scratch_shapes=[pltpu.VMEM((PAIR, 2, hots, min(b_group, BLOCK)), jnp.int32)],
        out_shape=jax.ShapeDtypeStruct((pairs * PAIR, low, others * b_group), jnp.int16),
        input_output_aliases={2: 0} if kept else {},
        compiler_params=pltpu.CompilerParams(vmem_limit_bytes=48 * MIB),
        cost_estimate=pl.CostEstimate(
            flops=size * 400, bytes_accessed=size * 2, transcendentals=0
        ),
        name="code",
    )(words, packed, *kept)


def clip_kernel(w_out_ref, labels_ref, w_ref, sent_ref, clip_ref):
    features, width, hidden = w_ref.shape
    devices = sent_ref.shape[0]
    share = features // devices
    tall = hidden + HALF
    w_out = w_out_ref[...]
    red = sent_ref[0, :tall].astype(jnp.float32)
    for device in range(1, devices):
        red = red + sent_ref[device, :tall].astype(jnp.float32)
    pre = red[:hidden]
    flat_sq = jnp.sum(red[hidden:], axis=0, keepdims=True)
    gate = jax.nn.sigmoid(pre)
    logit = jnp.sum(pre * gate * w_out, axis=0, keepdims=True)
    miss = jax.nn.sigmoid(logit) - labels_ref[...]
    delta = gate * (1.0 + pre * (1.0 - gate)) * w_out * miss
    delta_low = delta.astype(jnp.bfloat16)
    lanes = pre.shape[1]

    total = jnp.zeros((8, lanes), jnp.float32)
    for device in range(devices):
        w_part = w_ref[device * share : (device + 1) * share].reshape(share * width, hidden)
        grad = dot(w_part, delta_low)
        square = jnp.sum((grad * grad).reshape(share, width // 8, 8, lanes), axis=1)
        repeats = sent_ref[device, tall:].astype(jnp.float32)
        for inner in range(share):
            total = total + square[inner] * repeats[inner : inner + 1]
    norm_sq = jnp.sum(total, axis=0, keepdims=True)
    norm_sq = norm_sq + flat_sq * jnp.sum(delta * delta, axis=0, keepdims=True)
    factor = CLIP / jnp.maximum(jnp.sqrt(norm_sq), CLIP)
    clip_ref[...] = (factor * delta).T.astype(jnp.bfloat16)


def clip_rows(sent, w_out, labels, w_hidden):
    features, width, hidden = w_hidden.shape
    b_dev = labels.shape[0]
    vmem = pl.BlockSpec(memory_space=pltpu.VMEM)
    return pl.pallas_call(
        clip_kernel,
        in_specs=[vmem] * 4,
        out_specs=vmem,
        out_shape=jax.ShapeDtypeStruct((b_dev, hidden), jnp.bfloat16),
        compiler_params=pltpu.CompilerParams(vmem_limit_bytes=32 * MIB),
        cost_estimate=pl.CostEstimate(
            flops=2 * features * width * hidden * b_dev,
            bytes_accessed=w_hidden.size * 2,
            transcendentals=b_dev * hidden,
        ),
        name="clip",
    )(w_out.reshape(hidden, 1), labels.reshape(1, b_dev), w_hidden, sent)


def split(array, parts):
    found = []
    for part in range(parts):
        found.append(array.astype(jnp.bfloat16))
        array = array - found[-1].astype(jnp.float32)
    return found


def update_kernel(
    place_ref,
    listed_ref,
    own_counts_ref,
    codes_ref,
    near_ref,
    far_ref,
    table_ref,
    touched_ref,
    words_ref,
    accum_ref,
    noise_ref,
    w_ref,
    rows_ref,
    dense_noise_ref,
    table_out,
    accum_out,
    dense_out,
    update,
    clips,
):
    step = pl.program_id(0)
    last = pl.num_programs(0) - 1
    count, b_group = own_counts_ref.shape[1:]
    low = count // DIGITS
    groups = near_ref.shape[1]
    rows_f, width = table_ref.shape[1:]
    hidden = clips.shape[1]
    block = min(b_group, BLOCK)
    features = range(PAIR)

    @pl.when(step == 0)
    def _():
        chips, rows = near_ref.shape[0], near_ref.shape[2]
        for core, source in enumerate((near_ref, far_ref)):
            for chip in range(chips):
                for group in range(groups):
                    start = group * b_group + (place_ref[OWN] ^ (2 * chip + core)) * rows
                    clips[pl.ds(pl.multiple_of(start, rows), rows)] = source[chip, group]

    def put(side, start, stop):
        feature = jnp.maximum(step - 1, 0) * PAIR + side
        for first in range(start, stop, BATCH):
            batch = range(first, first + BATCH)
            spots = [pl.ds(listed_ref[feature, slot], 1) for slot in batch]
            rows = [table_ref[side, spot, :] for spot in spots]
            steps = [update[side, slot : slot + 1, :] for slot in batch]
            for spot, row, one_step in zip(spots, rows, steps):
                table_out[side, spot, :] = row - one_step

    def add(group, number, sums):
        where = pl.ds(pl.multiple_of(number * block, block), block)
        at = pl.ds(pl.multiple_of(group * b_group + number * block, block), block)
        found = []
        for side in features:
            if group == 0:
                counts = own_counts_ref[side, :, where]
            else:
                start = pl.multiple_of((group - 1) * b_group + number * block, block)
                counts = spread(codes_ref[side, :, pl.ds(start, block)])
            found.append(sums[side] + dot(counts, clips[at]))
        return tuple(found)

    def finish(side, sums):
        parts = [
            sums[digit * low : (digit + 1) * low] * (1 / scale(digit)) for digit in range(DIGITS)
        ]
        both = jnp.concatenate(split(jnp.concatenate(parts, axis=0), 2), axis=1)
        dense = dot(rows_ref[side], both)
        dense_out[side] = dense[:, :hidden] + dense[:, hidden:] + dense_noise_ref[side]
        w_twice = jnp.concatenate([w_ref[side], w_ref[side]], axis=1)
        listed = dot(both, w_twice, NT) + noise_ref[side]

        square = jnp.concatenate(split(listed * listed, 2), axis=1)
        mean = dot(square, jnp.full((2 * width, LANES), 1 / width, jnp.bfloat16))
        shape = (LANES, LANES)
        eye = iota(shape, 0) == iota(shape, 1)
        sections = [slice(start, start + LANES) for start in range(0, count, LANES)]
        touched = touched_ref[pl.ds(step * PAIR + side, 1)]
        touched = jnp.concatenate([touched[:, lanes] for lanes in sections * 2], axis=0)
        lines = [accum_ref[side, number : number + 1] for number in range(rows_f // LANES)]
        old = pick_lanes(lines, touched >> 7, touched & (LANES - 1))
        ones = jnp.where(eye, 1.0, 0.0).astype(jnp.bfloat16)
        parts = split(old, 3)
        diagonal = jnp.concatenate(
            [
                jnp.concatenate(
                    [ones * jnp.broadcast_to(part[q : q + 1], shape) for part in parts], axis=1
                )
                for q in range(len(sections))
            ],
            axis=0,
        )
        total = mean + dot(diagonal, jnp.full((3 * LANES, LANES), 1, jnp.bfloat16))
        update[side] = listed * (LEARN * lax.rsqrt(total))

        extra = [
            jnp.sum(jnp.where(eye, mean[rows], 0.0), axis=0, keepdims=True) for rows in sections
        ]
        words = words_ref[side]
        for half, word in enumerate((words & 0xFFFF, lax.shift_right_logical(words, HALF))):
            gain = pick_lanes(extra, (word >> 10) & (DIGITS - 1), word & (LANES - 1))
            rows = slice(half * words.shape[0], (half + 1) * words.shape[0])
            accum_out[side, rows] = accum_ref[side, rows] + jnp.where(
                (word >> 8) >= LISTED, gain, 0.0
            )

    @pl.when(step < last)
    def _():
        table_out[...] = table_ref[...]
        sums = tuple(jnp.zeros((count, hidden), jnp.float32) for side in features)
        share = count // groups
        for group in range(groups):
            for side in features:
                put(side, group * share, (group + 1) * share)
            if b_group == block:
                sums = add(group, 0, sums)
            else:
                sums = lax.fori_loop(0, b_group // block, functools.partial(add, group), sums)
        for side in features:
            finish(side, sums[side])

    @pl.when(step == last)
    def _():
        table_out[...] = table_ref[...]
        for side in features:
            put(side, 0, count)


def update_rows(
    place,
    own_counts,
    codes,
    near,
    far,
    table,
    touched,
    words,
    accum,
    noise,
    w_hidden,
    rows_t,
    dense_noise,
):
    f_dev, rows_f, width = table.shape
    count, b_group = own_counts.shape[1:]
    low = count // DIGITS
    others = codes.shape[2]
    hidden = near.shape[-1]
    part = dense_noise.shape[1]
    tall = rows_f // LANES
    steps = f_dev // PAIR

    def current(i):
        return jnp.minimum(i, steps - 1)

    def now(*shape):
        return pl.BlockSpec((PAIR,) + shape, lambda i, p, s: (current(i), 0, 0))

    def before(*shape):
        return pl.BlockSpec((PAIR,) + shape, lambda i, p, s: (jnp.maximum(i - 1, 0), 0, 0))

    def whole(array):
        return pl.BlockSpec(array.shape, lambda i, p, s: (0,) * array.ndim)

    new_table, new_accum, dense = pl.pallas_call(
        update_kernel,
        grid_spec=pltpu.PrefetchScalarGridSpec(
            num_scalar_prefetch=2,
            grid=(steps + 1,),
            in_specs=[
                now(count, b_group),
                now(low, others),
                whole(near),
                whole(far),
                before(rows_f, width),
                whole(touched),
                now(*words.shape[1:]),
                now(tall, LANES),
                now(count, width),
                pl.BlockSpec(
                    (PAIR, width, hidden), lambda i, p, s: (p[OWN] * steps + current(i), 0, 0)
                ),
                pl.BlockSpec((PAIR, part, count), lambda i, p, s: (current(i), p[GROUP], 0)),
                now(part, hidden),
            ],
            out_specs=[before(rows_f, width), now(tall, LANES), now(part, hidden)],
            scratch_shapes=[
                pltpu.VMEM((PAIR, count, width), jnp.float32),
                pltpu.VMEM((b_group + others, hidden), jnp.bfloat16),
            ],
        ),
        out_shape=[
            jax.ShapeDtypeStruct((f_dev, rows_f, width), jnp.float32),
            jax.ShapeDtypeStruct((f_dev, tall, LANES), jnp.float32),
            jax.ShapeDtypeStruct((f_dev, part, hidden), jnp.float32),
        ],
        compiler_params=pltpu.CompilerParams(vmem_limit_bytes=56 * MIB),
        cost_estimate=pl.CostEstimate(
            flops=2 * f_dev * count * (b_group + others) * hidden,
            bytes_accessed=table.size * 8 + codes.size * 2,
            transcendentals=0,
        ),
        name="update",
    )(
        place,
        touched,
        own_counts,
        codes,
        near,
        far,
        table,
        touched,
        words,
        accum.reshape(f_dev, tall, LANES),
        noise,
        w_hidden,
        rows_t,
        dense_noise,
    )
    return new_table, new_accum.reshape(f_dev, rows_f), dense


def swap(array, axis, apart):
    size = lax.axis_size(axis)
    return lax.ppermute(array, axis, [(i, i ^ apart) for i in range(size)])


def body(table, accum, w_hidden, w_out, ids, labels, touched, row_noise, dense_noise):
    f_dev = table.shape[0]
    b_dev = labels.shape[0]
    low = touched.shape[1] // DIGITS
    groups, tables = lax.axis_size("group"), lax.axis_size("table")
    own = lax.axis_index("table").astype(jnp.int32)
    group = lax.axis_index("group").astype(jnp.int32)
    place = jnp.stack([own, group])
    pairs = f_dev // PAIR

    packed = ids[0::2] | (ids[1::2] << HALF)
    ids, packed, place = lax.optimization_barrier((ids, packed, place))
    packed = [swap(packed, "group", d) for d in range(1, groups)]

    sent, rows_t, words, own_counts = pool(place, table, touched, ids, w_hidden, b_dev)
    packed = jnp.stack(packed)
    stops = [pairs * share // 4 for share in range(5)]

    def more_codes(number, codes, waits, ready=None):
        if stops[number + 1] > stops[number]:
            begin = words
            if ready is not None:
                begin, ready = lax.optimization_barrier((words, ready))
            codes = code_counts(
                begin, packed, low, stops[number], stops[number + 1], codes
            )
        return lax.optimization_barrier((codes, waits))

    sent, packed = lax.optimization_barrier((sent, packed))
    arrived = lax.all_to_all(sent, "table", split_axis=0, concat_axis=0, tiled=True)
    codes, arrived = more_codes(0, None, arrived)
    clips = clip_rows(arrived, w_out, labels, w_hidden)
    column = [clips] + [swap(clips, "group", d) for d in range(1, groups)]
    codes, column = more_codes(1, codes, column, clips)
    column = jnp.stack(column)
    near = [column] + [swap(column, "table", d) for d in range(2, tables, 2)]
    codes, near = more_codes(2, codes, near, column)
    near = jnp.stack(near)
    far = swap(near, "table", 1)
    codes, far = more_codes(3, codes, far, near)

    return update_rows(
        place,
        own_counts,
        codes,
        near,
        far,
        table,
        touched,
        words,
        accum,
        row_noise,
        w_hidden,
        rows_t,
        dense_noise,
    )


def solution(mesh):
    in_specs = (
        P("table", None, None),
        P("table", None),
        P(),
        P(),
        P("table", None, "group"),
        P(("group", "table")),
        P("table", None),
        P("table", None, None),
        P("table", "group", None),
    )
    out_specs = (P("table", None, None), P("table", None), P("table", "group", None))
    return jax.shard_map(body, mesh=mesh, in_specs=in_specs, out_specs=out_specs, check_vma=False)
```

```python
import functools

import jax
import jax.numpy as jnp
from jax import lax
from jax.experimental import pallas as pl
from jax.experimental.pallas import tpu as pltpu
from jax.sharding import PartitionSpec as P

CLIP = 1.0
LEARN = 0.05
LANES = 128
DIGITS = 4
HALF = 16
BLOCK = 1024
BATCH = 32
ROWS = 512
OWN, GROUP = range(2)
PAIR = 2
LISTED = 16
MIB = 1 << 20

NT = (((1,), (1,)), ((), ()))
TN = (((0,), (0,)), ((), ()))


def dot(left, right, dims=(((1,), (0,)), ((), ())), precision=None):
    return lax.dot_general(
        left, right, dims, preferred_element_type=jnp.float32, precision=precision
    )


def iota(shape, axis):
    return lax.broadcasted_iota(jnp.int32, shape, axis)


def slot_words(touched_row, rows_f):
    count = touched_row.shape[1]
    low = count // DIGITS
    tall = rows_f // LANES
    slot = iota((1, count), 1)
    rows = jnp.where((touched_row >> 7) == iota((tall, count), 0), 1.0, 0.0)
    lanes = jnp.where((touched_row & (LANES - 1)) == iota((LANES, count), 0), 1.0, 0.0)
    values = (lax.rem(slot, low), LISTED + 4 * lax.div(slot, low))
    held = jnp.concatenate([rows * value.astype(jnp.float32) for value in values], axis=0)
    parts = dot(held.astype(jnp.bfloat16), lanes.astype(jnp.bfloat16), NT).astype(jnp.int32)
    word = parts[:tall] | (parts[tall:] << 8)
    return word[: tall // 2] | (word[tall // 2 :] << HALF)


def pick_lanes(lines, row, lane):
    got = [
        jnp.take_along_axis(jnp.broadcast_to(line, row.shape), lane, axis=1) for line in lines
    ]
    bit = 1
    while len(got) > 1:
        odd = (row & bit) != 0
        got = [jnp.where(odd, got[i + 1], got[i]) for i in range(0, len(got), 2)]
        bit *= 2
    return got[0]


def look_up(lines, ids, slots, where):
    word = pick_lanes(lines, ids >> 7, ids & (LANES - 1))
    upper = ids >= len(lines) * LANES
    word = jnp.where(upper, lax.shift_right_logical(word, HALF), word) & 0xFFFF
    slots[0, :, where] = word & 0xFF
    slots[1, :, where] = jnp.left_shift(jnp.ones_like(word), (word >> 8) & (LISTED - 1))


def places(low):
    shape = (low // HALF, HALF, LANES)
    return (iota(shape, 0) * HALF + iota(shape, 1)).astype(jnp.int16)


def tally(place, slots, where):
    total = None
    nothing = jnp.zeros(place.shape, jnp.int16)
    wide = (HALF, LANES)
    for hot in range(slots.shape[1]):
        one_group = jnp.broadcast_to(slots[0, hot : hot + 1, where], wide).astype(jnp.int16)
        one_code = jnp.broadcast_to(slots[1, hot : hot + 1, where], wide).astype(jnp.int16)
        hit = place == jnp.broadcast_to(one_group[None], place.shape)
        part = jnp.where(hit, jnp.broadcast_to(one_code[None], place.shape), nothing)
        total = part if total is None else total + part
    return total.reshape(-1, LANES)


def spread(codes):
    parts = []
    for digit in range(DIGITS):
        if digit < DIGITS - 1:
            part = codes & jnp.full(codes.shape, 15 << (4 * digit), jnp.int16)
        else:
            part = lax.shift_right_logical(codes, jnp.full(codes.shape, 4 * digit, jnp.int16))
        parts.append(part.astype(jnp.bfloat16))
    return jnp.concatenate(parts, axis=0)


def scale(digit):
    return float(16**digit if digit < DIGITS - 1 else 1)


def pool_kernel(
    place_ref,
    table_ref,
    touched_ref,
    ids_ref,
    w_ref,
    sent_ref,
    rows_ref,
    words_ref,
    counts_ref,
    sums,
    same,
    slots,
):
    step = pl.program_id(0)
    rows_f, width = table_ref.shape[1:]
    hots, b_group = ids_ref.shape[1:]
    count = touched_ref.shape[1]
    low = count // DIGITS
    hidden = w_ref.shape[2]
    blocks, tall, chunk = sums.shape
    block = min(b_group, BLOCK)
    place = places(low)

    @pl.when(step == 0)
    def _():
        sums[...] = jnp.zeros_like(sums)
        same[...] = jnp.zeros_like(same)

    features = range(PAIR)
    lines = []
    for side in features:
        words = slot_words(touched_ref[pl.ds(step * PAIR + side, 1)], rows_f)
        words_ref[side] = words
        lines.append([words[number : number + 1] for number in range(words.shape[0])])
    lane = iota((HALF, LANES), 1)
    columns, picked = [], []
    for side in features:
        row = touched_ref[pl.ds(step * PAIR + side, 1)].astype(jnp.float32)
        column = jnp.broadcast_to(row, (LANES, count)).T.astype(jnp.int32).astype(jnp.int16)
        columns.append(column.reshape(count // HALF, HALF, LANES))
        picked.append(jnp.zeros((count, width), jnp.float32))
    one = jnp.ones(columns[0].shape, jnp.bfloat16)
    for start in range(0, rows_f, ROWS):
        for side in features:
            parts = []
            for first in range(start, start + ROWS, LANES):
                number = (lane + first).astype(jnp.int16)
                hit = columns[side] == jnp.broadcast_to(number[None], one.shape)
                parts.append(jnp.where(hit, one, jnp.zeros_like(one)).reshape(count, LANES))
            rows = table_ref[side, start : start + ROWS].astype(jnp.bfloat16)
            picked[side] = picked[side] + dot(jnp.concatenate(parts, axis=1), rows)
    rows_t, w_t = [], []
    for side in features:
        whole = picked[side].astype(jnp.bfloat16).T
        rows_ref[side] = whole
        parts = [
            whole[:, digit * low : (digit + 1) * low] * jnp.bfloat16(1 / scale(digit))
            for digit in range(DIGITS)
        ]
        rows_t.append(jnp.concatenate(parts, axis=1))
        w_t.append(w_ref[side].T)

    def one_block(number):
        for inner in range(0, block, chunk):
            for side in features:
                where = pl.ds(pl.multiple_of(number * block + inner, chunk), chunk)
                ids = ids_ref[side, :, where]
                look_up(lines[side], ids, slots.at[side], slice(inner, inner + chunk))
                pairs = jnp.zeros(ids.shape, jnp.float32)
                for turn in range(1, hots // 2 + 1):
                    weight = 2.0 if turn < hots // 2 else 1.0
                    pairs = pairs + jnp.where(ids == pltpu.roll(ids, turn, 0), weight, 0.0)
                pairs = jnp.sum(pairs, axis=0, keepdims=True) + hots
                part = number * (block // chunk) + inner // chunk
                same[part, pl.ds(step * PAIR + side, 1)] = pairs
        for inner in range(0, block, 2 * chunk):
            pre, square = 0.0, 0.0
            for side in features:
                parts = []
                for start in (inner, inner + chunk):
                    parts.append(
                        spread(tally(place, slots.at[side], slice(start, start + chunk)))
                    )
                counts = jnp.concatenate(parts, axis=1)
                where = pl.ds(pl.multiple_of(number * block + inner, 2 * chunk), 2 * chunk)
                counts_ref[side, :, where] = counts
                pooled = dot(rows_t[side], counts).astype(jnp.bfloat16)
                wide = pooled.astype(jnp.float32)
                square += jnp.sum((wide * wide).reshape(width // HALF, HALF, 2 * chunk), axis=0)
                pre += dot(w_t[side], pooled)
            for turn in range(2):
                part = number * (block // chunk) + inner // chunk + turn
                lanes = slice(turn * chunk, (turn + 1) * chunk)
                sums[part, :hidden] += pre[:, lanes]
                sums[part, hidden:] += square[:, lanes]

    each(b_group // block, one_block)

    @pl.when(step == pl.num_programs(0) - 1)
    def _():
        for part in range(blocks):
            sent_ref[part, :tall] = sums[part].astype(jnp.bfloat16)
            sent_ref[part, tall:] = same[part].astype(jnp.bfloat16)


def each(times, step):
    if times == 1:
        step(0)
    else:

        @pl.loop(0, times)
        def _(number):
            step(number)


def pool(place, table, touched, ids, w_hidden, chunk):
    f_dev, rows_f, width = table.shape
    hots, b_group = ids.shape[1:]
    count = touched.shape[1]
    hidden = w_hidden.shape[2]
    blocks = b_group // chunk
    repeat_rows = -(-f_dev // HALF) * HALF
    tall = hidden + HALF
    sent = (blocks, tall + repeat_rows, chunk)
    steps = f_dev // PAIR

    def now(*shape):
        return pl.BlockSpec((PAIR,) + shape, lambda i, p: (i, 0, 0))

    return pl.pallas_call(
        pool_kernel,
        grid_spec=pltpu.PrefetchScalarGridSpec(
            num_scalar_prefetch=1,
            grid=(steps,),
            in_specs=[
                now(rows_f, width),
                pl.BlockSpec(touched.shape, lambda i, p: (0, 0)),
                now(hots, b_group),
                pl.BlockSpec((PAIR, width, hidden), lambda i, p: (p[OWN] * steps + i, 0, 0)),
            ],
            out_specs=[
                pl.BlockSpec(sent, lambda i, p: (0, 0, 0)),
                now(width, count),
                now(rows_f // 256, LANES),
                now(count, b_group),
            ],
            scratch_shapes=[
                pltpu.VMEM((blocks, tall, chunk), jnp.float32),
                pltpu.VMEM((blocks, repeat_rows, chunk), jnp.float32),
                pltpu.VMEM((PAIR, 2, hots, min(b_group, BLOCK)), jnp.int32),
            ],
        ),
        out_shape=[
            jax.ShapeDtypeStruct(sent, jnp.bfloat16),
            jax.ShapeDtypeStruct((f_dev, width, count), jnp.bfloat16),
            jax.ShapeDtypeStruct((f_dev, rows_f // 256, LANES), jnp.int32),
            jax.ShapeDtypeStruct((f_dev, count, b_group), jnp.bfloat16),
        ],
        compiler_params=pltpu.CompilerParams(vmem_limit_bytes=56 * MIB),
        cost_estimate=pl.CostEstimate(
            flops=2 * f_dev * count * b_group * width * 8,
            bytes_accessed=table.size * 4,
            transcendentals=0,
        ),
        name="pool",
    )(place, table, touched, ids, w_hidden)


def code_kernel(words_ref, ids_ref, *rest):
    codes_ref, slots = rest[-2:]
    low, b_group = codes_ref.shape[1:]
    block = min(b_group, BLOCK)
    place = places(low)
    lines = [
        [words_ref[side, number : number + 1] for number in range(words_ref.shape[1])]
        for side in range(PAIR)
    ]

    def one_block(number):
        for inner in range(0, block, LANES):
            where = pl.ds(pl.multiple_of(number * block + inner, LANES), LANES)
            packed = ids_ref[0, 0, :, where]
            for side, ids in enumerate((packed & 0xFFFF, packed >> HALF)):
                look_up(lines[side], ids, slots.at[side], slice(inner, inner + LANES))
        for inner in range(0, block, LANES):
            where = pl.ds(pl.multiple_of(number * block + inner, LANES), LANES)
            for side in range(PAIR):
                codes_ref[side, :, where] = tally(
                    place, slots.at[side], slice(inner, inner + LANES)
                )

    each(b_group // block, one_block)


def code_counts(words, packed, low, start, stop, before=None):
    others, pairs, hots, b_group = packed.shape
    size = (stop - start) * PAIR * low * others * b_group
    kept = () if before is None else (before,)
    return pl.pallas_call(
        code_kernel,
        grid=(stop - start, others),
        in_specs=[
            pl.BlockSpec((PAIR,) + words.shape[1:], lambda f, g: (f + start, 0, 0)),
            pl.BlockSpec((1, 1, hots, b_group), lambda f, g: (g, f + start, 0, 0)),
        ]
        + [pl.BlockSpec(memory_space=pl.ANY)] * len(kept),
        out_specs=pl.BlockSpec((PAIR, low, b_group), lambda f, g: (f + start, 0, g)),
        scratch_shapes=[pltpu.VMEM((PAIR, 2, hots, min(b_group, BLOCK)), jnp.int32)],
        out_shape=jax.ShapeDtypeStruct((pairs * PAIR, low, others * b_group), jnp.int16),
        input_output_aliases={2: 0} if kept else {},
        compiler_params=pltpu.CompilerParams(vmem_limit_bytes=48 * MIB),
        cost_estimate=pl.CostEstimate(
            flops=size * 400, bytes_accessed=size * 2, transcendentals=0
        ),
        name="code",
    )(words, packed, *kept)


def clip_kernel(w_out_ref, labels_ref, w_ref, sent_ref, clip_ref):
    features, width, hidden = w_ref.shape
    devices = sent_ref.shape[0]
    share = features // devices
    tall = hidden + HALF
    w_out = w_out_ref[...]
    red = sent_ref[0, :tall].astype(jnp.float32)
    for device in range(1, devices):
        red = red + sent_ref[device, :tall].astype(jnp.float32)
    pre = red[:hidden]
    flat_sq = jnp.sum(red[hidden:], axis=0, keepdims=True)
    gate = jax.nn.sigmoid(pre)
    logit = jnp.sum(pre * gate * w_out, axis=0, keepdims=True)
    miss = jax.nn.sigmoid(logit) - labels_ref[...]
    delta = gate * (1.0 + pre * (1.0 - gate)) * w_out * miss
    delta_low = delta.astype(jnp.bfloat16)
    lanes = pre.shape[1]

    total = jnp.zeros((8, lanes), jnp.float32)
    for device in range(devices):
        w_part = w_ref[device * share : (device + 1) * share].reshape(share * width, hidden)
        grad = dot(w_part, delta_low)
        square = jnp.sum((grad * grad).reshape(share, width // 8, 8, lanes), axis=1)
        repeats = sent_ref[device, tall:].astype(jnp.float32)
        for inner in range(share):
            total = total + square[inner] * repeats[inner : inner + 1]
    norm_sq = jnp.sum(total, axis=0, keepdims=True)
    norm_sq = norm_sq + flat_sq * jnp.sum(delta * delta, axis=0, keepdims=True)
    factor = CLIP / jnp.maximum(jnp.sqrt(norm_sq), CLIP)
    clip_ref[...] = (factor * delta).T.astype(jnp.bfloat16)


def clip_rows(sent, w_out, labels, w_hidden):
    features, width, hidden = w_hidden.shape
    b_dev = labels.shape[0]
    vmem = pl.BlockSpec(memory_space=pltpu.VMEM)
    return pl.pallas_call(
        clip_kernel,
        in_specs=[vmem] * 4,
        out_specs=vmem,
        out_shape=jax.ShapeDtypeStruct((b_dev, hidden), jnp.bfloat16),
        compiler_params=pltpu.CompilerParams(vmem_limit_bytes=32 * MIB),
        cost_estimate=pl.CostEstimate(
            flops=2 * features * width * hidden * b_dev,
            bytes_accessed=w_hidden.size * 2,
            transcendentals=b_dev * hidden,
        ),
        name="clip",
    )(w_out.reshape(hidden, 1), labels.reshape(1, b_dev), w_hidden, sent)


def split(array, parts):
    found = []
    for part in range(parts):
        found.append(array.astype(jnp.bfloat16))
        array = array - found[-1].astype(jnp.float32)
    return found


def update_kernel(
    place_ref,
    listed_ref,
    own_counts_ref,
    codes_ref,
    near_ref,
    far_ref,
    table_ref,
    touched_ref,
    words_ref,
    accum_ref,
    noise_ref,
    w_ref,
    rows_ref,
    dense_noise_ref,
    table_out,
    accum_out,
    dense_out,
    update,
    clips,
):
    step = pl.program_id(0)
    last = pl.num_programs(0) - 1
    count, b_group = own_counts_ref.shape[1:]
    low = count // DIGITS
    groups = near_ref.shape[1]
    rows_f, width = table_ref.shape[1:]
    hidden = clips.shape[0]
    block = min(b_group, BLOCK)
    features = range(PAIR)

    @pl.when(step == 0)
    def _():
        chips, rows = near_ref.shape[0], near_ref.shape[2]
        for core, source in enumerate((near_ref, far_ref)):
            for chip in range(chips):
                for group in range(groups):
                    start = group * b_group + (place_ref[OWN] ^ (2 * chip + core)) * rows
                    clips[:, pl.ds(pl.multiple_of(start, rows), rows)] = source[chip, group].T

    def put(side, start, stop):
        feature = jnp.maximum(step - 1, 0) * PAIR + side
        for first in range(start, stop, BATCH):
            batch = range(first, first + BATCH)
            spots = [pl.ds(listed_ref[feature, slot], 1) for slot in batch]
            rows = [table_ref[side, spot, :] for spot in spots]
            steps = [update[side, slot : slot + 1, :] for slot in batch]
            for spot, row, one_step in zip(spots, rows, steps):
                table_out[side, spot, :] = row - one_step

    def add(group, number, sums):
        where = pl.ds(pl.multiple_of(number * block, block), block)
        at = pl.ds(pl.multiple_of(group * b_group + number * block, block), block)
        found = []
        for side in features:
            if group == 0:
                counts = own_counts_ref[side, :, where]
            else:
                start = pl.multiple_of((group - 1) * b_group + number * block, block)
                counts = spread(codes_ref[side, :, pl.ds(start, block)])
            found.append(sums[side] + dot(clips[:, at], counts, NT))
        return tuple(found)

    def finish(side, sums):
        sums = sums.T
        parts = [
            sums[digit * low : (digit + 1) * low] * (1 / scale(digit)) for digit in range(DIGITS)
        ]
        both = jnp.concatenate(split(jnp.concatenate(parts, axis=0), 2), axis=1)
        dense = dot(rows_ref[side], both)
        dense_out[side] = dense[:, :hidden] + dense[:, hidden:] + dense_noise_ref[side]
        w_twice = jnp.concatenate([w_ref[side], w_ref[side]], axis=1)
        listed = dot(both, w_twice, NT) + noise_ref[side]

        square = jnp.concatenate(split(listed * listed, 2), axis=1)
        mean = dot(square, jnp.full((2 * width, LANES), 1 / width, jnp.bfloat16))
        shape = (LANES, LANES)
        eye = iota(shape, 0) == iota(shape, 1)
        sections = [slice(start, start + LANES) for start in range(0, count, LANES)]
        touched = touched_ref[pl.ds(step * PAIR + side, 1)]
        touched = jnp.concatenate([touched[:, lanes] for lanes in sections * 2], axis=0)
        lines = [accum_ref[side, number : number + 1] for number in range(rows_f // LANES)]
        old = pick_lanes(lines, touched >> 7, touched & (LANES - 1))
        ones = jnp.where(eye, 1.0, 0.0).astype(jnp.bfloat16)
        parts = split(old, 2)
        diagonal = jnp.concatenate(
            [
                jnp.concatenate(
                    [ones * jnp.broadcast_to(part[q : q + 1], shape) for part in parts], axis=1
                )
                for q in range(len(sections))
            ],
            axis=0,
        )
        total = mean + dot(diagonal, jnp.full((2 * LANES, LANES), 1, jnp.bfloat16))
        update[side] = listed * (LEARN * lax.rsqrt(total))

        extra = [
            jnp.sum(jnp.where(eye, mean[rows], 0.0), axis=0, keepdims=True) for rows in sections
        ]
        words = words_ref[side]
        for half, word in enumerate((words & 0xFFFF, lax.shift_right_logical(words, HALF))):
            gain = pick_lanes(extra, (word >> 10) & (DIGITS - 1), word & (LANES - 1))
            rows = slice(half * words.shape[0], (half + 1) * words.shape[0])
            accum_out[side, rows] = accum_ref[side, rows] + jnp.where(
                (word >> 8) >= LISTED, gain, 0.0
            )

    @pl.when(step < last)
    def _():
        table_out[...] = table_ref[...]
        sums = tuple(jnp.zeros((hidden, count), jnp.float32) for side in features)
        share = count // groups
        for group in range(groups):
            for side in features:
                put(side, group * share, (group + 1) * share)
            if b_group == block:
                sums = add(group, 0, sums)
            else:
                sums = lax.fori_loop(0, b_group // block, functools.partial(add, group), sums)
        for side in features:
            finish(side, sums[side])

    @pl.when(step == last)
    def _():
        table_out[...] = table_ref[...]
        for side in features:
            put(side, 0, count)


def update_rows(
    place,
    own_counts,
    codes,
    near,
    far,
    table,
    touched,
    words,
    accum,
    noise,
    w_hidden,
    rows_t,
    dense_noise,
):
    f_dev, rows_f, width = table.shape
    count, b_group = own_counts.shape[1:]
    low = count // DIGITS
    others = codes.shape[2]
    hidden = near.shape[-1]
    part = dense_noise.shape[1]
    tall = rows_f // LANES
    steps = f_dev // PAIR

    def current(i):
        return jnp.minimum(i, steps - 1)

    def now(*shape):
        return pl.BlockSpec((PAIR,) + shape, lambda i, p, s: (current(i), 0, 0))

    def before(*shape):
        return pl.BlockSpec((PAIR,) + shape, lambda i, p, s: (jnp.maximum(i - 1, 0), 0, 0))

    def whole(array):
        return pl.BlockSpec(array.shape, lambda i, p, s: (0,) * array.ndim)

    new_table, new_accum, dense = pl.pallas_call(
        update_kernel,
        grid_spec=pltpu.PrefetchScalarGridSpec(
            num_scalar_prefetch=2,
            grid=(steps + 1,),
            in_specs=[
                now(count, b_group),
                now(low, others),
                whole(near),
                whole(far),
                before(rows_f, width),
                whole(touched),
                now(*words.shape[1:]),
                now(tall, LANES),
                now(count, width),
                pl.BlockSpec(
                    (PAIR, width, hidden), lambda i, p, s: (p[OWN] * steps + current(i), 0, 0)
                ),
                pl.BlockSpec((PAIR, part, count), lambda i, p, s: (current(i), p[GROUP], 0)),
                now(part, hidden),
            ],
            out_specs=[before(rows_f, width), now(tall, LANES), now(part, hidden)],
            scratch_shapes=[
                pltpu.VMEM((PAIR, count, width), jnp.float32),
                pltpu.VMEM((hidden, b_group + others), jnp.bfloat16),
            ],
        ),
        out_shape=[
            jax.ShapeDtypeStruct((f_dev, rows_f, width), jnp.float32),
            jax.ShapeDtypeStruct((f_dev, tall, LANES), jnp.float32),
            jax.ShapeDtypeStruct((f_dev, part, hidden), jnp.float32),
        ],
        compiler_params=pltpu.CompilerParams(vmem_limit_bytes=56 * MIB),
        cost_estimate=pl.CostEstimate(
            flops=2 * f_dev * count * (b_group + others) * hidden,
            bytes_accessed=table.size * 8 + codes.size * 2,
            transcendentals=0,
        ),
        name="update",
    )(
        place,
        touched,
        own_counts,
        codes,
        near,
        far,
        table,
        touched,
        words,
        accum.reshape(f_dev, tall, LANES),
        noise,
        w_hidden,
        rows_t,
        dense_noise,
    )
    return new_table, new_accum.reshape(f_dev, rows_f), dense


def swap(array, axis, apart):
    size = lax.axis_size(axis)
    return lax.ppermute(array, axis, [(i, i ^ apart) for i in range(size)])


def body(table, accum, w_hidden, w_out, ids, labels, touched, row_noise, dense_noise):
    f_dev = table.shape[0]
    b_dev = labels.shape[0]
    low = touched.shape[1] // DIGITS
    groups, tables = lax.axis_size("group"), lax.axis_size("table")
    own = lax.axis_index("table").astype(jnp.int32)
    group = lax.axis_index("group").astype(jnp.int32)
    place = jnp.stack([own, group])
    pairs = f_dev // PAIR

    packed = ids[0::2] | (ids[1::2] << HALF)
    ids, packed, place = lax.optimization_barrier((ids, packed, place))
    packed = [swap(packed, "group", d) for d in range(1, groups)]

    sent, rows_t, words, own_counts = pool(place, table, touched, ids, w_hidden, b_dev)
    packed = jnp.stack(packed)
    stops = [pairs * share // 4 for share in range(5)]

    def more_codes(number, codes, waits, ready=None):
        if stops[number + 1] > stops[number]:
            begin = words
            if ready is not None:
                begin, ready = lax.optimization_barrier((words, ready))
            codes = code_counts(
                begin, packed, low, stops[number], stops[number + 1], codes
            )
        return lax.optimization_barrier((codes, waits))

    sent, packed = lax.optimization_barrier((sent, packed))
    arrived = lax.all_to_all(sent, "table", split_axis=0, concat_axis=0, tiled=True)
    codes, arrived = more_codes(0, None, arrived)
    clips = clip_rows(arrived, w_out, labels, w_hidden)
    column = [clips] + [swap(clips, "group", d) for d in range(1, groups)]
    codes, column = more_codes(1, codes, column, clips)
    column = jnp.stack(column)
    near = [column] + [swap(column, "table", d) for d in range(2, tables, 2)]
    codes, near = more_codes(2, codes, near, column)
    near = jnp.stack(near)
    far = swap(near, "table", 1)
    codes, far = more_codes(3, codes, far, near)

    return update_rows(
        place,
        own_counts,
        codes,
        near,
        far,
        table,
        touched,
        words,
        accum,
        row_noise,
        w_hidden,
        rows_t,
        dense_noise,
    )


def solution(mesh):
    in_specs = (
        P("table", None, None),
        P("table", None),
        P(),
        P(),
        P("table", None, "group"),
        P(("group", "table")),
        P("table", None),
        P("table", None, None),
        P("table", "group", None),
    )
    out_specs = (P("table", None, None), P("table", None), P("table", "group", None))
    return jax.shard_map(body, mesh=mesh, in_specs=in_specs, out_specs=out_specs, check_vma=False)
```

```python
import functools

import jax
import jax.numpy as jnp
from jax import lax
from jax.experimental import pallas as pl
from jax.experimental.pallas import tpu as pltpu
from jax.sharding import PartitionSpec as P

CLIP = 1.0
LEARN = 0.05
LANES = 128
DIGITS = 4
HALF = 16
BLOCK = 1024
BATCH = 32
ROWS = 512
OWN, GROUP = range(2)
PAIR = 2
LISTED = 16
MIB = 1 << 20

NT = (((1,), (1,)), ((), ()))
TN = (((0,), (0,)), ((), ()))


def dot(left, right, dims=(((1,), (0,)), ((), ())), precision=None):
    return lax.dot_general(
        left, right, dims, preferred_element_type=jnp.float32, precision=precision
    )


def iota(shape, axis):
    return lax.broadcasted_iota(jnp.int32, shape, axis)


def slot_words(touched_row, rows_f):
    count = touched_row.shape[1]
    low = count // DIGITS
    tall = rows_f // LANES
    slot = iota((1, count), 1)
    rows = jnp.where((touched_row >> 7) == iota((tall, count), 0), 1.0, 0.0)
    lanes = jnp.where((touched_row & (LANES - 1)) == iota((LANES, count), 0), 1.0, 0.0)
    values = (lax.rem(slot, low), LISTED + 4 * lax.div(slot, low))
    held = jnp.concatenate([rows * value.astype(jnp.float32) for value in values], axis=0)
    parts = dot(held.astype(jnp.bfloat16), lanes.astype(jnp.bfloat16), NT).astype(jnp.int32)
    word = parts[:tall] | (parts[tall:] << 8)
    return word[: tall // 2] | (word[tall // 2 :] << HALF)


def pick_lanes(lines, row, lane):
    got = [
        jnp.take_along_axis(jnp.broadcast_to(line, row.shape), lane, axis=1) for line in lines
    ]
    bit = 1
    while len(got) > 1:
        odd = (row & bit) != 0
        got = [jnp.where(odd, got[i + 1], got[i]) for i in range(0, len(got), 2)]
        bit *= 2
    return got[0]


def look_up(lines, ids, slots, where):
    word = pick_lanes(lines, ids >> 7, ids & (LANES - 1))
    upper = ids >= len(lines) * LANES
    word = jnp.where(upper, lax.shift_right_logical(word, HALF), word) & 0xFFFF
    slots[0, :, where] = word & 0xFF
    slots[1, :, where] = jnp.left_shift(jnp.ones_like(word), (word >> 8) & (LISTED - 1))


def places(low):
    shape = (low // HALF, HALF, LANES)
    return (iota(shape, 0) * HALF + iota(shape, 1)).astype(jnp.int16)


def tally(place, slots, where):
    total = None
    nothing = jnp.zeros(place.shape, jnp.int16)
    wide = (HALF, LANES)
    for hot in range(slots.shape[1]):
        one_group = jnp.broadcast_to(slots[0, hot : hot + 1, where], wide).astype(jnp.int16)
        one_code = jnp.broadcast_to(slots[1, hot : hot + 1, where], wide).astype(jnp.int16)
        hit = place == jnp.broadcast_to(one_group[None], place.shape)
        part = jnp.where(hit, jnp.broadcast_to(one_code[None], place.shape), nothing)
        total = part if total is None else total + part
    return total.reshape(-1, LANES)


def spread(codes):
    parts = []
    for digit in range(DIGITS):
        if digit < DIGITS - 1:
            part = codes & jnp.full(codes.shape, 15 << (4 * digit), jnp.int16)
        else:
            part = lax.shift_right_logical(codes, jnp.full(codes.shape, 4 * digit, jnp.int16))
        parts.append(part.astype(jnp.bfloat16))
    return jnp.concatenate(parts, axis=0)


def scale(digit):
    return float(16**digit if digit < DIGITS - 1 else 1)


def pool_kernel(
    place_ref,
    table_ref,
    touched_ref,
    ids_ref,
    w_ref,
    sent_ref,
    rows_ref,
    words_ref,
    counts_ref,
    sums,
    same,
    slots,
):
    step = pl.program_id(0)
    rows_f, width = table_ref.shape[1:]
    hots, b_group = ids_ref.shape[1:]
    count = touched_ref.shape[1]
    low = count // DIGITS
    hidden = w_ref.shape[2]
    blocks, tall, chunk = sums.shape
    block = min(b_group, BLOCK)
    place = places(low)

    @pl.when(step == 0)
    def _():
        sums[...] = jnp.zeros_like(sums)
        same[...] = jnp.zeros_like(same)

    features = range(PAIR)
    lines = []
    for side in features:
        words = slot_words(touched_ref[pl.ds(step * PAIR + side, 1)], rows_f)
        words_ref[side] = words
        lines.append([words[number : number + 1] for number in range(words.shape[0])])
    lane = iota((HALF, LANES), 1)
    columns, picked = [], []
    for side in features:
        row = touched_ref[pl.ds(step * PAIR + side, 1)].astype(jnp.float32)
        column = jnp.broadcast_to(row, (LANES, count)).T.astype(jnp.int32).astype(jnp.int16)
        columns.append(column.reshape(count // HALF, HALF, LANES))
        picked.append(jnp.zeros((count, width), jnp.float32))
    one = jnp.ones(columns[0].shape, jnp.bfloat16)
    for start in range(0, rows_f, ROWS):
        for side in features:
            parts = []
            for first in range(start, start + ROWS, LANES):
                number = (lane + first).astype(jnp.int16)
                hit = columns[side] == jnp.broadcast_to(number[None], one.shape)
                parts.append(jnp.where(hit, one, jnp.zeros_like(one)).reshape(count, LANES))
            rows = table_ref[side, start : start + ROWS].astype(jnp.bfloat16)
            picked[side] = picked[side] + dot(jnp.concatenate(parts, axis=1), rows)
    rows_t, w_t = [], []
    for side in features:
        whole = picked[side].astype(jnp.bfloat16).T
        rows_ref[side] = whole
        parts = [
            whole[:, digit * low : (digit + 1) * low] * jnp.bfloat16(1 / scale(digit))
            for digit in range(DIGITS)
        ]
        rows_t.append(jnp.concatenate(parts, axis=1))
        w_t.append(w_ref[side].T)

    def one_block(number):
        for inner in range(0, block, chunk):
            for side in features:
                where = pl.ds(pl.multiple_of(number * block + inner, chunk), chunk)
                ids = ids_ref[side, :, where]
                look_up(lines[side], ids, slots.at[side], slice(inner, inner + chunk))
                pairs = jnp.zeros(ids.shape, jnp.float32)
                for turn in range(1, hots // 2 + 1):
                    weight = 2.0 if turn < hots // 2 else 1.0
                    pairs = pairs + jnp.where(ids == pltpu.roll(ids, turn, 0), weight, 0.0)
                pairs = jnp.sum(pairs, axis=0, keepdims=True) + hots
                part = number * (block // chunk) + inner // chunk
                same[part, pl.ds(step * PAIR + side, 1)] = pairs
        for inner in range(0, block, 2 * chunk):
            pre, square = 0.0, 0.0
            for side in features:
                parts = []
                for start in (inner, inner + chunk):
                    parts.append(
                        spread(tally(place, slots.at[side], slice(start, start + chunk)))
                    )
                counts = jnp.concatenate(parts, axis=1)
                where = pl.ds(pl.multiple_of(number * block + inner, 2 * chunk), 2 * chunk)
                counts_ref[side, :, where] = counts
                pooled = dot(rows_t[side], counts).astype(jnp.bfloat16)
                wide = pooled.astype(jnp.float32)
                square += jnp.sum((wide * wide).reshape(width // HALF, HALF, 2 * chunk), axis=0)
                pre += dot(w_t[side], pooled)
            for turn in range(2):
                part = number * (block // chunk) + inner // chunk + turn
                lanes = slice(turn * chunk, (turn + 1) * chunk)
                sums[part, :hidden] += pre[:, lanes]
                sums[part, hidden:] += square[:, lanes]

    each(b_group // block, one_block)

    @pl.when(step == pl.num_programs(0) - 1)
    def _():
        for part in range(blocks):
            sent_ref[part, :tall] = sums[part].astype(jnp.bfloat16)
            sent_ref[part, tall:] = same[part].astype(jnp.bfloat16)


def each(times, step):
    if times == 1:
        step(0)
    else:

        @pl.loop(0, times)
        def _(number):
            step(number)


def pool(place, table, touched, ids, w_hidden, chunk):
    f_dev, rows_f, width = table.shape
    hots, b_group = ids.shape[1:]
    count = touched.shape[1]
    hidden = w_hidden.shape[2]
    blocks = b_group // chunk
    repeat_rows = -(-f_dev // HALF) * HALF
    tall = hidden + HALF
    sent = (blocks, tall + repeat_rows, chunk)
    steps = f_dev // PAIR

    def now(*shape):
        return pl.BlockSpec((PAIR,) + shape, lambda i, p: (i, 0, 0))

    return pl.pallas_call(
        pool_kernel,
        grid_spec=pltpu.PrefetchScalarGridSpec(
            num_scalar_prefetch=1,
            grid=(steps,),
            in_specs=[
                now(rows_f, width),
                pl.BlockSpec(touched.shape, lambda i, p: (0, 0)),
                now(hots, b_group),
                pl.BlockSpec((PAIR, width, hidden), lambda i, p: (p[OWN] * steps + i, 0, 0)),
            ],
            out_specs=[
                pl.BlockSpec(sent, lambda i, p: (0, 0, 0)),
                now(width, count),
                now(rows_f // 256, LANES),
                now(count, b_group),
            ],
            scratch_shapes=[
                pltpu.VMEM((blocks, tall, chunk), jnp.float32),
                pltpu.VMEM((blocks, repeat_rows, chunk), jnp.float32),
                pltpu.VMEM((PAIR, 2, hots, min(b_group, BLOCK)), jnp.int32),
            ],
        ),
        out_shape=[
            jax.ShapeDtypeStruct(sent, jnp.bfloat16),
            jax.ShapeDtypeStruct((f_dev, width, count), jnp.bfloat16),
            jax.ShapeDtypeStruct((f_dev, rows_f // 256, LANES), jnp.int32),
            jax.ShapeDtypeStruct((f_dev, count, b_group), jnp.bfloat16),
        ],
        compiler_params=pltpu.CompilerParams(vmem_limit_bytes=56 * MIB),
        cost_estimate=pl.CostEstimate(
            flops=2 * f_dev * count * b_group * width * 8,
            bytes_accessed=table.size * 4,
            transcendentals=0,
        ),
        name="pool",
    )(place, table, touched, ids, w_hidden)


def code_kernel(words_ref, ids_ref, *rest):
    codes_ref, slots = rest[-2:]
    low, b_group = codes_ref.shape[1:]
    block = min(b_group, BLOCK)
    place = places(low)
    lines = [
        [words_ref[side, number : number + 1] for number in range(words_ref.shape[1])]
        for side in range(PAIR)
    ]

    def one_block(number):
        for inner in range(0, block, LANES):
            where = pl.ds(pl.multiple_of(number * block + inner, LANES), LANES)
            packed = ids_ref[0, 0, :, where]
            for side, ids in enumerate((packed & 0xFFFF, packed >> HALF)):
                look_up(lines[side], ids, slots.at[side], slice(inner, inner + LANES))
        for inner in range(0, block, LANES):
            where = pl.ds(pl.multiple_of(number * block + inner, LANES), LANES)
            for side in range(PAIR):
                codes_ref[side, :, where] = tally(
                    place, slots.at[side], slice(inner, inner + LANES)
                )

    each(b_group // block, one_block)


def code_counts(words, packed, low, start, stop, before=None):
    others, pairs, hots, b_group = packed.shape
    size = (stop - start) * PAIR * low * others * b_group
    kept = () if before is None else (before,)
    return pl.pallas_call(
        code_kernel,
        grid=(stop - start, others),
        in_specs=[
            pl.BlockSpec((PAIR,) + words.shape[1:], lambda f, g: (f + start, 0, 0)),
            pl.BlockSpec((1, 1, hots, b_group), lambda f, g: (g, f + start, 0, 0)),
        ]
        + [pl.BlockSpec(memory_space=pl.ANY)] * len(kept),
        out_specs=pl.BlockSpec((PAIR, low, b_group), lambda f, g: (f + start, 0, g)),
        scratch_shapes=[pltpu.VMEM((PAIR, 2, hots, min(b_group, BLOCK)), jnp.int32)],
        out_shape=jax.ShapeDtypeStruct((pairs * PAIR, low, others * b_group), jnp.int16),
        input_output_aliases={2: 0} if kept else {},
        compiler_params=pltpu.CompilerParams(vmem_limit_bytes=48 * MIB),
        cost_estimate=pl.CostEstimate(
            flops=size * 400, bytes_accessed=size * 2, transcendentals=0
        ),
        name="code",
    )(words, packed, *kept)


def clip_kernel(w_out_ref, labels_ref, w_ref, sent_ref, clip_ref):
    features, width, hidden = w_ref.shape
    devices = sent_ref.shape[0]
    share = features // devices
    tall = hidden + HALF
    w_out = w_out_ref[...]
    red = sent_ref[0, :tall].astype(jnp.float32)
    for device in range(1, devices):
        red = red + sent_ref[device, :tall].astype(jnp.float32)
    pre = red[:hidden]
    flat_sq = jnp.sum(red[hidden:], axis=0, keepdims=True)
    gate = jax.nn.sigmoid(pre)
    logit = jnp.sum(pre * gate * w_out, axis=0, keepdims=True)
    miss = jax.nn.sigmoid(logit) - labels_ref[...]
    delta = gate * (1.0 + pre * (1.0 - gate)) * w_out * miss
    delta_low = delta.astype(jnp.bfloat16)
    lanes = pre.shape[1]

    total = jnp.zeros((8, lanes), jnp.float32)
    for device in range(devices):
        w_part = w_ref[device * share : (device + 1) * share].reshape(share * width, hidden)
        grad = dot(w_part, delta_low)
        square = jnp.sum((grad * grad).reshape(share, width // 8, 8, lanes), axis=1)
        repeats = sent_ref[device, tall:].astype(jnp.float32)
        for inner in range(share):
            total = total + square[inner] * repeats[inner : inner + 1]
    norm_sq = jnp.sum(total, axis=0, keepdims=True)
    norm_sq = norm_sq + flat_sq * jnp.sum(delta * delta, axis=0, keepdims=True)
    factor = CLIP / jnp.maximum(jnp.sqrt(norm_sq), CLIP)
    clip_ref[...] = (factor * delta).T.astype(jnp.bfloat16)


def clip_rows(sent, w_out, labels, w_hidden):
    features, width, hidden = w_hidden.shape
    b_dev = labels.shape[0]
    vmem = pl.BlockSpec(memory_space=pltpu.VMEM)
    return pl.pallas_call(
        clip_kernel,
        in_specs=[vmem] * 4,
        out_specs=vmem,
        out_shape=jax.ShapeDtypeStruct((b_dev, hidden), jnp.bfloat16),
        compiler_params=pltpu.CompilerParams(vmem_limit_bytes=32 * MIB),
        cost_estimate=pl.CostEstimate(
            flops=2 * features * width * hidden * b_dev,
            bytes_accessed=w_hidden.size * 2,
            transcendentals=b_dev * hidden,
        ),
        name="clip",
    )(w_out.reshape(hidden, 1), labels.reshape(1, b_dev), w_hidden, sent)


def split(array, parts):
    found = []
    for part in range(parts):
        found.append(array.astype(jnp.bfloat16))
        array = array - found[-1].astype(jnp.float32)
    return found


def update_kernel(
    place_ref,
    listed_ref,
    own_counts_ref,
    codes_ref,
    near_ref,
    far_ref,
    table_ref,
    touched_ref,
    words_ref,
    accum_ref,
    noise_ref,
    w_ref,
    rows_ref,
    dense_noise_ref,
    table_out,
    accum_out,
    dense_out,
    update,
    clips,
):
    step = pl.program_id(0)
    last = pl.num_programs(0) - 1
    count, b_group = own_counts_ref.shape[1:]
    low = count // DIGITS
    groups = near_ref.shape[1]
    rows_f, width = table_ref.shape[1:]
    hidden = clips.shape[1]
    block = min(b_group, BLOCK)
    features = range(PAIR)

    @pl.when(step == 0)
    def _():
        chips, rows = near_ref.shape[0], near_ref.shape[2]
        for core, source in enumerate((near_ref, far_ref)):
            for chip in range(chips):
                for group in range(groups):
                    start = group * b_group + (place_ref[OWN] ^ (2 * chip + core)) * rows
                    clips[pl.ds(pl.multiple_of(start, rows), rows)] = source[chip, group]

    def put(side, start, stop):
        feature = jnp.maximum(step - 1, 0) * PAIR + side
        for first in range(start, stop, BATCH):
            batch = range(first, first + BATCH)
            spots = [pl.ds(listed_ref[feature, slot], 1) for slot in batch]
            rows = [table_ref[side, spot, :] for spot in spots]
            steps = [update[side, slot : slot + 1, :] for slot in batch]
            for spot, row, one_step in zip(spots, rows, steps):
                table_out[side, spot, :] = row - one_step

    def add(group, number, sums):
        where = pl.ds(pl.multiple_of(number * block, block), block)
        at = pl.ds(pl.multiple_of(group * b_group + number * block, block), block)
        found = []
        for side in features:
            if group == 0:
                counts = own_counts_ref[side, :, where]
            else:
                start = pl.multiple_of((group - 1) * b_group + number * block, block)
                counts = spread(codes_ref[side, :, pl.ds(start, block)])
            found.append(sums[side] + dot(counts, clips[at]))
        return tuple(found)

    def finish(side, sums):
        parts = [
            sums[digit * low : (digit + 1) * low] * (1 / scale(digit)) for digit in range(DIGITS)
        ]
        both = jnp.concatenate(split(jnp.concatenate(parts, axis=0), 2), axis=1)
        dense = dot(rows_ref[side], both)
        dense_out[side] = dense[:, :hidden] + dense[:, hidden:] + dense_noise_ref[side]
        w_twice = jnp.concatenate([w_ref[side], w_ref[side]], axis=1)
        listed = dot(both, w_twice, NT) + noise_ref[side]

        square = jnp.concatenate(split(listed * listed, 2), axis=1)
        mean = dot(square, jnp.full((2 * width, LANES), 1 / width, jnp.bfloat16))
        shape = (LANES, LANES)
        eye = iota(shape, 0) == iota(shape, 1)
        sections = [slice(start, start + LANES) for start in range(0, count, LANES)]
        touched = touched_ref[pl.ds(step * PAIR + side, 1)]
        touched = jnp.concatenate([touched[:, lanes] for lanes in sections * 2], axis=0)
        feature = step * PAIR + side
        mine = iota((accum_ref.shape[0], LANES), 0) == feature
        stretches = [slice(start, start + LANES) for start in range(0, rows_f, LANES)]
        lines = [
            jnp.sum(jnp.where(mine, accum_ref[:, lanes], 0.0), axis=0, keepdims=True)
            for lanes in stretches
        ]
        old = pick_lanes(lines, touched >> 7, touched & (LANES - 1))
        ones = jnp.where(eye, 1.0, 0.0).astype(jnp.bfloat16)
        parts = split(old, 2)
        diagonal = jnp.concatenate(
            [
                jnp.concatenate(
                    [ones * jnp.broadcast_to(part[q : q + 1], shape) for part in parts], axis=1
                )
                for q in range(len(sections))
            ],
            axis=0,
        )
        total = mean + dot(diagonal, jnp.full((2 * LANES, LANES), 1, jnp.bfloat16))
        update[side] = listed * (LEARN * lax.rsqrt(total))

        extra = [
            jnp.sum(jnp.where(eye, mean[rows], 0.0), axis=0, keepdims=True) for rows in sections
        ]
        words = words_ref[side]
        for half, word in enumerate((words & 0xFFFF, lax.shift_right_logical(words, HALF))):
            gain = pick_lanes(extra, (word >> 10) & (DIGITS - 1), word & (LANES - 1))
            gain = jnp.where((word >> 8) >= LISTED, gain, 0.0)
            for number in range(words.shape[0]):
                place = half * words.shape[0] + number
                line = jnp.broadcast_to(lines[place] + gain[number : number + 1], mine.shape)
                lanes = stretches[place]
                accum_out[:, lanes] = jnp.where(mine, line, accum_out[:, lanes])

    @pl.when(step < last)
    def _():
        table_out[...] = table_ref[...]
        sums = tuple(jnp.zeros((count, hidden), jnp.float32) for side in features)
        share = count // groups
        for group in range(groups):
            for side in features:
                put(side, group * share, (group + 1) * share)
            if b_group == block:
                sums = add(group, 0, sums)
            else:
                sums = lax.fori_loop(0, b_group // block, functools.partial(add, group), sums)
        for side in features:
            finish(side, sums[side])

    @pl.when(step == last)
    def _():
        table_out[...] = table_ref[...]
        for side in features:
            put(side, 0, count)


def update_rows(
    place,
    own_counts,
    codes,
    near,
    far,
    table,
    touched,
    words,
    accum,
    noise,
    w_hidden,
    rows_t,
    dense_noise,
):
    f_dev, rows_f, width = table.shape
    count, b_group = own_counts.shape[1:]
    low = count // DIGITS
    others = codes.shape[2]
    hidden = near.shape[-1]
    part = dense_noise.shape[1]
    steps = f_dev // PAIR

    def current(i):
        return jnp.minimum(i, steps - 1)

    def now(*shape):
        return pl.BlockSpec((PAIR,) + shape, lambda i, p, s: (current(i), 0, 0))

    def before(*shape):
        return pl.BlockSpec((PAIR,) + shape, lambda i, p, s: (jnp.maximum(i - 1, 0), 0, 0))

    def whole(array):
        return pl.BlockSpec(array.shape, lambda i, p, s: (0,) * array.ndim)

    return pl.pallas_call(
        update_kernel,
        grid_spec=pltpu.PrefetchScalarGridSpec(
            num_scalar_prefetch=2,
            grid=(steps + 1,),
            in_specs=[
                now(count, b_group),
                now(low, others),
                whole(near),
                whole(far),
                before(rows_f, width),
                whole(touched),
                now(*words.shape[1:]),
                whole(accum),
                now(count, width),
                pl.BlockSpec(
                    (PAIR, width, hidden), lambda i, p, s: (p[OWN] * steps + current(i), 0, 0)
                ),
                pl.BlockSpec((PAIR, part, count), lambda i, p, s: (current(i), p[GROUP], 0)),
                now(part, hidden),
            ],
            out_specs=[before(rows_f, width), whole(accum), now(part, hidden)],
            scratch_shapes=[
                pltpu.VMEM((PAIR, count, width), jnp.float32),
                pltpu.VMEM((b_group + others, hidden), jnp.bfloat16),
            ],
        ),
        out_shape=[
            jax.ShapeDtypeStruct((f_dev, rows_f, width), jnp.float32),
            jax.ShapeDtypeStruct(accum.shape, jnp.float32),
            jax.ShapeDtypeStruct((f_dev, part, hidden), jnp.float32),
        ],
        compiler_params=pltpu.CompilerParams(vmem_limit_bytes=56 * MIB),
        cost_estimate=pl.CostEstimate(
            flops=2 * f_dev * count * (b_group + others) * hidden,
            bytes_accessed=table.size * 8 + codes.size * 2,
            transcendentals=0,
        ),
        name="update",
    )(
        place,
        touched,
        own_counts,
        codes,
        near,
        far,
        table,
        touched,
        words,
        accum,
        noise,
        w_hidden,
        rows_t,
        dense_noise,
    )


def swap(array, axis, apart):
    size = lax.axis_size(axis)
    return lax.ppermute(array, axis, [(i, i ^ apart) for i in range(size)])


def body(table, accum, w_hidden, w_out, ids, labels, touched, row_noise, dense_noise):
    f_dev = table.shape[0]
    b_dev = labels.shape[0]
    low = touched.shape[1] // DIGITS
    groups, tables = lax.axis_size("group"), lax.axis_size("table")
    own = lax.axis_index("table").astype(jnp.int32)
    group = lax.axis_index("group").astype(jnp.int32)
    place = jnp.stack([own, group])
    pairs = f_dev // PAIR

    packed = ids[0::2] | (ids[1::2] << HALF)
    ids, packed, place = lax.optimization_barrier((ids, packed, place))
    packed = [swap(packed, "group", d) for d in range(1, groups)]

    sent, rows_t, words, own_counts = pool(place, table, touched, ids, w_hidden, b_dev)
    packed = jnp.stack(packed)
    stops = [pairs * share // 4 for share in range(5)]

    def more_codes(number, codes, waits, ready=None):
        if stops[number + 1] > stops[number]:
            begin = words
            if ready is not None:
                begin, ready = lax.optimization_barrier((words, ready))
            codes = code_counts(
                begin, packed, low, stops[number], stops[number + 1], codes
            )
        return lax.optimization_barrier((codes, waits))

    sent, packed = lax.optimization_barrier((sent, packed))
    arrived = lax.all_to_all(sent, "table", split_axis=0, concat_axis=0, tiled=True)
    codes, arrived = more_codes(0, None, arrived)
    clips = clip_rows(arrived, w_out, labels, w_hidden)
    column = [clips] + [swap(clips, "group", d) for d in range(1, groups)]
    codes, column = more_codes(1, codes, column, clips)
    column = jnp.stack(column)
    near = [column] + [swap(column, "table", d) for d in range(2, tables, 2)]
    codes, near = more_codes(2, codes, near, column)
    near = jnp.stack(near)
    far = swap(near, "table", 1)
    codes, far = more_codes(3, codes, far, near)

    return update_rows(
        place,
        own_counts,
        codes,
        near,
        far,
        table,
        touched,
        words,
        accum,
        row_noise,
        w_hidden,
        rows_t,
        dense_noise,
    )


def solution(mesh):
    in_specs = (
        P("table", None, None),
        P("table", None),
        P(),
        P(),
        P("table", None, "group"),
        P(("group", "table")),
        P("table", None),
        P("table", None, None),
        P("table", "group", None),
    )
    out_specs = (P("table", None, None), P("table", None), P("table", "group", None))
    return jax.shard_map(body, mesh=mesh, in_specs=in_specs, out_specs=out_specs, check_vma=False)
```

```python
import functools

import jax
import jax.numpy as jnp
from jax import lax
from jax.experimental import pallas as pl
from jax.experimental.pallas import tpu as pltpu
from jax.sharding import PartitionSpec as P

CLIP = 1.0
LEARN = 0.05
LANES = 128
DIGITS = 8
HALF = 16
BLOCK = 1024
BATCH = 32
ROWS = 512
OWN, GROUP = range(2)
PAIR = 2
LISTED = 32
MIB = 1 << 20

NT = (((1,), (1,)), ((), ()))
TN = (((0,), (0,)), ((), ()))


def dot(left, right, dims=(((1,), (0,)), ((), ())), precision=None):
    return lax.dot_general(
        left, right, dims, preferred_element_type=jnp.float32, precision=precision
    )


def iota(shape, axis):
    return lax.broadcasted_iota(jnp.int32, shape, axis)


def slot_words(touched_row, rows_f):
    count = touched_row.shape[1]
    low = count // DIGITS
    tall = rows_f // LANES
    slot = iota((1, count), 1)
    rows = jnp.where((touched_row >> 7) == iota((tall, count), 0), 1.0, 0.0)
    lanes = jnp.where((touched_row & (LANES - 1)) == iota((LANES, count), 0), 1.0, 0.0)
    values = (lax.rem(slot, low), LISTED + 4 * lax.div(slot, low))
    held = jnp.concatenate([rows * value.astype(jnp.float32) for value in values], axis=0)
    parts = dot(held.astype(jnp.bfloat16), lanes.astype(jnp.bfloat16), NT).astype(jnp.int32)
    word = parts[:tall] | (parts[tall:] << 8)
    return word[: tall // 2] | (word[tall // 2 :] << HALF)


def pick_lanes(lines, row, lane):
    got = [
        jnp.take_along_axis(jnp.broadcast_to(line, row.shape), lane, axis=1) for line in lines
    ]
    bit = 1
    while len(got) > 1:
        odd = (row & bit) != 0
        got = [jnp.where(odd, got[i + 1], got[i]) for i in range(0, len(got), 2)]
        bit *= 2
    return got[0]


def look_up(lines, ids, slots, where):
    word = pick_lanes(lines, ids >> 7, ids & (LANES - 1))
    upper = ids >= len(lines) * LANES
    word = jnp.where(upper, lax.shift_right_logical(word, HALF), word) & 0xFFFF
    slots[0, :, where] = (word >> 3) & 7
    slots[1, :, where] = word & 7
    slots[2, :, where] = jnp.left_shift(jnp.ones_like(word), (word >> 8) & (LISTED - 1))


def tally(slots, codes, where):
    shape = (8, LANES)
    row = iota(shape, 0)
    for hot in range(slots.shape[1]):
        high, code = (
            jnp.broadcast_to(slots[part, hot : hot + 1, where], shape) for part in (0, 2)
        )
        codes[hot, :, where] = jnp.where(row == high, code, 0)
    totals = [None] * 8
    for hot in range(slots.shape[1]):
        mask = jnp.where(row == jnp.broadcast_to(slots[1, hot : hot + 1, where], shape), -1, 0)
        for high in range(8):
            part = jnp.broadcast_to(codes[hot, high : high + 1, where], shape) & mask
            totals[high] = part if hot == 0 else totals[high] + part
    return jnp.concatenate(totals, axis=0)


def spread(codes):
    parts = []
    for digit in range(DIGITS):
        if digit < DIGITS - 1:
            part = codes & (15 << (4 * digit))
        else:
            part = lax.shift_right_logical(codes, 4 * digit)
        parts.append(part.astype(jnp.float32).astype(jnp.bfloat16))
    return jnp.concatenate(parts, axis=0)


def scale(digit):
    return float(16**digit if digit < DIGITS - 1 else 1)


def pool_kernel(
    place_ref,
    table_ref,
    touched_ref,
    ids_ref,
    w_ref,
    sent_ref,
    rows_ref,
    words_ref,
    counts_ref,
    sums,
    same,
    slots,
    codes,
):
    step = pl.program_id(0)
    rows_f, width = table_ref.shape[1:]
    hots, b_group = ids_ref.shape[1:]
    count = touched_ref.shape[1]
    low = count // DIGITS
    hidden = w_ref.shape[2]
    blocks, tall, chunk = sums.shape
    block = min(b_group, BLOCK)

    @pl.when(step == 0)
    def _():
        sums[...] = jnp.zeros_like(sums)
        same[...] = jnp.zeros_like(same)

    features = range(PAIR)
    lines = []
    for side in features:
        words = slot_words(touched_ref[pl.ds(step * PAIR + side, 1)], rows_f)
        words_ref[side] = words
        lines.append([words[number : number + 1] for number in range(words.shape[0])])
    lane = iota((HALF, LANES), 1)
    columns, picked = [], []
    for side in features:
        row = touched_ref[pl.ds(step * PAIR + side, 1)].astype(jnp.float32)
        column = jnp.broadcast_to(row, (LANES, count)).T.astype(jnp.int32).astype(jnp.int16)
        columns.append(column.reshape(count // HALF, HALF, LANES))
        picked.append(jnp.zeros((count, width), jnp.float32))
    one = jnp.ones(columns[0].shape, jnp.bfloat16)
    for start in range(0, rows_f, ROWS):
        for side in features:
            parts = []
            for first in range(start, start + ROWS, LANES):
                number = (lane + first).astype(jnp.int16)
                hit = columns[side] == jnp.broadcast_to(number[None], one.shape)
                parts.append(jnp.where(hit, one, jnp.zeros_like(one)).reshape(count, LANES))
            rows = table_ref[side, start : start + ROWS].astype(jnp.bfloat16)
            picked[side] = picked[side] + dot(jnp.concatenate(parts, axis=1), rows)
    rows_t, w_t = [], []
    for side in features:
        whole = picked[side].astype(jnp.bfloat16).T
        rows_ref[side] = whole
        parts = [
            whole[:, digit * low : (digit + 1) * low] * jnp.bfloat16(1 / scale(digit))
            for digit in range(DIGITS)
        ]
        rows_t.append(jnp.concatenate(parts, axis=1))
        w_t.append(w_ref[side].T)

    def one_block(number):
        for inner in range(0, block, chunk):
            for side in features:
                where = pl.ds(pl.multiple_of(number * block + inner, chunk), chunk)
                ids = ids_ref[side, :, where]
                look_up(lines[side], ids, slots.at[side], slice(inner, inner + chunk))
                pairs = jnp.zeros(ids.shape, jnp.float32)
                for turn in range(1, hots // 2 + 1):
                    weight = 2.0 if turn < hots // 2 else 1.0
                    pairs = pairs + jnp.where(ids == pltpu.roll(ids, turn, 0), weight, 0.0)
                pairs = jnp.sum(pairs, axis=0, keepdims=True) + hots
                part = number * (block // chunk) + inner // chunk
                same[part, pl.ds(step * PAIR + side, 1)] = pairs
        for inner in range(0, block, 2 * chunk):
            pre, square = 0.0, 0.0
            for side in features:
                parts = []
                for start in (inner, inner + chunk):
                    where = slice(start, start + chunk)
                    parts.append(spread(tally(slots.at[side], codes.at[side], where)))
                counts = jnp.concatenate(parts, axis=1)
                where = pl.ds(pl.multiple_of(number * block + inner, 2 * chunk), 2 * chunk)
                counts_ref[side, :, where] = counts
                pooled = dot(rows_t[side], counts).astype(jnp.bfloat16)
                wide = pooled.astype(jnp.float32)
                square += jnp.sum((wide * wide).reshape(width // HALF, HALF, 2 * chunk), axis=0)
                pre += dot(w_t[side], pooled)
            for turn in range(2):
                part = number * (block // chunk) + inner // chunk + turn
                lanes = slice(turn * chunk, (turn + 1) * chunk)
                sums[part, :hidden] += pre[:, lanes]
                sums[part, hidden:] += square[:, lanes]

    each(b_group // block, one_block)

    @pl.when(step == pl.num_programs(0) - 1)
    def _():
        for part in range(blocks):
            sent_ref[part, :tall] = sums[part].astype(jnp.bfloat16)
            sent_ref[part, tall:] = same[part].astype(jnp.bfloat16)


def each(times, step):
    if times == 1:
        step(0)
    else:

        @pl.loop(0, times)
        def _(number):
            step(number)


def pool(place, table, touched, ids, w_hidden, chunk):
    f_dev, rows_f, width = table.shape
    hots, b_group = ids.shape[1:]
    count = touched.shape[1]
    hidden = w_hidden.shape[2]
    blocks = b_group // chunk
    repeat_rows = -(-f_dev // HALF) * HALF
    tall = hidden + HALF
    sent = (blocks, tall + repeat_rows, chunk)
    steps = f_dev // PAIR

    def now(*shape):
        return pl.BlockSpec((PAIR,) + shape, lambda i, p: (i, 0, 0))

    return pl.pallas_call(
        pool_kernel,
        grid_spec=pltpu.PrefetchScalarGridSpec(
            num_scalar_prefetch=1,
            grid=(steps,),
            in_specs=[
                now(rows_f, width),
                pl.BlockSpec(touched.shape, lambda i, p: (0, 0)),
                now(hots, b_group),
                pl.BlockSpec((PAIR, width, hidden), lambda i, p: (p[OWN] * steps + i, 0, 0)),
            ],
            out_specs=[
                pl.BlockSpec(sent, lambda i, p: (0, 0, 0)),
                now(width, count),
                now(rows_f // 256, LANES),
                now(count, b_group),
            ],
            scratch_shapes=[
                pltpu.VMEM((blocks, tall, chunk), jnp.float32),
                pltpu.VMEM((blocks, repeat_rows, chunk), jnp.float32),
                pltpu.VMEM((PAIR, 3, hots, min(b_group, BLOCK)), jnp.int32),
                pltpu.VMEM((PAIR, hots, 8, min(b_group, BLOCK)), jnp.int32),
            ],
        ),
        out_shape=[
            jax.ShapeDtypeStruct(sent, jnp.bfloat16),
            jax.ShapeDtypeStruct((f_dev, width, count), jnp.bfloat16),
            jax.ShapeDtypeStruct((f_dev, rows_f // 256, LANES), jnp.int32),
            jax.ShapeDtypeStruct((f_dev, count, b_group), jnp.bfloat16),
        ],
        compiler_params=pltpu.CompilerParams(vmem_limit_bytes=56 * MIB),
        cost_estimate=pl.CostEstimate(
            flops=2 * f_dev * count * b_group * width * 8,
            bytes_accessed=table.size * 4,
            transcendentals=0,
        ),
        name="pool",
    )(place, table, touched, ids, w_hidden)


def code_kernel(words_ref, ids_ref, *rest):
    codes_ref, slots, codes = rest[-3:]
    b_group = codes_ref.shape[2]
    block = min(b_group, BLOCK)
    lines = [
        [words_ref[side, number : number + 1] for number in range(words_ref.shape[1])]
        for side in range(PAIR)
    ]

    def one_block(number):
        for inner in range(0, block, LANES):
            where = pl.ds(pl.multiple_of(number * block + inner, LANES), LANES)
            packed = ids_ref[0, 0, :, where]
            for side, ids in enumerate((packed & 0xFFFF, packed >> HALF)):
                look_up(lines[side], ids, slots.at[side], slice(inner, inner + LANES))
        for inner in range(0, block, LANES):
            where = pl.ds(pl.multiple_of(number * block + inner, LANES), LANES)
            for side in range(PAIR):
                codes_ref[side, :, where] = tally(
                    slots.at[side], codes.at[side], slice(inner, inner + LANES)
                )

    each(b_group // block, one_block)


def code_counts(words, packed, low, start, stop, before=None):
    others, pairs, hots, b_group = packed.shape
    size = (stop - start) * PAIR * low * others * b_group
    kept = () if before is None else (before,)
    return pl.pallas_call(
        code_kernel,
        grid=(stop - start, others),
        in_specs=[
            pl.BlockSpec((PAIR,) + words.shape[1:], lambda f, g: (f + start, 0, 0)),
            pl.BlockSpec((1, 1, hots, b_group), lambda f, g: (g, f + start, 0, 0)),
        ]
        + [pl.BlockSpec(memory_space=pl.ANY)] * len(kept),
        out_specs=pl.BlockSpec((PAIR, low, b_group), lambda f, g: (f + start, 0, g)),
        scratch_shapes=[
            pltpu.VMEM((PAIR, 3, hots, min(b_group, BLOCK)), jnp.int32),
            pltpu.VMEM((PAIR, hots, 8, min(b_group, BLOCK)), jnp.int32),
        ],
        out_shape=jax.ShapeDtypeStruct((pairs * PAIR, low, others * b_group), jnp.int32),
        input_output_aliases={2: 0} if kept else {},
        compiler_params=pltpu.CompilerParams(vmem_limit_bytes=48 * MIB),
        cost_estimate=pl.CostEstimate(
            flops=size * 800, bytes_accessed=size * 4, transcendentals=0
        ),
        name="code",
    )(words, packed, *kept)


def clip_kernel(w_out_ref, labels_ref, w_ref, sent_ref, clip_ref):
    features, width, hidden = w_ref.shape
    devices = sent_ref.shape[0]
    share = features // devices
    tall = hidden + HALF
    w_out = w_out_ref[...]
    red = sent_ref[0, :tall].astype(jnp.float32)
    for device in range(1, devices):
        red = red + sent_ref[device, :tall].astype(jnp.float32)
    pre = red[:hidden]
    flat_sq = jnp.sum(red[hidden:], axis=0, keepdims=True)
    gate = jax.nn.sigmoid(pre)
    logit = jnp.sum(pre * gate * w_out, axis=0, keepdims=True)
    miss = jax.nn.sigmoid(logit) - labels_ref[...]
    delta = gate * (1.0 + pre * (1.0 - gate)) * w_out * miss
    delta_low = delta.astype(jnp.bfloat16)
    lanes = pre.shape[1]

    total = jnp.zeros((8, lanes), jnp.float32)
    for device in range(devices):
        w_part = w_ref[device * share : (device + 1) * share].reshape(share * width, hidden)
        grad = dot(w_part, delta_low)
        square = jnp.sum((grad * grad).reshape(share, width // 8, 8, lanes), axis=1)
        repeats = sent_ref[device, tall:].astype(jnp.float32)
        for inner in range(share):
            total = total + square[inner] * repeats[inner : inner + 1]
    norm_sq = jnp.sum(total, axis=0, keepdims=True)
    norm_sq = norm_sq + flat_sq * jnp.sum(delta * delta, axis=0, keepdims=True)
    factor = CLIP / jnp.maximum(jnp.sqrt(norm_sq), CLIP)
    clip_ref[...] = (factor * delta).T.astype(jnp.bfloat16)


def clip_rows(sent, w_out, labels, w_hidden):
    features, width, hidden = w_hidden.shape
    b_dev = labels.shape[0]
    vmem = pl.BlockSpec(memory_space=pltpu.VMEM)
    return pl.pallas_call(
        clip_kernel,
        in_specs=[vmem] * 4,
        out_specs=vmem,
        out_shape=jax.ShapeDtypeStruct((b_dev, hidden), jnp.bfloat16),
        compiler_params=pltpu.CompilerParams(vmem_limit_bytes=32 * MIB),
        cost_estimate=pl.CostEstimate(
            flops=2 * features * width * hidden * b_dev,
            bytes_accessed=w_hidden.size * 2,
            transcendentals=b_dev * hidden,
        ),
        name="clip",
    )(w_out.reshape(hidden, 1), labels.reshape(1, b_dev), w_hidden, sent)


def split(array, parts):
    found = []
    for part in range(parts):
        found.append(array.astype(jnp.bfloat16))
        array = array - found[-1].astype(jnp.float32)
    return found


def update_kernel(
    place_ref,
    listed_ref,
    own_counts_ref,
    codes_ref,
    near_ref,
    far_ref,
    table_ref,
    touched_ref,
    words_ref,
    accum_ref,
    noise_ref,
    w_ref,
    rows_ref,
    dense_noise_ref,
    table_out,
    accum_out,
    dense_out,
    update,
    clips,
):
    step = pl.program_id(0)
    last = pl.num_programs(0) - 1
    count, b_group = own_counts_ref.shape[1:]
    low = count // DIGITS
    groups = near_ref.shape[1]
    rows_f, width = table_ref.shape[1:]
    hidden = clips.shape[1]
    block = min(b_group, BLOCK)
    features = range(PAIR)

    @pl.when(step == 0)
    def _():
        chips, rows = near_ref.shape[0], near_ref.shape[2]
        for core, source in enumerate((near_ref, far_ref)):
            for chip in range(chips):
                for group in range(groups):
                    start = group * b_group + (place_ref[OWN] ^ (2 * chip + core)) * rows
                    clips[pl.ds(pl.multiple_of(start, rows), rows)] = source[chip, group]

    def put(side, start, stop):
        feature = jnp.maximum(step - 1, 0) * PAIR + side
        for first in range(start, stop, BATCH):
            batch = range(first, first + BATCH)
            spots = [pl.ds(listed_ref[feature, slot], 1) for slot in batch]
            rows = [table_ref[side, spot, :] for spot in spots]
            steps = [update[side, slot : slot + 1, :] for slot in batch]
            for spot, row, one_step in zip(spots, rows, steps):
                table_out[side, spot, :] = row - one_step

    def add(group, number, sums):
        where = pl.ds(pl.multiple_of(number * block, block), block)
        at = pl.ds(pl.multiple_of(group * b_group + number * block, block), block)
        found = []
        for side in features:
            if group == 0:
                counts = own_counts_ref[side, :, where]
            else:
                start = pl.multiple_of((group - 1) * b_group + number * block, block)
                counts = spread(codes_ref[side, :, pl.ds(start, block)])
            found.append(sums[side] + dot(counts, clips[at]))
        return tuple(found)

    def finish(side, sums):
        parts = [
            sums[digit * low : (digit + 1) * low] * (1 / scale(digit)) for digit in range(DIGITS)
        ]
        both = jnp.concatenate(split(jnp.concatenate(parts, axis=0), 2), axis=1)
        dense = dot(rows_ref[side], both)
        dense_out[side] = dense[:, :hidden] + dense[:, hidden:] + dense_noise_ref[side]
        w_twice = jnp.concatenate([w_ref[side], w_ref[side]], axis=1)
        listed = dot(both, w_twice, NT) + noise_ref[side]

        square = jnp.concatenate(split(listed * listed, 2), axis=1)
        mean = dot(square, jnp.full((2 * width, LANES), 1 / width, jnp.bfloat16))
        shape = (LANES, LANES)
        eye = iota(shape, 0) == iota(shape, 1)
        sections = [slice(start, start + LANES) for start in range(0, count, LANES)]
        touched = touched_ref[pl.ds(step * PAIR + side, 1)]
        touched = jnp.concatenate([touched[:, lanes] for lanes in sections * 2], axis=0)
        feature = step * PAIR + side
        mine = iota((accum_ref.shape[0], LANES), 0) == feature
        stretches = [slice(start, start + LANES) for start in range(0, rows_f, LANES)]
        lines = [
            jnp.sum(jnp.where(mine, accum_ref[:, lanes], 0.0), axis=0, keepdims=True)
            for lanes in stretches
        ]
        old = pick_lanes(lines, touched >> 7, touched & (LANES - 1))
        ones = jnp.where(eye, 1.0, 0.0).astype(jnp.bfloat16)
        parts = split(old, 2)
        diagonal = jnp.concatenate(
            [
                jnp.concatenate(
                    [ones * jnp.broadcast_to(part[q : q + 1], shape) for part in parts], axis=1
                )
                for q in range(len(sections))
            ],
            axis=0,
        )
        total = mean + dot(diagonal, jnp.full((2 * LANES, LANES), 1, jnp.bfloat16))
        update[side] = listed * (LEARN * lax.rsqrt(total))

        extra = [
            jnp.sum(jnp.where(eye, mean[rows], 0.0), axis=0, keepdims=True) for rows in sections
        ]
        words = words_ref[side]
        for half, word in enumerate((words & 0xFFFF, lax.shift_right_logical(words, HALF))):
            digit = (word >> 10) & (DIGITS - 1)
            gain = pick_lanes(extra, digit >> 1, (word & 63) + ((digit & 1) << 6))
            gain = jnp.where((word >> 8) >= LISTED, gain, 0.0)
            for number in range(words.shape[0]):
                place = half * words.shape[0] + number
                line = jnp.broadcast_to(lines[place] + gain[number : number + 1], mine.shape)
                lanes = stretches[place]
                accum_out[:, lanes] = jnp.where(mine, line, accum_out[:, lanes])

    @pl.when(step < last)
    def _():
        table_out[...] = table_ref[...]
        sums = tuple(jnp.zeros((count, hidden), jnp.float32) for side in features)
        share = count // groups
        for group in range(groups):
            for side in features:
                put(side, group * share, (group + 1) * share)
            if b_group == block:
                sums = add(group, 0, sums)
            else:
                sums = lax.fori_loop(0, b_group // block, functools.partial(add, group), sums)
        for side in features:
            finish(side, sums[side])

    @pl.when(step == last)
    def _():
        table_out[...] = table_ref[...]
        for side in features:
            put(side, 0, count)


def update_rows(
    place,
    own_counts,
    codes,
    near,
    far,
    table,
    touched,
    words,
    accum,
    noise,
    w_hidden,
    rows_t,
    dense_noise,
):
    f_dev, rows_f, width = table.shape
    count, b_group = own_counts.shape[1:]
    low = count // DIGITS
    others = codes.shape[2]
    hidden = near.shape[-1]
    part = dense_noise.shape[1]
    steps = f_dev // PAIR

    def current(i):
        return jnp.minimum(i, steps - 1)

    def now(*shape):
        return pl.BlockSpec((PAIR,) + shape, lambda i, p, s: (current(i), 0, 0))

    def before(*shape):
        return pl.BlockSpec((PAIR,) + shape, lambda i, p, s: (jnp.maximum(i - 1, 0), 0, 0))

    def whole(array):
        return pl.BlockSpec(array.shape, lambda i, p, s: (0,) * array.ndim)

    return pl.pallas_call(
        update_kernel,
        grid_spec=pltpu.PrefetchScalarGridSpec(
            num_scalar_prefetch=2,
            grid=(steps + 1,),
            in_specs=[
                now(count, b_group),
                now(low, others),
                whole(near),
                whole(far),
                before(rows_f, width),
                whole(touched),
                now(*words.shape[1:]),
                whole(accum),
                now(count, width),
                pl.BlockSpec(
                    (PAIR, width, hidden), lambda i, p, s: (p[OWN] * steps + current(i), 0, 0)
                ),
                pl.BlockSpec((PAIR, part, count), lambda i, p, s: (current(i), p[GROUP], 0)),
                now(part, hidden),
            ],
            out_specs=[before(rows_f, width), whole(accum), now(part, hidden)],
            scratch_shapes=[
                pltpu.VMEM((PAIR, count, width), jnp.float32),
                pltpu.VMEM((b_group + others, hidden), jnp.bfloat16),
            ],
        ),
        out_shape=[
            jax.ShapeDtypeStruct((f_dev, rows_f, width), jnp.float32),
            jax.ShapeDtypeStruct(accum.shape, jnp.float32),
            jax.ShapeDtypeStruct((f_dev, part, hidden), jnp.float32),
        ],
        compiler_params=pltpu.CompilerParams(vmem_limit_bytes=56 * MIB),
        cost_estimate=pl.CostEstimate(
            flops=2 * f_dev * count * (b_group + others) * hidden,
            bytes_accessed=table.size * 8 + codes.size * 2,
            transcendentals=0,
        ),
        name="update",
    )(
        place,
        touched,
        own_counts,
        codes,
        near,
        far,
        table,
        touched,
        words,
        accum,
        noise,
        w_hidden,
        rows_t,
        dense_noise,
    )


def swap(array, axis, apart):
    size = lax.axis_size(axis)
    return lax.ppermute(array, axis, [(i, i ^ apart) for i in range(size)])


def body(table, accum, w_hidden, w_out, ids, labels, touched, row_noise, dense_noise):
    f_dev = table.shape[0]
    b_dev = labels.shape[0]
    low = touched.shape[1] // DIGITS
    groups, tables = lax.axis_size("group"), lax.axis_size("table")
    own = lax.axis_index("table").astype(jnp.int32)
    group = lax.axis_index("group").astype(jnp.int32)
    place = jnp.stack([own, group])
    pairs = f_dev // PAIR

    packed = ids[0::2] | (ids[1::2] << HALF)
    ids, packed, place = lax.optimization_barrier((ids, packed, place))
    packed = [swap(packed, "group", d) for d in range(1, groups)]

    sent, rows_t, words, own_counts = pool(place, table, touched, ids, w_hidden, b_dev)
    packed = jnp.stack(packed)
    stops = [pairs * share // 4 for share in range(5)]

    def more_codes(number, codes, waits, ready=None):
        if stops[number + 1] > stops[number]:
            begin = words
            if ready is not None:
                begin, ready = lax.optimization_barrier((words, ready))
            codes = code_counts(
                begin, packed, low, stops[number], stops[number + 1], codes
            )
        return lax.optimization_barrier((codes, waits))

    sent, packed = lax.optimization_barrier((sent, packed))
    arrived = lax.all_to_all(sent, "table", split_axis=0, concat_axis=0, tiled=True)
    codes, arrived = more_codes(0, None, arrived)
    clips = clip_rows(arrived, w_out, labels, w_hidden)
    column = [clips] + [swap(clips, "group", d) for d in range(1, groups)]
    codes, column = more_codes(1, codes, column, clips)
    column = jnp.stack(column)
    near = [column] + [swap(column, "table", d) for d in range(2, tables, 2)]
    codes, near = more_codes(2, codes, near, column)
    near = jnp.stack(near)
    far = swap(near, "table", 1)
    codes, far = more_codes(3, codes, far, near)

    return update_rows(
        place,
        own_counts,
        codes,
        near,
        far,
        table,
        touched,
        words,
        accum,
        row_noise,
        w_hidden,
        rows_t,
        dense_noise,
    )


def solution(mesh):
    in_specs = (
        P("table", None, None),
        P("table", None),
        P(),
        P(),
        P("table", None, "group"),
        P(("group", "table")),
        P("table", None),
        P("table", None, None),
        P("table", "group", None),
    )
    out_specs = (P("table", None, None), P("table", None), P("table", "group", None))
    return jax.shard_map(body, mesh=mesh, in_specs=in_specs, out_specs=out_specs, check_vma=False)
```
